128 devices in a mesh: row: 8 (over z, x_hi), col: 16 (over y, x_lo, core).
Axes of the slice: x: 4 (x_hi: 2, x_lo: 2; x = x_hi * 2 + x_lo), y: 4, z: 4, core: 2. Of those that a mesh axis runs over, the one named last changes fastest.
Arguments:
- atoms: bfloat16 [32768, 128], P(('row', 'col')), may hold values from -6 to 6
- tokens: bfloat16 [4096, 768], P('row', 'col'), may hold values from -6 to 6
- atom_bias: bfloat16 [1024, 4, 32, 128], P(('row', 'col')), may hold values from -7.5 to 250
- token_bias: bfloat16 [16, 4096, 4096], P(None, 'row', 'col'), may hold values from -8 to 250
- atom_index: int32 [32768], P(('row', 'col')), may hold values from 0 to 4095, as said below
- atom_counts: int32 [4096], P('row'), may hold values from 1 to 15, as said below
- window_starts: int32 [1024], P(('row', 'col')), may hold values from 0 to 32640, as said below
- gain_atom: float32 [128], replicated, may hold values from 0.5 to 1.5
- w_atom_q: bfloat16 [128, 128], replicated, may hold values from -0.5 to 0.5
- w_atom_kv: bfloat16 [128, 256], replicated, may hold values from -0.5 to 0.5
- w_atom_o: bfloat16 [128, 128], replicated, may hold values from -0.5 to 0.5
- w_agg: bfloat16 [128, 768], replicated, may hold values from -0.5 to 0.5
- gain_token: float32 [768], replicated, may hold values from 0.5 to 1.5
- w_query: bfloat16 [768, 768], replicated, may hold values from -0.21875 to 0.21875
- w_keyval: bfloat16 [768, 1536], replicated, may hold values from -0.21875 to 0.21875
- w_gate: bfloat16 [768, 768], replicated, may hold values from -0.21875 to 0.21875
- w_out: bfloat16 [768, 768], replicated, may hold values from -0.21875 to 0.21875
- w_t2a: bfloat16 [768, 128], replicated, may hold values from -0.21875 to 0.21875
- atoms_cot: bfloat16 [32768, 128], P(('row', 'col')), may hold values from -6 to 6
- tokens_cot: bfloat16 [4096, 768], P('row', 'col'), may hold values from -6 to 6
Outputs:
- atoms_out: bfloat16 [32768, 128], P(('row', 'col'))
- tokens_out: bfloat16 [4096, 768], P('row', 'col')
- grad_atoms: bfloat16 [32768, 128], P(('row', 'col'))
- grad_tokens: bfloat16 [4096, 768], P('row', 'col')
The draws below stay inside these ranges and needn't reach their ends.
Inputs may be any that keep to these rules, and one draw needn't show every extreme that they name: atom_index never falls and names each token t exactly atom_counts[t] times. `atom_counts`: the counts of each aligned run of 512 tokens sum to 4096. window_starts[b] = min(max(32 * b - 48 + o_b, 0), 32640) with o_b an integer in -16 to 16; every window therefore reaches at most 64 atoms past the atoms of the device that holds block b.
All inputs are finite; a program needn't handle non-finite values.
Results may differ from the reference program's by a relative error of at most 0.013.
Values may be sent and summed in bfloat16 or wider, within the bound.
No kernel may reach another device: no remote copies, remote signals or barrier semaphores. Data moves between devices by JAX's collectives and lax.ppermute only.
A program may use at most 192 MiB of HBM per device.

```python
import math
import jax
import jax.numpy as jnp
from jax import lax

D = 768
H = 16
HD = 48
DA = 128
AH = 4
AHD = 32
QBLK = 32
KWIN = 128
TOK_ROW = 512
TOKENS = 4096
ATOMS = 32768


def token_counts(key):
    groups = TOKENS // TOK_ROW
    shifts = jax.random.randint(key, (groups, TOK_ROW // 2), -7, 8)
    column = jnp.arange(TOK_ROW // 2, dtype=jnp.int32)[None, :]
    shifts = jnp.where(column == 0, 7, shifts)
    paired = jnp.stack([8 + shifts, 8 - shifts], axis=-1).reshape(groups, TOK_ROW)
    order_keys = jax.random.split(jax.random.fold_in(key, 101), groups)
    orders = jax.vmap(lambda sub_key: jax.random.permutation(sub_key, TOK_ROW))(order_keys)
    mixed = jnp.take_along_axis(paired, orders, axis=1)
    return mixed.reshape(TOKENS).astype(jnp.int32)


def draw_atom_counts(key, part):
    counts_drawn = token_counts(key)
    return counts_drawn


def draw_atom_index(key, part):
    counts_drawn = token_counts(key)
    return jnp.repeat(jnp.arange(TOKENS, dtype=jnp.int32), counts_drawn, total_repeat_length=ATOMS).astype(jnp.int32)


def draw_window_starts(key, part):
    key = jax.random.fold_in(key, 5)
    block_total = ATOMS // QBLK
    reach = (KWIN - QBLK) // 2
    offsets = jax.random.randint(key, (block_total,), -16, 17)
    blocks_at = jnp.arange(block_total, dtype=jnp.int32)
    offsets = jnp.where(blocks_at == 5, -16, jnp.where(blocks_at == 6, 16, offsets))
    return jnp.clip(blocks_at * QBLK - reach + offsets, 0, ATOMS - KWIN).astype(jnp.int32)


def draw_atom_bias(key, part):
    key = jax.random.fold_in(key, 7)
    sub_keys = jax.random.split(key, 1)
    values = 1.5 * jax.random.truncated_normal(sub_keys[0], -5.0, 5.0, (ATOMS // QBLK, AH, QBLK, KWIN))
    return values.astype(jnp.bfloat16)


def draw_token_bias(key, part):
    key = jax.random.fold_in(key, 11)
    sub_keys = jax.random.split(key, 1)
    values = 2.5 * jax.random.truncated_normal(sub_keys[0], -3.2, 3.2, (H, TOKENS, TOKENS))
    return values.astype(jnp.bfloat16)


def levels(rng, extent, cuts, smallest, top_value):
    def one(position, blocks):
        draws = jax.random.uniform(jax.random.fold_in(jax.random.fold_in(rng, 6), position), (blocks,), jnp.float32, smallest / len(cuts), top_value / len(cuts))
        return jnp.repeat(jnp.exp(draws), extent[position] // blocks).reshape((-1,) + (1,) * (len(extent) - position - 1))

    factor_of = one(*cuts[0])
    for cut in cuts[1:]:
        factor_of = factor_of * one(*cut)
    return factor_of


def centred(stream_key, extent, scale, most, pieces=(), held_as=jnp.bfloat16):
    entries = scale * jax.random.normal(stream_key, extent, jnp.float32)
    if pieces:
        entries = entries * levels(stream_key, extent, pieces, -0.22, 0.18)
    return jnp.clip(entries, -most, most).astype(held_as)


def setup_inputs(seed: int = 0) -> dict:
    arg_keys = jax.random.split(jax.random.key(seed), 21)
    atoms = centred(arg_keys[0], (ATOMS, DA), 1.0, 6.0, ((0, 128),))
    tokens = centred(arg_keys[1], (TOKENS, D), 1.0, 6.0, ((0, 8), (1, 16)))
    atom_bias = draw_atom_bias(jax.random.fold_in(arg_keys[20], 71), 0)
    token_bias = draw_token_bias(jax.random.fold_in(arg_keys[20], 71), 0)
    atom_index = draw_atom_index(jax.random.fold_in(arg_keys[20], 71), 0)
    atom_counts = draw_atom_counts(jax.random.fold_in(arg_keys[20], 71), 0)
    window_starts = draw_window_starts(jax.random.fold_in(arg_keys[20], 71), 0)
    gain_atom = jnp.clip(1.0 + 0.1 * jax.random.normal(arg_keys[7], (DA,), jnp.float32), 0.5, 1.5)
    w_atom_q = centred(arg_keys[8], (DA, DA), DA ** -0.5, 0.5)
    w_atom_kv = centred(arg_keys[9], (DA, 2 * DA), DA ** -0.5, 0.5)
    w_atom_o = centred(arg_keys[10], (DA, DA), DA ** -0.5, 0.5)
    w_agg = centred(arg_keys[11], (DA, D), DA ** -0.5, 0.5)
    gain_token = jnp.clip(1.0 + 0.1 * jax.random.normal(arg_keys[12], (D,), jnp.float32), 0.5, 1.5)
    w_query = centred(arg_keys[13], (D, D), D ** -0.5, 0.21875)
    w_keyval = centred(arg_keys[14], (D, 2 * D), D ** -0.5, 0.21875)
    w_gate = centred(arg_keys[15], (D, D), D ** -0.5, 0.21875)
    w_out = centred(arg_keys[16], (D, D), D ** -0.5, 0.21875)
    w_t2a = centred(arg_keys[17], (D, DA), D ** -0.5, 0.21875)
    atoms_cot = centred(arg_keys[18], (ATOMS, DA), 1.0, 6.0, ((0, 128),))
    tokens_cot = centred(arg_keys[19], (TOKENS, D), 1.0, 6.0, ((0, 8), (1, 16)))
    return {"atoms": atoms, "tokens": tokens, "atom_bias": atom_bias, "token_bias": token_bias, "atom_index": atom_index, "atom_counts": atom_counts, "window_starts": window_starts, "gain_atom": gain_atom, "w_atom_q": w_atom_q, "w_atom_kv": w_atom_kv, "w_atom_o": w_atom_o, "w_agg": w_agg, "gain_token": gain_token, "w_query": w_query, "w_keyval": w_keyval, "w_gate": w_gate, "w_out": w_out, "w_t2a": w_t2a, "atoms_cot": atoms_cot, "tokens_cot": tokens_cot}


EPS = 1e-05

def layer_norm(values, gain_vec):
    center = values - lax.optimization_barrier(jnp.mean(values, axis=-1, keepdims=True))
    spread = lax.optimization_barrier(jnp.mean(center * center, axis=-1, keepdims=True))
    return center * lax.rsqrt(spread + EPS) * gain_vec

def norm_back(values, gain_vec, cotangent):
    return jax.vjp(lambda inner: layer_norm(inner, gain_vec), values)[1](cotangent)[0]

def reference(atoms, tokens, atom_bias, token_bias, atom_index, atom_counts, window_starts, gain_atom, w_atom_q, w_atom_kv, w_atom_o, w_agg, gain_token, w_query, w_keyval, w_gate, w_out, w_t2a, atoms_cot, tokens_cot):
    atom_vals = atoms.astype(jnp.float32)
    atom_normed = layer_norm(atom_vals, gain_atom).astype(jnp.bfloat16)
    atom_query = jnp.dot(atom_normed, w_atom_q, preferred_element_type=jnp.float32).astype(jnp.bfloat16)
    atom_keyval = jnp.dot(atom_normed, w_atom_kv, preferred_element_type=jnp.float32).astype(jnp.bfloat16)
    block_count = window_starts.shape[0]
    window_slots = window_starts.astype(jnp.int32)[:, None] + jnp.arange(KWIN, dtype=jnp.int32)[None, :]
    window_rows = jnp.take(atom_keyval, window_slots, axis=0).astype(jnp.float32)
    query_blocks = atom_query.reshape(block_count, QBLK, AH, AHD).astype(jnp.float32)
    key_blocks = window_rows[:, :, :DA].reshape(block_count, KWIN, AH, AHD)
    value_blocks = window_rows[:, :, DA:].reshape(block_count, KWIN, AH, AHD)
    atom_scale = 1.0 / math.sqrt(AHD)
    atom_scores = jnp.einsum('bqhd,bkhd->bhqk', query_blocks, key_blocks) * atom_scale + atom_bias.astype(jnp.float32)
    atom_prob = jax.nn.softmax(atom_scores, axis=-1)
    atom_weights = atom_prob.astype(jnp.bfloat16)
    atom_mixed = jnp.einsum('bhqk,bkhd->bqhd', atom_weights.astype(jnp.float32), value_blocks).reshape(-1, DA).astype(jnp.bfloat16)
    atoms_mid = (atom_vals + jnp.dot(atom_mixed, w_atom_o, preferred_element_type=jnp.float32)).astype(jnp.bfloat16)
    agg_pre = jnp.dot(atoms_mid, w_agg, preferred_element_type=jnp.float32)
    agg_hidden = jax.nn.silu(agg_pre).astype(jnp.bfloat16)
    inverse_count = 1.0 / atom_counts.astype(jnp.float32)
    token_sums = jax.ops.segment_sum(agg_hidden.astype(jnp.float32), atom_index, num_segments=TOKENS)
    tokens_mid = tokens.astype(jnp.float32) + token_sums * inverse_count[:, None]
    token_normed = layer_norm(tokens_mid, gain_token).astype(jnp.bfloat16)
    token_query = jnp.dot(token_normed, w_query, preferred_element_type=jnp.float32).astype(jnp.bfloat16)
    token_keyval = jnp.dot(token_normed, w_keyval, preferred_element_type=jnp.float32).astype(jnp.bfloat16)
    gate_open = jax.nn.sigmoid(jnp.dot(token_normed, w_gate, preferred_element_type=jnp.float32))
    query_heads = token_query.reshape(TOKENS, H, HD).transpose(1, 0, 2)
    key_heads = token_keyval[:, :D].reshape(TOKENS, H, HD).transpose(1, 0, 2)
    value_heads = token_keyval[:, D:].reshape(TOKENS, H, HD).transpose(1, 0, 2)
    token_scale = 1.0 / math.sqrt(HD)

    def head_forward(operands):
        query_one, key_one, value_one, bias_one = operands
        token_scores = jnp.dot(query_one, key_one.T, preferred_element_type=jnp.float32) * token_scale + bias_one.astype(jnp.float32)
        row_max = lax.optimization_barrier(jnp.max(token_scores, axis=-1))
        exp_scores = jnp.exp(token_scores - row_max[:, None])
        row_total = lax.optimization_barrier(jnp.sum(exp_scores, axis=-1))
        weighted = jnp.dot(exp_scores.astype(jnp.bfloat16), value_one, preferred_element_type=jnp.float32)
        return (weighted / row_total[:, None], row_max, row_total)
    head_out, row_max, row_total = lax.map(head_forward, (query_heads, key_heads, value_heads, token_bias))
    attended = head_out.transpose(1, 0, 2).reshape(TOKENS, D)
    gated_out = (gate_open * attended).astype(jnp.bfloat16)
    tokens_new = (tokens_mid + jnp.dot(gated_out, w_out, preferred_element_type=jnp.float32)).astype(jnp.bfloat16)
    lifted = jnp.dot(tokens_new, w_t2a, preferred_element_type=jnp.float32)
    atoms_new = (atoms_mid.astype(jnp.float32) + jnp.take(lifted, atom_index, axis=0)).astype(jnp.bfloat16)
    cot_sums = jax.ops.segment_sum(atoms_cot.astype(jnp.float32), atom_index, num_segments=TOKENS).astype(jnp.bfloat16)
    grad_new = tokens_cot.astype(jnp.float32) + jnp.dot(cot_sums, w_t2a.T, preferred_element_type=jnp.float32)
    grad_gated = jnp.dot(grad_new.astype(jnp.bfloat16), w_out.T, preferred_element_type=jnp.float32)
    grad_attended = (grad_gated * gate_open).astype(jnp.bfloat16)
    grad_gate = (grad_gated * attended * gate_open * (1.0 - gate_open)).astype(jnp.bfloat16)
    row_delta = lax.optimization_barrier(jnp.sum((grad_attended.astype(jnp.float32) * attended).reshape(TOKENS, H, HD), axis=-1)).T
    grad_heads = grad_attended.reshape(TOKENS, H, HD).transpose(1, 0, 2)

    def head_back(operands):
        query_one, key_one, value_one, bias_one, max_one, total_one, grad_one, delta_one = operands
        token_scores = jnp.dot(query_one, key_one.T, preferred_element_type=jnp.float32) * token_scale + bias_one.astype(jnp.float32)
        token_prob = jnp.exp(token_scores - max_one[:, None]) / total_one[:, None]
        prob_grad = jnp.dot(grad_one, value_one.T, preferred_element_type=jnp.float32)
        score_grad = (token_prob * (prob_grad - delta_one[:, None])).astype(jnp.bfloat16)
        query_grad = jnp.dot(score_grad, key_one, preferred_element_type=jnp.float32) * token_scale
        key_grad = jnp.dot(score_grad.T, query_one, preferred_element_type=jnp.float32) * token_scale
        value_grad = jnp.dot(token_prob.astype(jnp.bfloat16).T, grad_one, preferred_element_type=jnp.float32)
        return (query_grad, key_grad, value_grad)
    query_grad, key_grad, value_grad = lax.map(head_back, (query_heads, key_heads, value_heads, token_bias, row_max, row_total, grad_heads, row_delta))
    query_grad = query_grad.transpose(1, 0, 2).reshape(TOKENS, D).astype(jnp.bfloat16)
    keyval_grad = jnp.concatenate([key_grad.transpose(1, 0, 2).reshape(TOKENS, D), value_grad.transpose(1, 0, 2).reshape(TOKENS, D)], axis=1).astype(jnp.bfloat16)
    normed_grad = jnp.dot(query_grad, w_query.T, preferred_element_type=jnp.float32)
    normed_grad = normed_grad + jnp.dot(keyval_grad, w_keyval.T, preferred_element_type=jnp.float32)
    normed_grad = normed_grad + jnp.dot(grad_gate, w_gate.T, preferred_element_type=jnp.float32)
    grad_mid = grad_new + norm_back(tokens_mid, gain_token, normed_grad)
    grad_tokens = grad_mid.astype(jnp.bfloat16)
    pre_sigmoid = jax.nn.sigmoid(agg_pre)
    silu_slope = pre_sigmoid * (1.0 + agg_pre * (1.0 - pre_sigmoid))
    hidden_grad = (jnp.take(grad_mid * inverse_count[:, None], atom_index, axis=0) * silu_slope).astype(jnp.bfloat16)
    atoms_grad = atoms_cot.astype(jnp.float32) + jnp.dot(hidden_grad, w_agg.T, preferred_element_type=jnp.float32)
    mixed_grad = jnp.dot(atoms_grad.astype(jnp.bfloat16), w_atom_o.T, preferred_element_type=jnp.float32).astype(jnp.bfloat16)
    mixed_blocks = mixed_grad.reshape(block_count, QBLK, AH, AHD).astype(jnp.float32)
    atom_pgrad = jnp.einsum('bqhd,bkhd->bhqk', mixed_blocks, value_blocks)
    atom_delta = lax.optimization_barrier(jnp.sum(mixed_blocks * atom_mixed.reshape(block_count, QBLK, AH, AHD).astype(jnp.float32), axis=-1)).transpose(0, 2, 1)
    atom_sgrad = (atom_prob * (atom_pgrad - atom_delta[..., None])).astype(jnp.bfloat16).astype(jnp.float32)
    atom_qgrad = (jnp.einsum('bhqk,bkhd->bqhd', atom_sgrad, key_blocks) * atom_scale).reshape(-1, DA).astype(jnp.bfloat16)
    atom_kgrad = jnp.einsum('bhqk,bqhd->bkhd', atom_sgrad, query_blocks) * atom_scale
    atom_vgrad = jnp.einsum('bhqk,bqhd->bkhd', atom_weights.astype(jnp.float32), mixed_blocks)
    window_grad = jnp.concatenate([atom_kgrad.reshape(block_count, KWIN, DA), atom_vgrad.reshape(block_count, KWIN, DA)], axis=-1)
    keyval_atoms = jnp.zeros((ATOMS, 2 * DA), jnp.float32).at[window_slots].add(window_grad).astype(jnp.bfloat16)
    atom_feat_grad = jnp.dot(atom_qgrad, w_atom_q.T, preferred_element_type=jnp.float32) + jnp.dot(keyval_atoms, w_atom_kv.T, preferred_element_type=jnp.float32)
    grad_atoms = (atoms_grad + norm_back(atom_vals, gain_atom, atom_feat_grad)).astype(jnp.bfloat16)
    return (atoms_new, tokens_new, grad_atoms, grad_tokens)
```

```python
import math

import jax
import jax.numpy as jnp
from jax import lax
from jax.sharding import PartitionSpec as P

D = 768
H = 16
HD = 48
DA = 128
AH = 4
AHD = 32
QBLK = 32
KWIN = 128
RIM = 64
EPS = 1e-05
BF = jnp.bfloat16
F32 = jnp.float32


def dot(a, b):
    return jnp.dot(a, b, preferred_element_type=F32)


def dot_t(a, b):
    return lax.dot_general(a, b, (((1,), (1,)), ((), ())), preferred_element_type=F32)


def layer_norm(values, gain_vec):
    center = values - jnp.mean(values, axis=-1, keepdims=True)
    spread = jnp.mean(center * center, axis=-1, keepdims=True)
    return center * lax.rsqrt(spread + EPS) * gain_vec


def norm_back(values, gain_vec, cotangent):
    center = values - jnp.mean(values, axis=-1, keepdims=True)
    inv = lax.rsqrt(jnp.mean(center * center, axis=-1, keepdims=True) + EPS)
    unit = center * inv
    g = cotangent * gain_vec
    return inv * (
        g
        - jnp.mean(g, axis=-1, keepdims=True)
        - unit * jnp.mean(g * unit, axis=-1, keepdims=True)
    )


def exchange(x, axis):
    return lax.all_to_all(x, axis, 0, 0)


def spread_all(x, axis):
    copies = jnp.broadcast_to(x[None], (lax.axis_size(axis),) + x.shape)
    return lax.all_to_all(copies, axis, 0, 0)


def neighbours(x, width):
    axes = ("row", "col")
    devices = lax.axis_size("row") * lax.axis_size("col")
    up = [(i, i + 1) for i in range(devices - 1)]
    down = [(j, i) for i, j in up]
    before = lax.ppermute(x[x.shape[0] - width :], axes, up)
    after = lax.ppermute(x[:width], axes, down)
    return before, after


def local(
    atoms,
    tokens,
    atom_bias,
    token_bias,
    atom_index,
    atom_counts,
    window_starts,
    gain_atom,
    w_atom_q,
    w_atom_kv,
    w_atom_o,
    w_agg,
    gain_token,
    w_query,
    w_keyval,
    w_gate,
    w_out,
    w_t2a,
    atoms_cot,
    tokens_cot,
):
    rows = lax.axis_size("row")
    cols = lax.axis_size("col")
    row_index = lax.axis_index("row")
    col_index = lax.axis_index("col")
    atom_dev = atoms.shape[0]
    blocks = window_starts.shape[0]
    tok_row = tokens.shape[0]
    tok_col = token_bias.shape[2]
    own = tok_row // cols
    width = tokens.shape[1]
    first_atom = (row_index * cols + col_index) * atom_dev
    padded_rows = atom_dev + 2 * RIM

    before, after = neighbours(atoms, RIM)

    local_token = atom_index - row_index * tok_row
    member = (local_token[None, :] == jnp.arange(tok_row, dtype=jnp.int32)[:, None]).astype(BF)
    inverse_count = 1.0 / atom_counts.astype(F32)
    cot_part = dot(member, atoms_cot).astype(BF)
    early = jnp.concatenate([tokens, tokens_cot, cot_part], axis=1)
    early = exchange(early.reshape(cols, own, -1), "col")
    tokens_own = early[:, :, :width].transpose(1, 0, 2).reshape(own, D).astype(F32)
    tokcot_own = early[:, :, width : 2 * width].transpose(1, 0, 2).reshape(own, D).astype(F32)
    cot_own = jnp.sum(early[:, :, 2 * width :].astype(F32), axis=0).astype(BF)
    grad_new = tokcot_own + dot_t(cot_own, w_t2a)
    grad_new_all = spread_all(grad_new.astype(BF), "col").reshape(tok_row, D)
    grad_gated_all = dot_t(grad_new_all, w_out)
    own_start = col_index * own
    inv_own = lax.dynamic_slice_in_dim(inverse_count, own_start, own, 0)

    padded = jnp.concatenate([before, atoms, after], axis=0).astype(F32)
    padded_normed = layer_norm(padded, gain_atom).astype(BF)
    atom_vals = atoms.astype(F32)
    atom_query = dot(padded_normed[RIM : RIM + atom_dev], w_atom_q).astype(BF)
    atom_keyval = dot(padded_normed, w_atom_kv).astype(BF)
    starts = window_starts - first_atom + RIM
    slots = (starts[:, None] + jnp.arange(KWIN, dtype=jnp.int32)[None, :]).reshape(-1)
    pick = (slots[:, None] == jnp.arange(padded_rows, dtype=jnp.int32)[None, :]).astype(BF)
    window_rows = dot(pick, atom_keyval).astype(BF).reshape(blocks, KWIN, 2 * DA)
    wkeys = window_rows[:, :, :DA]
    wvals = window_rows[:, :, DA:]
    head_mask = (
        jnp.arange(DA, dtype=jnp.int32)[None, :] // AHD == jnp.arange(AH, dtype=jnp.int32)[:, None]
    ).astype(BF)

    def by_head(x):
        x = x.reshape(blocks, 1, QBLK, DA) * head_mask[None, :, None, :]
        return x.reshape(blocks, AH * QBLK, DA)

    def from_head(x):
        x = x.reshape(blocks, AH, QBLK, DA) * head_mask[None, :, None, :].astype(F32)
        return jnp.sum(x, axis=1).reshape(atom_dev, DA)

    atom_scale = 1.0 / math.sqrt(AHD)
    query_heads = by_head(atom_query)
    atom_scores = jnp.einsum(
        "bqd,bkd->bqk", query_heads, wkeys, preferred_element_type=F32
    ) * atom_scale + atom_bias.reshape(blocks, AH * QBLK, KWIN).astype(F32)
    atom_prob = jax.nn.softmax(atom_scores, axis=-1)
    atom_weights = atom_prob.astype(BF)
    atom_mixed = from_head(
        jnp.einsum("bqk,bkd->bqd", atom_weights, wvals, preferred_element_type=F32)
    ).astype(BF)
    atoms_mid = (atom_vals + dot(atom_mixed, w_atom_o)).astype(BF)
    agg_pre = dot(atoms_mid, w_agg)
    pre_sigmoid = jax.nn.sigmoid(agg_pre)
    agg_hidden = (agg_pre * pre_sigmoid).astype(BF)
    silu_slope = pre_sigmoid * (1.0 + agg_pre * (1.0 - pre_sigmoid))

    sums_part = dot(member, agg_hidden).astype(BF).reshape(cols, own, D)
    sums = jnp.sum(exchange(sums_part, "col").astype(F32), axis=0)
    tokens_mid = tokens_own + sums * inv_own[:, None]
    normed_own = layer_norm(tokens_mid, gain_token).astype(BF)
    to_key = [(b, (b % rows) * cols + b // rows) for b in range(rows * cols)]
    to_row = [(j, i) for i, j in to_key]
    key_own = lax.ppermute(normed_own, ("row", "col"), to_key)
    normed = spread_all(normed_own, "col").reshape(tok_row, D)
    key_normed = spread_all(key_own, "row").reshape(tok_col, D)
    token_query = dot(normed, w_query).astype(BF)
    gate_all = jax.nn.sigmoid(dot(normed, w_gate))
    grad_attended = (grad_gated_all * gate_all).astype(BF)
    token_keyval = dot(key_normed, w_keyval).astype(BF)
    q_heads = token_query.reshape(tok_row, H, HD)
    g_heads = grad_attended.reshape(tok_row, H, HD)
    k_heads = token_keyval[:, :D].reshape(tok_col, H, HD)
    v_heads = token_keyval[:, D:].reshape(tok_col, H, HD)
    token_scale = 1.0 / math.sqrt(HD)
    scores = jnp.einsum(
        "qhd,khd->hqk", q_heads, k_heads, preferred_element_type=F32
    ) * token_scale + token_bias.astype(F32)
    row_max = jnp.max(scores, axis=-1)
    exps = jnp.exp(scores - row_max[..., None])
    total = jnp.sum(exps, axis=-1)
    mixed = jnp.einsum(
        "hqk,khd->qhd", exps.astype(BF), v_heads, preferred_element_type=F32
    ) * (1.0 / total).T[:, :, None]
    lse_part = row_max + jnp.log(total)
    delta_part = jnp.sum(g_heads.astype(F32) * mixed, axis=-1).T
    stats = spread_all(jnp.stack([lse_part, delta_part]), "col")
    mixed_parts = exchange(mixed.astype(BF).reshape(cols, own, H, HD), "col")
    top = jnp.max(stats[:, 0], axis=0)
    share = jnp.exp(stats[:, 0] - top)
    share_sum = jnp.sum(share, axis=0)
    lse = top + jnp.log(share_sum)
    row_delta = jnp.sum(share * stats[:, 1], axis=0) / share_sum

    prob = jnp.exp(scores - lse[..., None])
    prob_grad = jnp.einsum("qhd,khd->hqk", g_heads, v_heads, preferred_element_type=F32)
    score_grad = (prob * (prob_grad - row_delta[..., None])).astype(BF)
    key_grad = jnp.einsum("hqk,qhd->khd", score_grad, q_heads, preferred_element_type=F32)
    value_grad = jnp.einsum("hqk,qhd->khd", prob.astype(BF), g_heads, preferred_element_type=F32)
    kv_grad = jnp.concatenate(
        [(key_grad * token_scale).reshape(tok_col, D), value_grad.reshape(tok_col, D)], axis=1
    ).astype(BF)
    kv_parts = exchange(kv_grad.reshape(rows, own, 2 * D), "row")
    query_grad = (
        jnp.einsum("hqk,khd->qhd", score_grad, k_heads, preferred_element_type=F32) * token_scale
    )
    q_parts = exchange(query_grad.astype(BF).reshape(cols, own, D), "col")
    kv_sum = jnp.sum(kv_parts.astype(F32), axis=0).astype(BF)
    kv_back = lax.ppermute(dot_t(kv_sum, w_keyval), ("row", "col"), to_row)

    lse_own = lax.dynamic_slice_in_dim(stats[:, 0], own_start, own, 2)
    part_weight = jax.nn.softmax(lse_own, axis=0).transpose(0, 2, 1)[..., None]
    attended = jnp.sum(mixed_parts.astype(F32) * part_weight, axis=0).reshape(own, D)
    gate_own = lax.dynamic_slice_in_dim(gate_all, own_start, own, 0)
    gated_out = (gate_own * attended).astype(BF)
    tokens_new = (tokens_mid + dot(gated_out, w_out)).astype(BF)
    lifted = dot(tokens_new, w_t2a).astype(BF)
    new_slices = tokens_new.reshape(own, cols, width).transpose(1, 0, 2)
    out_parts = jnp.concatenate(
        [new_slices, jnp.broadcast_to(lifted[None], (cols, own, DA))], axis=2
    )
    out_parts = exchange(out_parts, "col").reshape(tok_row, width + DA)
    tokens_out = out_parts[:, :width]
    lift_all = out_parts[:, width:]
    atoms_new = (
        atoms_mid.astype(F32)
        + lax.dot_general(member, lift_all, (((0,), (0,)), ((), ())), preferred_element_type=F32)
    ).astype(BF)
    grad_gated_own = lax.dynamic_slice_in_dim(grad_gated_all, own_start, own, 0)
    grad_gate = (grad_gated_own * attended * gate_own * (1.0 - gate_own)).astype(BF)
    q_sum = jnp.sum(q_parts.astype(F32), axis=0).astype(BF)
    normed_grad = dot_t(q_sum, w_query) + dot_t(grad_gate, w_gate) + kv_back
    grad_mid = (grad_new + norm_back(tokens_mid, gain_token, normed_grad)).astype(BF)
    mid_all = spread_all(grad_mid, "col").reshape(tok_row, D)
    grad_tokens = lax.dynamic_slice_in_dim(mid_all, col_index * width, width, 1)

    atom_inverse = jnp.sum(member.astype(F32) * inverse_count[:, None], axis=0)
    lifted_grad = lax.dot_general(
        member, mid_all, (((0,), (0,)), ((), ())), preferred_element_type=F32
    )
    hidden_grad = (lifted_grad * atom_inverse[:, None] * silu_slope).astype(BF)
    atoms_grad = atoms_cot.astype(F32) + dot_t(hidden_grad, w_agg)
    mixed_grad = dot_t(atoms_grad.astype(BF), w_atom_o).astype(BF)
    mixed_heads = by_head(mixed_grad)
    atom_pgrad = jnp.einsum("bqd,bkd->bqk", mixed_heads, wvals, preferred_element_type=F32)
    atom_delta = jnp.sum(
        by_head(atom_mixed).astype(F32) * mixed_heads.astype(F32), axis=-1, keepdims=True
    )
    atom_sgrad = (atom_prob * (atom_pgrad - atom_delta)).astype(BF)
    atom_qgrad = (
        from_head(jnp.einsum("bqk,bkd->bqd", atom_sgrad, wkeys, preferred_element_type=F32))
        * atom_scale
    ).astype(BF)
    atom_kgrad = (
        jnp.einsum("bqk,bqd->bkd", atom_sgrad, query_heads, preferred_element_type=F32)
        * atom_scale
    )
    atom_vgrad = jnp.einsum("bqk,bqd->bkd", atom_weights, mixed_heads, preferred_element_type=F32)
    window_grad = jnp.concatenate([atom_kgrad, atom_vgrad], axis=-1).astype(BF)
    padded_grad = lax.dot_general(
        pick,
        window_grad.reshape(blocks * KWIN, 2 * DA),
        (((0,), (0,)), ((), ())),
        preferred_element_type=F32,
    )
    rim = jnp.concatenate([padded_grad[:RIM], padded_grad[atom_dev + RIM :]], axis=0).astype(BF)
    axes = ("row", "col")
    up = [(i, i + 1) for i in range(rows * cols - 1)]
    down = [(j, i) for i, j in up]
    from_before = lax.ppermute(rim[RIM:], axes, up)
    from_after = lax.ppermute(rim[:RIM], axes, down)
    keyval_atoms = padded_grad[RIM : RIM + atom_dev]
    keyval_atoms = jnp.concatenate(
        [
            keyval_atoms[:RIM] + from_before.astype(F32),
            keyval_atoms[RIM : atom_dev - RIM],
            keyval_atoms[atom_dev - RIM :] + from_after.astype(F32),
        ],
        axis=0,
    ).astype(BF)
    feat_grad = dot_t(atom_qgrad, w_atom_q) + dot_t(keyval_atoms, w_atom_kv)
    grad_atoms = (atoms_grad + norm_back(atom_vals, gain_atom, feat_grad)).astype(BF)
    return (atoms_new, tokens_out, grad_atoms, grad_tokens)


def solution(mesh):
    placed = (
        P(("row", "col"), None),
        P("row", "col"),
        P(("row", "col"), None, None, None),
        P(None, "row", "col"),
        P(("row", "col")),
        P("row"),
        P(("row", "col")),
        P(),
        P(),
        P(),
        P(),
        P(),
        P(),
        P(),
        P(),
        P(),
        P(),
        P(),
        P(("row", "col"), None),
        P("row", "col"),
    )
    return jax.shard_map(
        local,
        mesh=mesh,
        in_specs=placed,
        out_specs=(
            P(("row", "col"), None),
            P("row", "col"),
            P(("row", "col"), None),
            P("row", "col"),
        ),
        check_vma=False,
    )
```

```python
import math

import jax
import jax.numpy as jnp
from jax import lax
from jax.experimental import pallas as pl
from jax.experimental.pallas import tpu as pltpu
from jax.sharding import PartitionSpec as P

D = 768
H = 16
HD = 48
DA = 128
AH = 4
AHD = 32
QBLK = 32
KWIN = 128
RIM = 64
EPS = 1e-05
BF = jnp.bfloat16
F32 = jnp.float32
GROUP = 8
CORES = 2
CHUNK = 128
VMEM_LIMIT = 24 * 1024 * 1024
SMALL_LIMIT = 14 * 1024 * 1024


def dot(a, b):
    return jnp.dot(a, b, preferred_element_type=F32)


def dot_t(a, b):
    return lax.dot_general(a, b, (((1,), (1,)), ((), ())), preferred_element_type=F32)


def centred(values):
    center = values - jnp.mean(values, axis=-1, keepdims=True)
    inv = lax.rsqrt(jnp.mean(center * center, axis=-1, keepdims=True) + EPS)
    return center * inv, inv


def layer_norm(values, gain_vec):
    return centred(values)[0] * gain_vec


def norm_back(values, gain_vec, cotangent):
    unit, inv = centred(values)
    g = cotangent * gain_vec
    return inv * (
        g
        - jnp.mean(g, axis=-1, keepdims=True)
        - unit * jnp.mean(g * unit, axis=-1, keepdims=True)
    )


def sigmoid(x):
    return 1.0 / (1.0 + jnp.exp(-x))


def exchange(x, axis):
    return lax.all_to_all(x, axis, 0, 0)


def halves_of(x):
    cols = lax.axis_size("col")
    groups = [list(range(core, cols, CORES)) for core in range(CORES)]
    mine = lax.all_to_all(x, "col", 0, 0, axis_index_groups=groups)
    theirs = lax.ppermute(mine, "col", [(i, i ^ 1) for i in range(cols)])
    return mine, theirs


def neighbours(x, width):
    axes = ("row", "col")
    devices = lax.axis_size("row") * lax.axis_size("col")
    up = [(i, i + 1) for i in range(devices - 1)]
    down = [(j, i) for i, j in up]
    before = lax.ppermute(x[x.shape[0] - width :], axes, up)
    after = lax.ppermute(x[:width], axes, down)
    return before, after


def slab(k, count):
    return k % CORES * (count // CORES) + k // CORES


def rows_dot(a, b):
    return lax.dot_general(a, b, (((0,), (0,)), ((), ())), preferred_element_type=F32)


def head_window(head):
    start = head * HD
    low = start // 128 * 128
    high = -(-(start + HD) // 128) * 128
    return start, low, high


def widened(x_t, head):
    start, low, high = head_window(head)
    parts = []
    if start > low:
        parts.append(jnp.zeros((start - low, x_t.shape[1]), x_t.dtype))
    parts.append(x_t[start : start + HD])
    if high > start + HD:
        parts.append(jnp.zeros((high - start - HD, x_t.shape[1]), x_t.dtype))
    return jnp.concatenate(parts, axis=0)


def project_kernel(normed, grad_new, wq, wg, wout, gate, gated, both):
    query = dot(normed[...], wq[...]).astype(BF)
    opened = sigmoid(dot(normed[...], wg[...]))
    grad = dot_t(grad_new[...].astype(BF), wout[...])
    gate[...] = opened
    gated[...] = grad
    both[:, :D] = query
    both[:, D:] = (grad * opened).astype(BF)


def pack_kernel(both, keys, out):
    for k in range(keys.shape[0]):
        out[k, :, : 2 * D] = both[...]
        out[k, :, 2 * D :] = keys[k]


def forward_kernel(
    core, key_normed, wk, wv, q_mine, q_theirs, g_mine, g_theirs, bias,
    k_t, v_t, q, q_t, g, g_t, mixed, stats, exps, out_t,
):
    half = q_mine.shape[0]
    mine = pl.ds(pl.multiple_of(core[0] * half, half), half)
    theirs = pl.ds(pl.multiple_of((1 - core[0]) * half, half), half)
    q[mine, :] = q_mine[...]
    q[theirs, :] = q_theirs[...]
    g[mine, :] = g_mine[...]
    g[theirs, :] = g_theirs[...]
    q_t[...] = q[...].T
    g_t[...] = g[...].T
    copies = stats.shape[0]
    rows = q.shape[0]
    scale = 1.0 / math.sqrt(HD)
    keys = dot(key_normed[...], wk[...]).astype(BF).T
    values = dot(key_normed[...], wv[...]).astype(BF).T
    k_t[...] = keys
    v_t[...] = values
    lane = lax.broadcasted_iota(jnp.int32, (CHUNK, 128), 1)
    tops = [jnp.zeros((CHUNK, 128), F32) for _ in range(rows // CHUNK)]
    totals = []
    deltas = []
    for head in range(GROUP):
        start, low, high = head_window(head)
        wide = widened(keys, head)
        for part in range(rows // CHUNK):
            at = pl.ds(part * CHUNK, CHUNK)
            score = dot(q[at, low:high], wide) * scale + bias[head, at, :].astype(F32)
            top = jnp.max(score, axis=1, keepdims=True)
            exps[at, :] = jnp.exp(score - top).astype(BF)
            tops[part] = jnp.where(lane == head, top, tops[part])
        ones = jnp.ones((16, values.shape[1]), BF)
        weighted = dot_t(jnp.concatenate([values[start : start + HD], ones], axis=0), exps[...])
        total = weighted[HD : HD + 1]
        one = weighted[:HD] / total
        out_t[start : start + HD, :] = one
        totals.append(total)
        deltas.append(
            jnp.sum(g_t[start : start + HD, :].astype(F32) * one, axis=0, keepdims=True)
        )
    tops_t = jnp.concatenate(tops, axis=0).T[:GROUP]
    lse = tops_t + jnp.log(jnp.concatenate(totals, axis=0))
    delta = jnp.concatenate(deltas, axis=0)
    high = lse.astype(BF).astype(F32)
    middle = (lse - high).astype(BF).astype(F32)
    triple = jnp.concatenate([high, middle, delta], axis=0).astype(BF)
    for copy in range(copies):
        stats[copy, 0] = triple
    straight = out_t[...].T.astype(BF)
    cols, own, _ = mixed.shape
    for k in range(cols):
        at = slice(slab(k, cols) * own, (slab(k, cols) + 1) * own)
        mixed[k] = straight[at]


def token_forward(core, w_keyval, mine, theirs, bias, cols):
    copies = cols // CORES
    half = mine.shape[0]
    tok_col = half
    rows = CORES * half
    span = GROUP * HD
    groups = H // GROUP
    return pl.pallas_call(
        forward_kernel,
        grid=(groups,),
        in_specs=[
            pl.BlockSpec(memory_space=pltpu.SMEM),
            pl.BlockSpec((tok_col, D), lambda i: (0, 2)),
            pl.BlockSpec((D, span), lambda i: (0, i)),
            pl.BlockSpec((D, span), lambda i: (0, groups + i)),
            pl.BlockSpec((half, span), lambda i: (0, i)),
            pl.BlockSpec((half, span), lambda i: (0, i)),
            pl.BlockSpec((half, span), lambda i: (0, groups + i)),
            pl.BlockSpec((half, span), lambda i: (0, groups + i)),
            pl.BlockSpec((GROUP, rows, tok_col), lambda i: (i, 0, 0)),
        ],
        out_specs=[
            pl.BlockSpec((span, tok_col), lambda i: (i, 0)),
            pl.BlockSpec((span, tok_col), lambda i: (i, 0)),
            pl.BlockSpec((rows, span), lambda i: (0, i)),
            pl.BlockSpec((span, rows), lambda i: (i, 0)),
            pl.BlockSpec((rows, span), lambda i: (0, i)),
            pl.BlockSpec((span, rows), lambda i: (i, 0)),
            pl.BlockSpec((cols, rows // cols, span), lambda i: (0, 0, i)),
            pl.BlockSpec((copies, 1, 3 * GROUP, rows), lambda i: (0, i, 0, 0)),
        ],
        out_shape=[
            pltpu.HBM((D, tok_col), BF),
            pltpu.HBM((D, tok_col), BF),
            pltpu.HBM((rows, D), BF),
            pltpu.HBM((D, rows), BF),
            pltpu.HBM((rows, D), BF),
            pltpu.HBM((D, rows), BF),
            pltpu.HBM((cols, rows // cols, D), BF),
            pltpu.HBM((copies, groups, 3 * GROUP, rows), BF),
        ],
        scratch_shapes=[pltpu.VMEM((rows, tok_col), BF), pltpu.VMEM((span, rows), F32)],
        compiler_params=pltpu.CompilerParams(vmem_limit_bytes=VMEM_LIMIT),
        name="token_forward",
    )(core, mine, far(w_keyval), far(w_keyval), mine, theirs, mine, theirs, far(bias))


def backward_kernel(
    mine, theirs, q, q_t, g, g_t, k_t, v_t, bias, q_grad, kv_grad, probs, slopes, q_acc, k_acc, v_acc
):
    rows = q.shape[0]
    tok_col = k_t.shape[1]
    scale = 1.0 / math.sqrt(HD)
    logs = []
    deltas = []
    for part in (mine, theirs):
        for k in range(part.shape[0]):
            triple = part[k, 0].astype(F32)
            logs.append(triple[:GROUP] + triple[GROUP : 2 * GROUP])
            deltas.append(triple[2 * GROUP :])
    top = logs[0]
    for one in logs[1:]:
        top = jnp.maximum(top, one)
    share_sum = jnp.zeros_like(top)
    delta = jnp.zeros_like(top)
    for one, other in zip(logs, deltas):
        share = jnp.exp(one - top)
        share_sum = share_sum + share
        delta = delta + share * other
    lse = top + jnp.log(share_sum)
    delta = delta / share_sum
    filler = jnp.zeros((128 - 2 * GROUP, rows), F32)
    columns = jnp.concatenate([lse, delta, filler], axis=0).T
    for head in range(GROUP):
        start, low, high = head_window(head)
        wide_k = widened(k_t[...], head)
        wide_v = widened(v_t[...], head)
        for part in range(rows // CHUNK):
            at = pl.ds(part * CHUNK, CHUNK)
            some = columns[part * CHUNK : (part + 1) * CHUNK]
            score = dot(q[at, low:high], wide_k) * scale + bias[head, at, :].astype(F32)
            prob = jnp.exp(score - some[:, head : head + 1])
            grad = dot(g[at, low:high], wide_v) - some[:, GROUP + head : GROUP + head + 1]
            probs[at, :] = prob.astype(BF)
            slopes[at, :] = (prob * grad).astype(BF)
        here = pl.ds(start, HD)
        k_acc[here, :] = dot(q_t[here, :], slopes[...]) * scale
        v_acc[here, :] = dot(g_t[here, :], probs[...])
        q_acc[here, :] = dot_t(k_t[here, :], slopes[...]) * scale
    own = kv_grad.shape[2]
    kv_grad[:, 0] = k_acc[...].T.astype(BF).reshape(tok_col // own, own, GROUP * HD)
    kv_grad[:, 1] = v_acc[...].T.astype(BF).reshape(tok_col // own, own, GROUP * HD)
    straight = q_acc[...].T.astype(BF)
    cols = q_grad.shape[0]
    for k in range(cols):
        q_grad[k] = straight[slab(k, cols) * own : (slab(k, cols) + 1) * own]


def token_backward(mine, theirs, q, q_t, g, g_t, k_t, v_t, bias, own):
    rows = q.shape[0]
    tok_col = k_t.shape[1]
    parts = mine.shape[0]
    cols = rows // own
    span = GROUP * HD
    straight = lambda: pl.BlockSpec((rows, span), lambda i: (0, i))
    turned = lambda: pl.BlockSpec((span, rows), lambda i: (i, 0))
    keyed = lambda: pl.BlockSpec((span, tok_col), lambda i: (i, 0))
    steps = tok_col // own
    return pl.pallas_call(
        backward_kernel,
        grid=(H // GROUP,),
        in_specs=[
            pl.BlockSpec((parts, 1, 3 * GROUP, rows), lambda i: (0, i, 0, 0)),
            pl.BlockSpec((parts, 1, 3 * GROUP, rows), lambda i: (0, i, 0, 0)),
            straight(),
            turned(),
            straight(),
            turned(),
            keyed(),
            keyed(),
            pl.BlockSpec((GROUP, rows, tok_col), lambda i: (i, 0, 0)),
        ],
        out_specs=[
            pl.BlockSpec((cols, own, span), lambda i: (0, 0, i)),
            pl.BlockSpec((steps, 2, own, span), lambda i: (0, 0, 0, i)),
        ],
        out_shape=[
            pltpu.HBM((cols, own, D), BF),
            pltpu.HBM((steps, 2, own, D), BF),
        ],
        scratch_shapes=[
            pltpu.VMEM((rows, tok_col), BF),
            pltpu.VMEM((rows, tok_col), BF),
            pltpu.VMEM((span, rows), F32),
            pltpu.VMEM((span, tok_col), F32),
            pltpu.VMEM((span, tok_col), F32),
        ],
        compiler_params=pltpu.CompilerParams(vmem_limit_bytes=VMEM_LIMIT),
        name="token_backward",
    )(mine, theirs, far(q), far(q_t), far(g), far(g_t), far(k_t), far(v_t), far(bias))


def far(x):
    return pltpu.with_memory_space_constraint(x, pltpu.HBM)


def shaped(shape, dtype):
    return jax.ShapeDtypeStruct(shape, dtype)


def whole(kernel, outs, args, name, scalars=0, scratch=()):
    specs = [pl.BlockSpec(memory_space=pltpu.SMEM)] * scalars
    specs += [pl.BlockSpec(memory_space=pltpu.VMEM)] * (len(args) - scalars)
    return pl.pallas_call(
        kernel,
        in_specs=specs,
        out_specs=[pl.BlockSpec(memory_space=pltpu.VMEM)] * len(outs),
        out_shape=list(outs),
        scratch_shapes=list(scratch),
        compiler_params=pltpu.CompilerParams(vmem_limit_bytes=SMALL_LIMIT),
        name=name,
    )(*args)


def head_lanes(head):
    lane = lax.broadcasted_iota(jnp.int32, (1, DA), 1)
    return (lane >= head * AHD) & (lane < (head + 1) * AHD)


def stacked(x):
    return jnp.concatenate(
        [jnp.where(head_lanes(head), x, jnp.zeros_like(x)) for head in range(AH)], axis=0
    )


def unstacked(x):
    total = jnp.zeros((QBLK, DA), F32)
    for head in range(AH):
        total = jnp.where(head_lanes(head), x[head * QBLK : (head + 1) * QBLK], total)
    return total


def picked(start, padded_rows):
    row = lax.broadcasted_iota(jnp.int32, (KWIN, padded_rows), 0)
    lane = lax.broadcasted_iota(jnp.int32, (KWIN, padded_rows), 1)
    return jnp.where(row + start == lane, 1.0, 0.0).astype(BF)


def atoms_forward_kernel(
    starts, before, atoms, after, bias, token, gain, wq, wkv, wo, wagg, cot, tokens, tokens_cot,
    part, mid, slope, query, window, prob, mixed,
):
    atom_dev = atoms.shape[0]
    blocks = window.shape[0]
    cols, own, _ = part.shape
    tok_row = cols * own
    scale = 1.0 / math.sqrt(AHD)
    padded = jnp.concatenate([before[...], atoms[...], after[...]], axis=0).astype(F32)
    padded_rows = padded.shape[0]
    normed = layer_norm(padded, gain[...]).astype(BF)
    query[...] = dot(normed[RIM : RIM + atom_dev], wq[...]).astype(BF)
    keyval = dot(normed, wkv[...]).astype(BF)
    for block in range(blocks):
        at = pl.ds(block * QBLK, QBLK)
        rows = dot(picked(starts[block], padded_rows), keyval).astype(BF)
        window[block] = rows
        score = dot_t(stacked(query[at, :]), rows[:, :DA]) * scale + bias[block].astype(F32)
        exps = jnp.exp(score - jnp.max(score, axis=-1, keepdims=True))
        one = exps / jnp.sum(exps, axis=-1, keepdims=True)
        prob[block] = one
        mixed[at, :] = unstacked(dot(one.astype(BF), rows[:, DA:])).astype(BF)
    mid[...] = (atoms[...].astype(F32) + dot(mixed[...], wo[...])).astype(BF)
    slot = lax.broadcasted_iota(jnp.int32, (tok_row, atom_dev), 0)
    member = jnp.where(slot == token[...], 1.0, 0.0).astype(BF)
    width = tokens.shape[0]
    cot_part = dot(member, cot[...]).astype(BF)
    blank = jnp.zeros((part.shape[2] - D - DA - 2 * width, tok_row), BF)
    rest = jnp.concatenate([tokens[...], tokens_cot[...], blank], axis=0).T
    for k in range(cols):
        at = slice(slab(k, cols) * own, (slab(k, cols) + 1) * own)
        part[k, :, D : D + DA] = cot_part[at]
        part[k, :, D + DA :] = rest[at]
    for low in range(0, D, 256):
        at = pl.ds(low, 256)
        pre = dot(mid[...], wagg[:, at])
        gate = sigmoid(pre)
        slope[:, at] = gate * (1.0 + pre * (1.0 - gate))
        sums = dot(member, (pre * gate).astype(BF)).astype(BF)
        for k in range(cols):
            part[k, :, at] = sums[slab(k, cols) * own : (slab(k, cols) + 1) * own]


def summed(parts):
    total = parts[0].astype(F32)
    for k in range(1, parts.shape[0]):
        total = total + parts[k].astype(F32)
    return total


def norm_kernel(parts, inverse, gain, wt2a, mid, normed, grad_new, spread):
    cols = parts.shape[0]
    width = D // cols
    total = summed(parts[:, :, : D + DA])
    for k in range(cols):
        at = slice(k * width, (k + 1) * width)
        low = D + DA
        mid[:, at] = parts[k, :, low : low + width].astype(F32)
        grad_new[:, at] = parts[k, :, low + width : low + 2 * width].astype(F32)
    grad = grad_new[...] + dot_t(total[:, D:].astype(BF), wt2a[...])
    grad_new[...] = grad
    value = mid[...] + total[:, :D] * inverse[...]
    mid[...] = value
    out = layer_norm(value, gain[...]).astype(BF)
    normed[...] = out
    for k in range(spread.shape[0]):
        spread[k] = out


def keyval_kernel(parts, w, out):
    total = summed(parts).astype(BF)
    out[...] = dot_t(total[0], w[:, :D]) + dot_t(total[1], w[:, D:])


def own_kernel(
    place, parts, mine, theirs, gate_ref, gated_ref, token_mid, wout, wgate, wt2a, tokens, lifted, feature, attended
):
    cols, own, _ = parts.shape
    span = GROUP * HD
    lane = lax.broadcasted_iota(jnp.int32, (GROUP, span), 1)
    row = lax.broadcasted_iota(jnp.int32, (GROUP, span), 0)
    widen = jnp.where((lane >= row * HD) & (lane < (row + 1) * HD), 1.0, 0.0).astype(BF)
    half = cols // CORES
    rows = mine.shape[3]
    slot = lax.broadcasted_iota(jnp.int32, (rows, own), 0)
    token = lax.broadcasted_iota(jnp.int32, (rows, own), 1)
    select = jnp.where(slot == token + place[0], 1.0, 0.0).astype(BF)
    tables = []
    for part in (mine, theirs):
        flat = part[...].reshape(half * (H // GROUP) * 3 * GROUP, rows)
        tables.append(dot(flat, select).T)
    for group in range(H // GROUP):
        logs = []
        for k in range(cols):
            low = (k // CORES * (H // GROUP) + group) * 3 * GROUP
            mine_first = jnp.where(place[1] == k % CORES, 1.0, 0.0)
            triple = (
                tables[0][:, low : low + 2 * GROUP] * mine_first
                + tables[1][:, low : low + 2 * GROUP] * (1.0 - mine_first)
            )
            logs.append(triple[:, :GROUP] + triple[:, GROUP:])
        top = logs[0]
        for k in range(1, cols):
            top = jnp.maximum(top, logs[k])
        shares = [jnp.exp(one - top) for one in logs]
        total = shares[0]
        for k in range(1, cols):
            total = total + shares[k]
        value = jnp.zeros((own, span), F32)
        for k in range(cols):
            share = shares[k] / total
            high = share.astype(BF)
            rest = (share - high.astype(F32)).astype(BF)
            weight = dot(high, widen) + dot(rest, widen)
            at = slice(group * span, (group + 1) * span)
            value = value + weight * parts[k, :, at].astype(F32)
        attended[:, group * span : (group + 1) * span] = value
    gate = gate_ref[...]
    value = attended[...]
    new = (token_mid[...] + dot((gate * value).astype(BF), wout[...])).astype(BF)
    tokens[...] = new
    lifted[...] = dot(new, wt2a[...]).astype(BF)
    grad_gate = (gated_ref[...] * value * gate * (1.0 - gate)).astype(BF)
    feature[...] = dot_t(grad_gate, wgate[...])


def token_kernel(parts, key_feature, feature, grad_new, token_mid, gain, wquery, tokens, lifted, out):
    cols = parts.shape[0]
    width = D // cols
    total = summed(parts[...]).astype(BF)
    normed_grad = dot_t(total, wquery[...]) + feature[...] + key_feature[...]
    grad = grad_new[...] + norm_back(token_mid[...], gain[...], normed_grad)
    grad = grad.astype(BF)
    new = tokens[...]
    low = D + DA
    pair = CORES * width
    for k in range(cols // CORES):
        out[k, :, :D] = grad
        out[k, :, D:low] = lifted[...]
        out[k, :, low:] = new[:, k * pair : (k + 1) * pair]


def atoms_backward_kernel(
    starts, place, mine, theirs, token, inverse, slope, cot, mid, query, window, prob, mixed,
    wagg, wo, wq, new, tokens_out, grad_tokens, inner, first, last, atoms_grad, feature, padded,
):
    atom_dev = cot.shape[0]
    blocks = window.shape[0]
    half = mine.shape[0]
    tok_row = CORES * half
    width = tokens_out.shape[1]
    core = place[0]
    padded_rows = padded.shape[0]
    scale = 1.0 / math.sqrt(AHD)
    slot = lax.broadcasted_iota(jnp.int32, (atom_dev, tok_row), 1)
    atom_inverse = jnp.sum(
        jnp.where(slot == token[...], inverse[...], 0.0), axis=1, keepdims=True
    )
    parts = ((mine, core * half), (theirs, (1 - core) * half))
    slot = lax.broadcasted_iota(jnp.int32, (atom_dev, half), 1)
    members = [
        jnp.where(slot + base == token[...], 1.0, 0.0).astype(BF) for _, base in parts
    ]

    def gathered(at):
        return dot(members[0], mine[:, at]) + dot(members[1], theirs[:, at])

    row = lax.broadcasted_iota(jnp.int32, (D, width), 0)
    lane = lax.broadcasted_iota(jnp.int32, (D, width), 1)
    column = jnp.where(row == lane + place[1] * width, 1.0, 0.0).astype(BF)
    for part, base in parts:
        here = pl.ds(pl.multiple_of(base, half), half)
        low = D + DA
        pair = part[:, low:].astype(F32)
        tokens_out[here, :] = jnp.where(core == 0, pair[:, :width], pair[:, width:]).astype(BF)
        grad_tokens[here, :] = dot(part[:, :D], column).astype(BF)
    grads = cot[...].astype(F32)
    for low in range(0, D, 256):
        at = pl.ds(low, 256)
        hidden = (gathered(at) * atom_inverse * slope[:, at]).astype(BF)
        grads = grads + dot_t(hidden, wagg[:, at])
    atoms_grad[...] = grads
    mixed_grad = dot_t(grads.astype(BF), wo[...]).astype(BF)
    padded[...] = jnp.zeros(padded.shape, F32)
    for block in range(blocks):
        at = slice(block * QBLK, (block + 1) * QBLK)
        rows = window[block]
        one = prob[block]
        grad_heads = stacked(mixed_grad[at])
        query_heads = stacked(query[at, :])
        grad_wide = grad_heads.astype(F32)
        tall = jnp.concatenate([mixed[at, :]] * AH, axis=0).astype(F32)
        delta = jnp.sum(grad_wide * tall, axis=-1, keepdims=True)
        sgrad = (one * (dot_t(grad_heads, rows[:, DA:]) - delta)).astype(BF)
        qgrad = (unstacked(dot(sgrad, rows[:, :DA])) * scale).astype(BF)
        feature[at, :] = dot_t(qgrad, wq[...])
        key_grad = rows_dot(sgrad, query_heads) * scale
        value_grad = rows_dot(one.astype(BF), grad_heads)
        both = jnp.concatenate([key_grad, value_grad], axis=1).astype(BF)
        padded[...] += rows_dot(picked(starts[block], padded_rows), both)
    first[...] = padded[:RIM, :].astype(BF)
    last[...] = padded[RIM + atom_dev :, :].astype(BF)
    inner[...] = padded[RIM : RIM + atom_dev, :]
    lift = gathered(slice(D, D + DA))
    new[...] = (mid[...].astype(F32) + lift).astype(BF)


def atoms_last_kernel(inner, before, after, feature, atoms_grad, atoms, gain, wkv, out):
    atom_dev = atoms.shape[0]
    keyval = jnp.concatenate(
        [
            inner[:RIM, :] + before[...].astype(F32),
            inner[RIM : atom_dev - RIM, :],
            inner[atom_dev - RIM :, :] + after[...].astype(F32),
        ],
        axis=0,
    ).astype(BF)
    feat = feature[...] + dot_t(keyval, wkv[...])
    back = norm_back(atoms[...].astype(F32), gain[...], feat)
    out[...] = (atoms_grad[...] + back).astype(BF)


def local(
    atoms,
    tokens,
    atom_bias,
    token_bias,
    atom_index,
    atom_counts,
    window_starts,
    gain_atom,
    w_atom_q,
    w_atom_kv,
    w_atom_o,
    w_agg,
    gain_token,
    w_query,
    w_keyval,
    w_gate,
    w_out,
    w_t2a,
    atoms_cot,
    tokens_cot,
):
    rows = lax.axis_size("row")
    cols = lax.axis_size("col")
    row_index = lax.axis_index("row")
    col_index = lax.axis_index("col")
    atom_dev = atoms.shape[0]
    blocks = window_starts.shape[0]
    tok_row = tokens.shape[0]
    tok_col = token_bias.shape[2]
    own = tok_row // cols
    width = tokens.shape[1]
    first_atom = (row_index * cols + col_index) * atom_dev

    before, after = neighbours(atoms, RIM)

    local_token = atom_index - row_index * tok_row
    inverse_count = 1.0 / atom_counts.astype(F32)
    core = col_index % CORES
    half = tok_row // CORES
    first_own = core * half + col_index // CORES * own
    inv_own = lax.dynamic_slice_in_dim(inverse_count, first_own, own, 0)

    starts = window_starts - first_atom + RIM
    gain_a = gain_atom[None, :]
    gain_t = gain_token[None, :]
    part, atoms_mid, slope, atom_query, window, atom_prob, atom_mixed = whole(
        atoms_forward_kernel,
        [
            pltpu.HBM((cols, own, D + 2 * DA), BF),
            pltpu.HBM((atom_dev, DA), BF),
            pltpu.HBM((atom_dev, D), F32),
            pltpu.HBM((atom_dev, DA), BF),
            pltpu.HBM((blocks, KWIN, 2 * DA), BF),
            pltpu.HBM((blocks, AH * QBLK, KWIN), F32),
            pltpu.HBM((atom_dev, DA), BF),
        ],
        (
            starts,
            before,
            far(atoms),
            after,
            far(atom_bias.reshape(blocks, AH * QBLK, KWIN)),
            local_token[None, :],
            gain_a,
            far(w_atom_q),
            far(w_atom_kv),
            far(w_atom_o),
            far(w_agg),
            far(atoms_cot),
            far(tokens.T),
            far(tokens_cot.T),
        ),
        "atoms_forward",
        scalars=1,
    )

    sums = exchange(part, "col")
    tokens_mid, normed_own, grad_new, spread = whole(
        norm_kernel,
        [
            pltpu.HBM((own, D), F32),
            shaped((own, D), BF),
            pltpu.HBM((own, D), F32),
            pltpu.HBM((rows, own, D), BF),
        ],
        (sums, inv_own[:, None], gain_t, far(w_t2a)),
        "token_norm",
    )
    keys_own = exchange(spread, "row")
    gate_own, gated_own, both = whole(
        project_kernel,
        [pltpu.HBM((own, D), F32), pltpu.HBM((own, D), F32), shaped((own, 2 * D), BF)],
        (normed_own, grad_new, w_query, w_gate, w_out),
        "token_project",
    )
    (packed,) = whole(
        pack_kernel, [pltpu.HBM((rows, own, 3 * D), BF)], (both, keys_own), "token_pack"
    )
    mine, theirs = halves_of(packed)
    to_row = [
        (i * cols + r * CORES + p, r * cols + i * CORES + p)
        for r in range(rows)
        for i in range(rows)
        for p in range(CORES)
    ]
    k_t, v_t, q, q_t, g, g_t, mixed, stats = token_forward(
        core[None],
        w_keyval,
        mine.reshape(half, 3 * D),
        theirs.reshape(half, 3 * D),
        token_bias,
        cols,
    )
    stats = halves_of(stats)
    mixed_parts = exchange(mixed, "col")
    q_grad, kv_grad = token_backward(*stats, q, q_t, g, g_t, k_t, v_t, token_bias, own)
    kv_parts = exchange(kv_grad, "row")
    q_parts = exchange(q_grad, "col")
    tokens_new, lifted, gate_feat = whole(
        own_kernel,
        [shaped((own, D), BF), shaped((own, DA), BF), shaped((own, D), F32)],
        (
            jnp.stack([first_own, core]),
            mixed_parts,
            *stats,
            far(gate_own),
            far(gated_own),
            far(tokens_mid),
            far(w_out),
            far(w_gate),
            far(w_t2a),
        ),
        "token_own",
        scalars=1,
        scratch=[pltpu.VMEM((own, D), F32)],
    )
    (kv_feat,) = whole(
        keyval_kernel,
        [shaped((own, D), F32)],
        (kv_parts, far(w_keyval)),
        "token_keyval",
    )
    kv_back = lax.ppermute(kv_feat, ("row", "col"), to_row)
    (mid_spread,) = whole(
        token_kernel,
        [pltpu.HBM((cols // CORES, own, D + DA + CORES * width), BF)],
        (
            q_parts,
            kv_back,
            gate_feat,
            far(grad_new),
            far(tokens_mid),
            gain_t,
            far(w_query),
            tokens_new,
            lifted,
        ),
        "token_grads",
    )
    mine, theirs = halves_of(mid_spread)

    atoms_new, tokens_out, grad_tokens, inner, first, last, atoms_grad, query_feat = whole(
        atoms_backward_kernel,
        [
            shaped((atom_dev, DA), BF),
            shaped((tok_row, width), BF),
            shaped((tok_row, width), BF),
            shaped((atom_dev, 2 * DA), F32),
            shaped((RIM, 2 * DA), BF),
            shaped((RIM, 2 * DA), BF),
            shaped((atom_dev, DA), F32),
            shaped((atom_dev, DA), F32),
        ],
        (
            starts,
            jnp.stack([core, col_index]),
            mine.reshape(half, -1),
            theirs.reshape(half, -1),
            local_token[:, None],
            inverse_count[None, :],
            far(slope),
            far(atoms_cot),
            far(atoms_mid),
            far(atom_query),
            far(window),
            far(atom_prob),
            far(atom_mixed),
            far(w_agg),
            far(w_atom_o),
            far(w_atom_q),
        ),
        "atoms_backward",
        scalars=2,
        scratch=[pltpu.VMEM((atom_dev + 2 * RIM, 2 * DA), F32)],
    )
    axes = ("row", "col")
    up = [(i, i + 1) for i in range(rows * cols - 1)]
    down = [(j, i) for i, j in up]
    from_before = lax.ppermute(last, axes, up)
    from_after = lax.ppermute(first, axes, down)
    (grad_atoms,) = whole(
        atoms_last_kernel,
        [shaped((atom_dev, DA), BF)],
        (
            inner,
            from_before,
            from_after,
            query_feat,
            atoms_grad,
            far(atoms),
            gain_a,
            far(w_atom_kv),
        ),
        "atoms_last",
    )
    return (atoms_new, tokens_out, grad_atoms, grad_tokens)


def solution(mesh):
    placed = (
        P(("row", "col"), None),
        P("row", "col"),
        P(("row", "col"), None, None, None),
        P(None, "row", "col"),
        P(("row", "col")),
        P("row"),
        P(("row", "col")),
        P(),
        P(),
        P(),
        P(),
        P(),
        P(),
        P(),
        P(),
        P(),
        P(),
        P(),
        P(("row", "col"), None),
        P("row", "col"),
    )
    return jax.shard_map(
        local,
        mesh=mesh,
        in_specs=placed,
        out_specs=(
            P(("row", "col"), None),
            P("row", "col"),
            P(("row", "col"), None),
            P("row", "col"),
        ),
        check_vma=False,
    )
```

```python
import math

import jax
import jax.numpy as jnp
from jax import lax
from jax.experimental import pallas as pl
from jax.experimental.pallas import tpu as pltpu
from jax.sharding import PartitionSpec as P

D = 768
H = 16
HD = 48
DA = 128
AH = 4
AHD = 32
QBLK = 32
KWIN = 128
RIM = 64
EPS = 1e-05
BF = jnp.bfloat16
F32 = jnp.float32
GROUP = 8
CORES = 2
CHUNK = 128
VMEM_LIMIT = 24 * 1024 * 1024
SMALL_LIMIT = 14 * 1024 * 1024


def dot(a, b):
    return jnp.dot(a, b, preferred_element_type=F32)


def dot_t(a, b):
    return lax.dot_general(a, b, (((1,), (1,)), ((), ())), preferred_element_type=F32)


def centred(values):
    center = values - jnp.mean(values, axis=-1, keepdims=True)
    inv = lax.rsqrt(jnp.mean(center * center, axis=-1, keepdims=True) + EPS)
    return center * inv, inv


def layer_norm(values, gain_vec):
    return centred(values)[0] * gain_vec


def norm_back(values, gain_vec, cotangent):
    unit, inv = centred(values)
    g = cotangent * gain_vec
    return inv * (
        g
        - jnp.mean(g, axis=-1, keepdims=True)
        - unit * jnp.mean(g * unit, axis=-1, keepdims=True)
    )


def sigmoid(x):
    return 1.0 / (1.0 + jnp.exp(-x))


def exchange(x, axis):
    return lax.all_to_all(x, axis, 0, 0)


def among_core(x):
    cols = lax.axis_size("col")
    groups = [list(range(core, cols, CORES)) for core in range(CORES)]
    return lax.all_to_all(x, "col", 0, 0, axis_index_groups=groups)


def halves_of(x):
    cols = lax.axis_size("col")
    mine = among_core(x)
    theirs = lax.ppermute(mine, "col", [(i, i ^ 1) for i in range(cols)])
    return mine, theirs


def neighbours(x, width):
    axes = ("row", "col")
    devices = lax.axis_size("row") * lax.axis_size("col")
    up = [(i, i + 1) for i in range(devices - 1)]
    down = [(j, i) for i, j in up]
    before = lax.ppermute(x[x.shape[0] - width :], axes, up)
    after = lax.ppermute(x[:width], axes, down)
    return before, after


def slab(k, count):
    return k % CORES * (count // CORES) + k // CORES


def rows_dot(a, b):
    return lax.dot_general(a, b, (((0,), (0,)), ((), ())), preferred_element_type=F32)


def head_window(head):
    start = head * HD
    low = start // 128 * 128
    high = -(-(start + HD) // 128) * 128
    return start, low, high


def widened(x_t, head):
    start, low, high = head_window(head)
    parts = []
    if start > low:
        parts.append(jnp.zeros((start - low, x_t.shape[1]), x_t.dtype))
    parts.append(x_t[start : start + HD])
    if high > start + HD:
        parts.append(jnp.zeros((high - start - HD, x_t.shape[1]), x_t.dtype))
    return jnp.concatenate(parts, axis=0)


def project_kernel(normed, grad_new, wq, wg, wout, gate, gated, both):
    query = dot(normed[...], wq[...]).astype(BF)
    opened = sigmoid(dot(normed[...], wg[...]))
    grad = dot_t(grad_new[...].astype(BF), wout[...])
    gate[...] = opened
    gated[...] = grad
    grad = (grad * opened).astype(BF)
    for k in range(both.shape[0]):
        both[k, :, :D] = query
        both[k, :, D:] = grad


def token_project(normed, grad_new, w_query, w_gate, w_out, copies):
    own = normed.shape[0]
    full = lambda *shape: pl.BlockSpec(shape, lambda i: (0,) * len(shape))
    return pl.pallas_call(
        project_kernel,
        grid=(1,),
        in_specs=[full(own, D), full(own, D), full(D, D), full(D, D), full(D, D)],
        out_specs=[full(own, D), full(own, D), full(copies, own, 2 * D)],
        out_shape=[
            pltpu.HBM((own, D), F32),
            pltpu.HBM((own, D), F32),
            pltpu.HBM((copies, own, 3 * D), BF),
        ],
        compiler_params=pltpu.CompilerParams(vmem_limit_bytes=SMALL_LIMIT),
        name="token_project",
    )(normed, grad_new, w_query, w_gate, w_out)


def pack_kernel(packed, keys, out):
    out[...] = keys[...]


def token_pack(packed, keys):
    return pl.pallas_call(
        pack_kernel,
        grid=(1,),
        in_specs=[
            pl.BlockSpec(memory_space=pl.ANY),
            pl.BlockSpec(keys.shape, lambda i: (0, 0, 0)),
        ],
        out_specs=pl.BlockSpec(keys.shape, lambda i: (0, 0, 2)),
        out_shape=pltpu.HBM(packed.shape, BF),
        input_output_aliases={0: 0},
        compiler_params=pltpu.CompilerParams(vmem_limit_bytes=SMALL_LIMIT),
        name="token_pack",
    )(packed, keys)


def key_kernel(key_normed, wk, wv, k_t, v_t):
    k_t[...] = dot(key_normed[...], wk[...]).astype(BF).T
    v_t[...] = dot(key_normed[...], wv[...]).astype(BF).T


def token_keys(mine, w_keyval):
    tok_col = mine.shape[0]
    span = GROUP * HD
    groups = H // GROUP
    return pl.pallas_call(
        key_kernel,
        grid=(groups,),
        in_specs=[
            pl.BlockSpec((tok_col, D), lambda i: (0, 2)),
            pl.BlockSpec((D, span), lambda i: (0, i)),
            pl.BlockSpec((D, span), lambda i: (0, groups + i)),
        ],
        out_specs=[pl.BlockSpec((span, tok_col), lambda i: (i, 0)) for _ in range(2)],
        out_shape=[pltpu.HBM((D, tok_col), BF) for _ in range(2)],
        compiler_params=pltpu.CompilerParams(vmem_limit_bytes=SMALL_LIMIT),
        name="token_keys",
    )(mine, far(w_keyval), far(w_keyval))


def forward_kernel(
    core, k_t, v_t, q_mine, q_theirs, g_mine, g_theirs, bias,
    q, q_t, g, g_t, mixed, stats, exps, out_t,
):
    half = q_mine.shape[0]
    mine = pl.ds(pl.multiple_of(core[0] * half, half), half)
    theirs = pl.ds(pl.multiple_of((1 - core[0]) * half, half), half)
    q[mine, :] = q_mine[...]
    q[theirs, :] = q_theirs[...]
    g[mine, :] = g_mine[...]
    g[theirs, :] = g_theirs[...]
    q_t[...] = q[...].T
    g_t[...] = g[...].T
    copies = stats.shape[0]
    rows = q.shape[0]
    scale = 1.0 / math.sqrt(HD)
    keys = k_t[...]
    values = v_t[...]
    lane = lax.broadcasted_iota(jnp.int32, (CHUNK, 128), 1)
    tops = [jnp.zeros((CHUNK, 128), F32) for _ in range(rows // CHUNK)]
    totals = []
    deltas = []
    for head in range(GROUP):
        start, low, high = head_window(head)
        wide = widened(keys, head)
        for part in range(rows // CHUNK):
            at = pl.ds(part * CHUNK, CHUNK)
            score = dot(q[at, low:high], wide) * scale + bias[head, at, :].astype(F32)
            top = jnp.max(score, axis=1, keepdims=True)
            exps[at, :] = jnp.exp(score - top).astype(BF)
            tops[part] = jnp.where(lane == head, top, tops[part])
        ones = jnp.ones((16, values.shape[1]), BF)
        weighted = dot_t(jnp.concatenate([values[start : start + HD], ones], axis=0), exps[...])
        total = weighted[HD : HD + 1]
        one = weighted[:HD] / total
        out_t[start : start + HD, :] = one
        totals.append(total)
        deltas.append(
            jnp.sum(g_t[start : start + HD, :].astype(F32) * one, axis=0, keepdims=True)
        )
    tops_t = jnp.concatenate(tops, axis=0).T[:GROUP]
    lse = tops_t + jnp.log(jnp.concatenate(totals, axis=0))
    delta = jnp.concatenate(deltas, axis=0)
    high = lse.astype(BF).astype(F32)
    middle = (lse - high).astype(BF).astype(F32)
    triple = jnp.concatenate([high, middle, delta], axis=0).astype(BF)
    for copy in range(copies):
        stats[copy, 0] = triple
    straight = out_t[...].astype(BF).T
    cols, own, _ = mixed.shape
    for k in range(cols):
        at = slice(slab(k, cols) * own, (slab(k, cols) + 1) * own)
        mixed[k] = straight[at]


def token_forward(core, k_t, v_t, mine, theirs, bias, cols):
    copies = cols // CORES
    half = mine.shape[0]
    tok_col = half
    rows = CORES * half
    span = GROUP * HD
    groups = H // GROUP
    return pl.pallas_call(
        forward_kernel,
        grid=(groups,),
        in_specs=[
            pl.BlockSpec(memory_space=pltpu.SMEM),
            pl.BlockSpec((span, tok_col), lambda i: (i, 0)),
            pl.BlockSpec((span, tok_col), lambda i: (i, 0)),
            pl.BlockSpec((half, span), lambda i: (0, i)),
            pl.BlockSpec((half, span), lambda i: (0, i)),
            pl.BlockSpec((half, span), lambda i: (0, groups + i)),
            pl.BlockSpec((half, span), lambda i: (0, groups + i)),
            pl.BlockSpec((GROUP, rows, tok_col), lambda i: (i, 0, 0)),
        ],
        out_specs=[
            pl.BlockSpec((rows, span), lambda i: (0, i)),
            pl.BlockSpec((span, rows), lambda i: (i, 0)),
            pl.BlockSpec((rows, span), lambda i: (0, i)),
            pl.BlockSpec((span, rows), lambda i: (i, 0)),
            pl.BlockSpec((cols, rows // cols, span), lambda i: (0, 0, i)),
            pl.BlockSpec((copies, 1, 3 * GROUP, rows), lambda i: (0, i, 0, 0)),
        ],
        out_shape=[
            pltpu.HBM((rows, D), BF),
            pltpu.HBM((D, rows), BF),
            pltpu.HBM((rows, D), BF),
            pltpu.HBM((D, rows), BF),
            pltpu.HBM((cols, rows // cols, D), BF),
            pltpu.HBM((copies, groups, 3 * GROUP, rows), BF),
        ],
        scratch_shapes=[pltpu.VMEM((rows, tok_col), BF), pltpu.VMEM((span, rows), F32)],
        compiler_params=pltpu.CompilerParams(vmem_limit_bytes=VMEM_LIMIT),
        name="token_forward",
    )(core, far(k_t), far(v_t), mine, theirs, mine, theirs, far(bias))


def backward_kernel(
    core, mine, theirs, q, q_t, g, g_t, k_t, v_t, bias, wk, wv, q_mine, q_theirs, kv_feat,
    probs, slopes, q_acc, k_acc, v_acc, straight, feat,
):
    rows = q.shape[0]
    tok_col = k_t.shape[1]
    scale = 1.0 / math.sqrt(HD)
    logs = []
    deltas = []
    for part in (mine, theirs):
        for k in range(part.shape[0]):
            triple = part[k, 0].astype(F32)
            logs.append(triple[:GROUP] + triple[GROUP : 2 * GROUP])
            deltas.append(triple[2 * GROUP :])
    top = logs[0]
    for one in logs[1:]:
        top = jnp.maximum(top, one)
    share_sum = jnp.zeros_like(top)
    delta = jnp.zeros_like(top)
    for one, other in zip(logs, deltas):
        share = jnp.exp(one - top)
        share_sum = share_sum + share
        delta = delta + share * other
    lse = top + jnp.log(share_sum)
    delta = delta / share_sum
    filler = jnp.zeros((128 - 2 * GROUP, rows), F32)
    columns = jnp.concatenate([lse, delta, filler], axis=0).T
    for head in range(GROUP):
        start, low, high = head_window(head)
        wide_k = widened(k_t[...], head)
        wide_v = widened(v_t[...], head)
        for part in range(rows // CHUNK):
            at = pl.ds(part * CHUNK, CHUNK)
            some = columns[part * CHUNK : (part + 1) * CHUNK]
            score = dot(q[at, low:high], wide_k) * scale + bias[head, at, :].astype(F32)
            prob = jnp.exp(score - some[:, head : head + 1])
            grad = dot(g[at, low:high], wide_v) - some[:, GROUP + head : GROUP + head + 1]
            probs[at, :] = prob.astype(BF)
            slopes[at, :] = (prob * grad).astype(BF)
        here = pl.ds(start, HD)
        k_acc[here, :] = dot(q_t[here, :], slopes[...]) * scale
        v_acc[here, :] = dot(g_t[here, :], probs[...])
        q_acc[here, :] = dot_t(k_t[here, :], slopes[...]) * scale
    new = dot(wk[...], k_acc[...].astype(BF)) + dot(wv[...], v_acc[...].astype(BF))

    @pl.when(pl.program_id(0) == 0)
    def _():
        feat[...] = new

    @pl.when(pl.program_id(0) > 0)
    def _():
        kv_feat[...] = (feat[...] + new).astype(BF).T

    straight[...] = q_acc[...].astype(BF).T
    half = q_mine.shape[0]
    q_mine[...] = straight[pl.ds(pl.multiple_of(core[0] * half, half), half), :]
    q_theirs[...] = straight[pl.ds(pl.multiple_of((1 - core[0]) * half, half), half), :]


def token_backward(core, mine, theirs, q, q_t, g, g_t, k_t, v_t, bias, w_keyval):
    rows = q.shape[0]
    tok_col = k_t.shape[1]
    parts = mine.shape[0]
    half = rows // CORES
    groups = H // GROUP
    span = GROUP * HD
    straight = lambda: pl.BlockSpec((rows, span), lambda i: (0, i))
    turned = lambda: pl.BlockSpec((span, rows), lambda i: (i, 0))
    keyed = lambda: pl.BlockSpec((span, tok_col), lambda i: (i, 0))
    return pl.pallas_call(
        backward_kernel,
        grid=(groups,),
        in_specs=[
            pl.BlockSpec(memory_space=pltpu.SMEM),
            pl.BlockSpec((parts, 1, 3 * GROUP, rows), lambda i: (0, i, 0, 0)),
            pl.BlockSpec((parts, 1, 3 * GROUP, rows), lambda i: (0, i, 0, 0)),
            straight(),
            turned(),
            straight(),
            turned(),
            keyed(),
            keyed(),
            pl.BlockSpec((GROUP, rows, tok_col), lambda i: (i, 0, 0)),
            pl.BlockSpec((D, span), lambda i: (0, i)),
            pl.BlockSpec((D, span), lambda i: (0, groups + i)),
        ],
        out_specs=[
            pl.BlockSpec((half, span), lambda i: (0, i)),
            pl.BlockSpec((half, span), lambda i: (0, i)),
            pl.BlockSpec((tok_col, D), lambda i: (0, 0)),
        ],
        out_shape=[
            pltpu.HBM((half, D), BF),
            pltpu.HBM((half, D), BF),
            pltpu.HBM((tok_col, D), BF),
        ],
        scratch_shapes=[
            pltpu.VMEM((rows, tok_col), BF),
            pltpu.VMEM((rows, tok_col), BF),
            pltpu.VMEM((span, rows), F32),
            pltpu.VMEM((span, tok_col), F32),
            pltpu.VMEM((span, tok_col), F32),
            pltpu.VMEM((rows, span), BF),
            pltpu.VMEM((D, tok_col), F32),
        ],
        compiler_params=pltpu.CompilerParams(vmem_limit_bytes=VMEM_LIMIT),
        name="token_backward",
    )(
        core,
        mine,
        theirs,
        far(q),
        far(q_t),
        far(g),
        far(g_t),
        far(k_t),
        far(v_t),
        far(bias),
        far(w_keyval),
        far(w_keyval),
    )


def far(x):
    return pltpu.with_memory_space_constraint(x, pltpu.HBM)


def shaped(shape, dtype):
    return jax.ShapeDtypeStruct(shape, dtype)


def whole(kernel, outs, args, name, scalars=0, scratch=()):
    specs = [pl.BlockSpec(memory_space=pltpu.SMEM)] * scalars
    specs += [pl.BlockSpec(memory_space=pltpu.VMEM)] * (len(args) - scalars)
    return pl.pallas_call(
        kernel,
        in_specs=specs,
        out_specs=[pl.BlockSpec(memory_space=pltpu.VMEM)] * len(outs),
        out_shape=list(outs),
        scratch_shapes=list(scratch),
        compiler_params=pltpu.CompilerParams(vmem_limit_bytes=SMALL_LIMIT),
        name=name,
    )(*args)


def head_lanes(head):
    lane = lax.broadcasted_iota(jnp.int32, (1, DA), 1)
    return (lane >= head * AHD) & (lane < (head + 1) * AHD)


def stacked(x):
    return jnp.concatenate(
        [jnp.where(head_lanes(head), x, jnp.zeros_like(x)) for head in range(AH)], axis=0
    )


def unstacked(x):
    total = jnp.zeros((QBLK, DA), F32)
    for head in range(AH):
        total = jnp.where(head_lanes(head), x[head * QBLK : (head + 1) * QBLK], total)
    return total


def picked(start, padded_rows):
    row = lax.broadcasted_iota(jnp.int32, (KWIN, padded_rows), 0)
    lane = lax.broadcasted_iota(jnp.int32, (KWIN, padded_rows), 1)
    return jnp.where(row + start == lane, 1.0, 0.0).astype(BF)


def atoms_forward_kernel(
    starts, before, atoms, after, bias, token, gain, wq, wkv, wo, wagg, cot, tokens, tokens_cot,
    part, mid, slope, query, window, prob, mixed,
):
    atom_dev = atoms.shape[0]
    blocks = window.shape[0]
    cols, own, _ = part.shape
    tok_row = cols * own
    scale = 1.0 / math.sqrt(AHD)
    padded = jnp.concatenate([before[...], atoms[...], after[...]], axis=0).astype(F32)
    padded_rows = padded.shape[0]
    normed = layer_norm(padded, gain[...]).astype(BF)
    query[...] = dot(normed[RIM : RIM + atom_dev], wq[...]).astype(BF)
    keyval = dot(normed, wkv[...]).astype(BF)
    for block in range(blocks):
        at = pl.ds(block * QBLK, QBLK)
        rows = dot(picked(starts[block], padded_rows), keyval).astype(BF)
        window[block] = rows
        score = dot_t(stacked(query[at, :]), rows[:, :DA]) * scale + bias[block].astype(F32)
        exps = jnp.exp(score - jnp.max(score, axis=-1, keepdims=True))
        one = exps / jnp.sum(exps, axis=-1, keepdims=True)
        prob[block] = one
        mixed[at, :] = unstacked(dot(one.astype(BF), rows[:, DA:])).astype(BF)
    mid[...] = (atoms[...].astype(F32) + dot(mixed[...], wo[...])).astype(BF)
    slot = lax.broadcasted_iota(jnp.int32, (tok_row, atom_dev), 0)
    member = jnp.where(slot == token[...], 1.0, 0.0).astype(BF)
    width = tokens.shape[0]
    cot_part = dot(member, cot[...]).astype(BF)
    blank = jnp.zeros((part.shape[2] - D - DA - 2 * width, tok_row), BF)
    rest = jnp.concatenate([tokens[...], tokens_cot[...], blank], axis=0).T
    for k in range(cols):
        at = slice(slab(k, cols) * own, (slab(k, cols) + 1) * own)
        part[k, :, D : D + DA] = cot_part[at]
        part[k, :, D + DA :] = rest[at]
    for low in range(0, D, 256):
        at = pl.ds(low, 256)
        pre = dot(mid[...], wagg[:, at])
        gate = sigmoid(pre)
        slope[:, at] = gate * (1.0 + pre * (1.0 - gate))
        sums = dot(member, (pre * gate).astype(BF)).astype(BF)
        for k in range(cols):
            part[k, :, at] = sums[slab(k, cols) * own : (slab(k, cols) + 1) * own]


def summed(parts):
    total = parts[0].astype(F32)
    for k in range(1, parts.shape[0]):
        total = total + parts[k].astype(F32)
    return total


def norm_kernel(parts, inverse, gain, wt2a, mid, normed, grad_new, spread):
    cols = parts.shape[0]
    width = D // cols
    total = summed(parts[:, :, : D + DA])
    for k in range(cols):
        at = slice(k * width, (k + 1) * width)
        low = D + DA
        mid[:, at] = parts[k, :, low : low + width].astype(F32)
        grad_new[:, at] = parts[k, :, low + width : low + 2 * width].astype(F32)
    grad = grad_new[...] + dot_t(total[:, D:].astype(BF), wt2a[...])
    grad_new[...] = grad
    value = mid[...] + total[:, :D] * inverse[...]
    mid[...] = value
    out = layer_norm(value, gain[...]).astype(BF)
    normed[...] = out
    for k in range(spread.shape[0]):
        spread[k] = out


def keyval_kernel(parts, out):
    out[...] = summed(parts[...])


def own_kernel(
    place, parts, mine, theirs, gate_ref, gated_ref, token_mid, wout, wgate, wt2a, tokens, lifted, feature, attended
):
    cols, own, _ = parts.shape
    span = GROUP * HD
    lane = lax.broadcasted_iota(jnp.int32, (GROUP, span), 1)
    row = lax.broadcasted_iota(jnp.int32, (GROUP, span), 0)
    widen = jnp.where((lane >= row * HD) & (lane < (row + 1) * HD), 1.0, 0.0).astype(BF)
    half = cols // CORES
    rows = mine.shape[3]
    slot = lax.broadcasted_iota(jnp.int32, (rows, own), 0)
    token = lax.broadcasted_iota(jnp.int32, (rows, own), 1)
    select = jnp.where(slot == token + place[0], 1.0, 0.0).astype(BF)
    tables = []
    for part in (mine, theirs):
        flat = part[...].reshape(half * (H // GROUP) * 3 * GROUP, rows)
        tables.append(dot(flat, select).T)
    for group in range(H // GROUP):
        logs = []
        for k in range(cols):
            low = (k // CORES * (H // GROUP) + group) * 3 * GROUP
            mine_first = jnp.where(place[1] == k % CORES, 1.0, 0.0)
            triple = (
                tables[0][:, low : low + 2 * GROUP] * mine_first
                + tables[1][:, low : low + 2 * GROUP] * (1.0 - mine_first)
            )
            logs.append(triple[:, :GROUP] + triple[:, GROUP:])
        top = logs[0]
        for k in range(1, cols):
            top = jnp.maximum(top, logs[k])
        shares = [jnp.exp(one - top) for one in logs]
        total = shares[0]
        for k in range(1, cols):
            total = total + shares[k]
        value = jnp.zeros((own, span), F32)
        for k in range(cols):
            share = shares[k] / total
            high = share.astype(BF)
            rest = (share - high.astype(F32)).astype(BF)
            weight = dot(high, widen) + dot(rest, widen)
            at = slice(group * span, (group + 1) * span)
            value = value + weight * parts[k, :, at].astype(F32)
        attended[:, group * span : (group + 1) * span] = value
    gate = gate_ref[...]
    value = attended[...]
    new = (token_mid[...] + dot((gate * value).astype(BF), wout[...])).astype(BF)
    tokens[...] = new
    lifted[...] = dot(new, wt2a[...]).astype(BF)
    grad_gate = (gated_ref[...] * value * gate * (1.0 - gate)).astype(BF)
    feature[...] = dot_t(grad_gate, wgate[...])


def token_kernel(parts, key_feature, feature, grad_new, token_mid, gain, wquery, tokens, lifted, out):
    cols = CORES * parts.shape[0]
    width = D // cols
    total = summed(parts[...]).astype(BF)
    normed_grad = dot_t(total, wquery[...]) + feature[...] + key_feature[...]
    grad = grad_new[...] + norm_back(token_mid[...], gain[...], normed_grad)
    grad = grad.astype(BF)
    new = tokens[...]
    low = D + DA
    pair = CORES * width
    for k in range(cols // CORES):
        out[k, :, :D] = grad
        out[k, :, D:low] = lifted[...]
        out[k, :, low:] = new[:, k * pair : (k + 1) * pair]


def atoms_backward_kernel(
    starts, place, mine, theirs, token, inverse, slope, cot, mid, query, window, prob, mixed,
    wagg, wo, wq, new, tokens_out, grad_tokens, inner, first, last, atoms_grad, feature, padded,
):
    atom_dev = cot.shape[0]
    blocks = window.shape[0]
    half = mine.shape[0]
    tok_row = CORES * half
    width = tokens_out.shape[1]
    core = place[0]
    padded_rows = padded.shape[0]
    scale = 1.0 / math.sqrt(AHD)
    slot = lax.broadcasted_iota(jnp.int32, (atom_dev, tok_row), 1)
    atom_inverse = jnp.sum(
        jnp.where(slot == token[...], inverse[...], 0.0), axis=1, keepdims=True
    )
    parts = ((mine, core * half), (theirs, (1 - core) * half))
    slot = lax.broadcasted_iota(jnp.int32, (atom_dev, half), 1)
    members = [
        jnp.where(slot + base == token[...], 1.0, 0.0).astype(BF) for _, base in parts
    ]

    def gathered(at):
        return dot(members[0], mine[:, at]) + dot(members[1], theirs[:, at])

    row = lax.broadcasted_iota(jnp.int32, (D, width), 0)
    lane = lax.broadcasted_iota(jnp.int32, (D, width), 1)
    column = jnp.where(row == lane + place[1] * width, 1.0, 0.0).astype(BF)
    for part, base in parts:
        here = pl.ds(pl.multiple_of(base, half), half)
        low = D + DA
        pair = part[:, low:].astype(F32)
        tokens_out[here, :] = jnp.where(core == 0, pair[:, :width], pair[:, width:]).astype(BF)
        grad_tokens[here, :] = dot(part[:, :D], column).astype(BF)
    grads = cot[...].astype(F32)
    for low in range(0, D, 256):
        at = pl.ds(low, 256)
        hidden = (gathered(at) * atom_inverse * slope[:, at]).astype(BF)
        grads = grads + dot_t(hidden, wagg[:, at])
    atoms_grad[...] = grads
    mixed_grad = dot_t(grads.astype(BF), wo[...]).astype(BF)
    padded[...] = jnp.zeros(padded.shape, F32)
    for block in range(blocks):
        at = slice(block * QBLK, (block + 1) * QBLK)
        rows = window[block]
        one = prob[block]
        grad_heads = stacked(mixed_grad[at])
        query_heads = stacked(query[at, :])
        grad_wide = grad_heads.astype(F32)
        tall = jnp.concatenate([mixed[at, :]] * AH, axis=0).astype(F32)
        delta = jnp.sum(grad_wide * tall, axis=-1, keepdims=True)
        sgrad = (one * (dot_t(grad_heads, rows[:, DA:]) - delta)).astype(BF)
        qgrad = (unstacked(dot(sgrad, rows[:, :DA])) * scale).astype(BF)
        feature[at, :] = dot_t(qgrad, wq[...])
        key_grad = rows_dot(sgrad, query_heads) * scale
        value_grad = rows_dot(one.astype(BF), grad_heads)
        both = jnp.concatenate([key_grad, value_grad], axis=1).astype(BF)
        padded[...] += rows_dot(picked(starts[block], padded_rows), both)
    first[...] = padded[:RIM, :].astype(BF)
    last[...] = padded[RIM + atom_dev :, :].astype(BF)
    inner[...] = padded[RIM : RIM + atom_dev, :]
    lift = gathered(slice(D, D + DA))
    new[...] = (mid[...].astype(F32) + lift).astype(BF)


def atoms_last_kernel(inner, before, after, feature, atoms_grad, atoms, gain, wkv, out):
    atom_dev = atoms.shape[0]
    keyval = jnp.concatenate(
        [
            inner[:RIM, :] + before[...].astype(F32),
            inner[RIM : atom_dev - RIM, :],
            inner[atom_dev - RIM :, :] + after[...].astype(F32),
        ],
        axis=0,
    ).astype(BF)
    feat = feature[...] + dot_t(keyval, wkv[...])
    back = norm_back(atoms[...].astype(F32), gain[...], feat)
    out[...] = (atoms_grad[...] + back).astype(BF)


def local(
    atoms,
    tokens,
    atom_bias,
    token_bias,
    atom_index,
    atom_counts,
    window_starts,
    gain_atom,
    w_atom_q,
    w_atom_kv,
    w_atom_o,
    w_agg,
    gain_token,
    w_query,
    w_keyval,
    w_gate,
    w_out,
    w_t2a,
    atoms_cot,
    tokens_cot,
):
    rows = lax.axis_size("row")
    cols = lax.axis_size("col")
    row_index = lax.axis_index("row")
    col_index = lax.axis_index("col")
    atom_dev = atoms.shape[0]
    blocks = window_starts.shape[0]
    tok_row = tokens.shape[0]
    tok_col = token_bias.shape[2]
    own = tok_row // cols
    width = tokens.shape[1]
    first_atom = (row_index * cols + col_index) * atom_dev

    before, after = neighbours(atoms, RIM)

    local_token = atom_index - row_index * tok_row
    inverse_count = 1.0 / atom_counts.astype(F32)
    core = col_index % CORES
    half = tok_row // CORES
    first_own = core * half + col_index // CORES * own
    inv_own = lax.dynamic_slice_in_dim(inverse_count, first_own, own, 0)

    starts = window_starts - first_atom + RIM
    gain_a = gain_atom[None, :]
    gain_t = gain_token[None, :]
    part, atoms_mid, slope, atom_query, window, atom_prob, atom_mixed = whole(
        atoms_forward_kernel,
        [
            pltpu.HBM((cols, own, D + 2 * DA), BF),
            pltpu.HBM((atom_dev, DA), BF),
            pltpu.HBM((atom_dev, D), F32),
            pltpu.HBM((atom_dev, DA), BF),
            pltpu.HBM((blocks, KWIN, 2 * DA), BF),
            pltpu.HBM((blocks, AH * QBLK, KWIN), F32),
            pltpu.HBM((atom_dev, DA), BF),
        ],
        (
            starts,
            before,
            far(atoms),
            after,
            far(atom_bias.reshape(blocks, AH * QBLK, KWIN)),
            local_token[None, :],
            gain_a,
            far(w_atom_q),
            far(w_atom_kv),
            far(w_atom_o),
            far(w_agg),
            far(atoms_cot),
            far(tokens.T),
            far(tokens_cot.T),
        ),
        "atoms_forward",
        scalars=1,
    )

    sums = exchange(part, "col")
    tokens_mid, normed_own, grad_new, spread = whole(
        norm_kernel,
        [
            pltpu.HBM((own, D), F32),
            shaped((own, D), BF),
            pltpu.HBM((own, D), F32),
            pltpu.HBM((rows, own, D), BF),
        ],
        (sums, inv_own[:, None], gain_t, far(w_t2a)),
        "token_norm",
    )
    keys_own = exchange(spread, "row")
    gate_own, gated_own, packed = token_project(
        normed_own, grad_new, w_query, w_gate, w_out, rows
    )
    packed = token_pack(packed, keys_own)
    mine, theirs = halves_of(packed)
    to_row = [
        (i * cols + r * CORES + p, r * cols + i * CORES + p)
        for r in range(rows)
        for i in range(rows)
        for p in range(CORES)
    ]
    k_t, v_t = token_keys(mine.reshape(half, 3 * D), w_keyval)
    q, q_t, g, g_t, mixed, stats = token_forward(
        core[None],
        k_t,
        v_t,
        mine.reshape(half, 3 * D),
        theirs.reshape(half, 3 * D),
        token_bias,
        cols,
    )
    stats = halves_of(stats)
    mixed_parts = exchange(mixed, "col")
    q_mine, q_theirs, kv_feat = token_backward(
        core[None], *stats, q, q_t, g, g_t, k_t, v_t, token_bias, w_keyval
    )
    swap = [(i, i ^ 1) for i in range(cols)]
    q_other = lax.ppermute(q_theirs, "col", swap)
    kv_parts = exchange(kv_feat.reshape(rows, own, D), "row")
    q_pair = (q_mine.astype(F32) + q_other.astype(F32)).astype(BF)
    q_parts = among_core(q_pair.reshape(cols // CORES, own, D))
    tokens_new, lifted, gate_feat = whole(
        own_kernel,
        [shaped((own, D), BF), shaped((own, DA), BF), shaped((own, D), F32)],
        (
            jnp.stack([first_own, core]),
            mixed_parts,
            *stats,
            far(gate_own),
            far(gated_own),
            far(tokens_mid),
            far(w_out),
            far(w_gate),
            far(w_t2a),
        ),
        "token_own",
        scalars=1,
        scratch=[pltpu.VMEM((own, D), F32)],
    )
    (kv_own,) = whole(
        keyval_kernel,
        [shaped((own, D), F32)],
        (kv_parts,),
        "token_keyval",
    )
    kv_back = lax.ppermute(kv_own, ("row", "col"), to_row)
    (mid_spread,) = whole(
        token_kernel,
        [pltpu.HBM((cols // CORES, own, D + DA + CORES * width), BF)],
        (
            q_parts,
            kv_back,
            gate_feat,
            far(grad_new),
            far(tokens_mid),
            gain_t,
            far(w_query),
            tokens_new,
            lifted,
        ),
        "token_grads",
    )
    mine, theirs = halves_of(mid_spread)

    atoms_new, tokens_out, grad_tokens, inner, first, last, atoms_grad, query_feat = whole(
        atoms_backward_kernel,
        [
            shaped((atom_dev, DA), BF),
            shaped((tok_row, width), BF),
            shaped((tok_row, width), BF),
            pltpu.HBM((atom_dev, 2 * DA), F32),
            shaped((RIM, 2 * DA), BF),
            shaped((RIM, 2 * DA), BF),
            pltpu.HBM((atom_dev, DA), F32),
            pltpu.HBM((atom_dev, DA), F32),
        ],
        (
            starts,
            jnp.stack([core, col_index]),
            mine.reshape(half, -1),
            theirs.reshape(half, -1),
            local_token[:, None],
            inverse_count[None, :],
            slope,
            far(atoms_cot),
            far(atoms_mid),
            far(atom_query),
            window,
            atom_prob,
            far(atom_mixed),
            far(w_agg),
            far(w_atom_o),
            far(w_atom_q),
        ),
        "atoms_backward",
        scalars=2,
        scratch=[pltpu.VMEM((atom_dev + 2 * RIM, 2 * DA), F32)],
    )
    axes = ("row", "col")
    up = [(i, i + 1) for i in range(rows * cols - 1)]
    down = [(j, i) for i, j in up]
    from_before = lax.ppermute(last, axes, up)
    from_after = lax.ppermute(first, axes, down)
    (grad_atoms,) = whole(
        atoms_last_kernel,
        [shaped((atom_dev, DA), BF)],
        (
            far(inner),
            from_before,
            from_after,
            far(query_feat),
            far(atoms_grad),
            far(atoms),
            gain_a,
            far(w_atom_kv),
        ),
        "atoms_last",
    )
    return (atoms_new, tokens_out, grad_atoms, grad_tokens)


def solution(mesh):
    placed = (
        P(("row", "col"), None),
        P("row", "col"),
        P(("row", "col"), None, None, None),
        P(None, "row", "col"),
        P(("row", "col")),
        P("row"),
        P(("row", "col")),
        P(),
        P(),
        P(),
        P(),
        P(),
        P(),
        P(),
        P(),
        P(),
        P(),
        P(),
        P(("row", "col"), None),
        P("row", "col"),
    )
    return jax.shard_map(
        local,
        mesh=mesh,
        in_specs=placed,
        out_specs=(
            P(("row", "col"), None),
            P("row", "col"),
            P(("row", "col"), None),
            P("row", "col"),
        ),
        check_vma=False,
    )
```

```python
import math

import jax
import jax.numpy as jnp
from jax import lax
from jax.experimental import pallas as pl
from jax.experimental.pallas import tpu as pltpu
from jax.sharding import PartitionSpec as P

D = 768
H = 16
HD = 48
DA = 128
AH = 4
AHD = 32
QBLK = 32
KWIN = 128
RIM = 64
EPS = 1e-05
BF = jnp.bfloat16
F32 = jnp.float32
GROUP = 8
CORES = 2
CHUNK = 128
VMEM_LIMIT = 24 * 1024 * 1024
SMALL_LIMIT = 14 * 1024 * 1024


def dot(a, b):
    return jnp.dot(a, b, preferred_element_type=F32)


def dot_t(a, b):
    return lax.dot_general(a, b, (((1,), (1,)), ((), ())), preferred_element_type=F32)


def centred(values):
    center = values - jnp.mean(values, axis=-1, keepdims=True)
    inv = lax.rsqrt(jnp.mean(center * center, axis=-1, keepdims=True) + EPS)
    return center * inv, inv


def layer_norm(values, gain_vec):
    return centred(values)[0] * gain_vec


def norm_back(values, gain_vec, cotangent):
    unit, inv = centred(values)
    g = cotangent * gain_vec
    return inv * (
        g
        - jnp.mean(g, axis=-1, keepdims=True)
        - unit * jnp.mean(g * unit, axis=-1, keepdims=True)
    )


def sigmoid(x):
    return 1.0 / (1.0 + jnp.exp(-x))


def exchange(x, axis):
    return lax.all_to_all(x, axis, 0, 0)


def among_core(x):
    cols = lax.axis_size("col")
    groups = [list(range(core, cols, CORES)) for core in range(CORES)]
    return lax.all_to_all(x, "col", 0, 0, axis_index_groups=groups)


def halves_of(x):
    cols = lax.axis_size("col")
    mine = among_core(x)
    theirs = lax.ppermute(mine, "col", [(i, i ^ 1) for i in range(cols)])
    return mine, theirs


def neighbours(x, width):
    axes = ("row", "col")
    devices = lax.axis_size("row") * lax.axis_size("col")
    up = [(i, i + 1) for i in range(devices - 1)]
    down = [(j, i) for i, j in up]
    before = lax.ppermute(x[x.shape[0] - width :], axes, up)
    after = lax.ppermute(x[:width], axes, down)
    return before, after


def slab(k, count):
    return k % CORES * (count // CORES) + k // CORES


def rows_dot(a, b):
    return lax.dot_general(a, b, (((0,), (0,)), ((), ())), preferred_element_type=F32)


def head_window(head):
    start = head * HD
    low = start // 128 * 128
    high = -(-(start + HD) // 128) * 128
    return start, low, high


def widened(x_t, head):
    start, low, high = head_window(head)
    parts = []
    if start > low:
        parts.append(jnp.zeros((start - low, x_t.shape[1]), x_t.dtype))
    parts.append(x_t[start : start + HD])
    if high > start + HD:
        parts.append(jnp.zeros((high - start - HD, x_t.shape[1]), x_t.dtype))
    return jnp.concatenate(parts, axis=0)


def project_kernel(parts, normed, wt2a, wq, wg, wout, gate, gated, grad_new, both):
    cols = parts.shape[0]
    width = D // cols
    for k in range(cols):
        at = slice(k * width, (k + 1) * width)
        grad_new[:, at] = parts[k, :, DA + width : DA + 2 * width].astype(F32)
    cot = summed(parts[:, :, :DA]).astype(BF)
    grad_new[...] = grad_new[...] + dot_t(cot, wt2a[...])
    query = dot(normed[...], wq[...]).astype(BF)
    opened = sigmoid(dot(normed[...], wg[...]))
    grad = dot_t(grad_new[...].astype(BF), wout[...])
    gate[...] = opened
    gated[...] = grad
    grad = (grad * opened).astype(BF)
    for k in range(both.shape[0]):
        both[k, :, :D] = query
        both[k, :, D:] = grad


def token_project(parts, normed, w_t2a, w_query, w_gate, w_out, copies):
    cols, own, _ = parts.shape
    last = D // (2 * DA)
    full = lambda *shape: pl.BlockSpec(shape, lambda i: (0,) * len(shape))
    return pl.pallas_call(
        project_kernel,
        grid=(1,),
        in_specs=[
            pl.BlockSpec((cols, own, 2 * DA), lambda i: (0, 0, last)),
            full(own, D),
            full(D, DA),
            full(D, D),
            full(D, D),
            full(D, D),
        ],
        out_specs=[full(own, D), full(own, D), full(own, D), full(copies, own, 2 * D)],
        out_shape=[
            pltpu.HBM((own, D), F32),
            pltpu.HBM((own, D), F32),
            pltpu.HBM((own, D), F32),
            pltpu.HBM((copies, own, 3 * D), BF),
        ],
        compiler_params=pltpu.CompilerParams(vmem_limit_bytes=SMALL_LIMIT),
        name="token_project",
    )(parts, far(normed), far(w_t2a), w_query, w_gate, w_out)


def pack_kernel(packed, keys, out):
    out[...] = keys[...]


def token_pack(packed, keys):
    return pl.pallas_call(
        pack_kernel,
        grid=(1,),
        in_specs=[
            pl.BlockSpec(memory_space=pl.ANY),
            pl.BlockSpec(keys.shape, lambda i: (0, 0, 0)),
        ],
        out_specs=pl.BlockSpec(keys.shape, lambda i: (0, 0, 2)),
        out_shape=pltpu.HBM(packed.shape, BF),
        input_output_aliases={0: 0},
        compiler_params=pltpu.CompilerParams(vmem_limit_bytes=SMALL_LIMIT),
        name="token_pack",
    )(packed, keys)


def key_kernel(key_normed, wk, wv, k_t, v_t):
    k_t[...] = dot(key_normed[...], wk[...]).astype(BF).T
    v_t[...] = dot(key_normed[...], wv[...]).astype(BF).T


def token_keys(mine, w_keyval):
    tok_col = mine.shape[0]
    span = GROUP * HD
    groups = H // GROUP
    return pl.pallas_call(
        key_kernel,
        grid=(groups,),
        in_specs=[
            pl.BlockSpec((tok_col, D), lambda i: (0, 2)),
            pl.BlockSpec((D, span), lambda i: (0, i)),
            pl.BlockSpec((D, span), lambda i: (0, groups + i)),
        ],
        out_specs=[pl.BlockSpec((span, tok_col), lambda i: (i, 0)) for _ in range(2)],
        out_shape=[pltpu.HBM((D, tok_col), BF) for _ in range(2)],
        compiler_params=pltpu.CompilerParams(vmem_limit_bytes=SMALL_LIMIT),
        name="token_keys",
    )(mine, far(w_keyval), far(w_keyval))


def forward_kernel(
    core, k_t, v_t, q_mine, q_theirs, g_mine, g_theirs, bias,
    q, q_t, g, g_t, mixed, stats, exps, out_t,
):
    half = q_mine.shape[0]
    mine = pl.ds(pl.multiple_of(core[0] * half, half), half)
    theirs = pl.ds(pl.multiple_of((1 - core[0]) * half, half), half)
    q[mine, :] = q_mine[...]
    q[theirs, :] = q_theirs[...]
    g[mine, :] = g_mine[...]
    g[theirs, :] = g_theirs[...]
    q_t[...] = q[...].T
    g_t[...] = g[...].T
    copies = stats.shape[0]
    rows = q.shape[0]
    scale = 1.0 / math.sqrt(HD)
    keys = k_t[...]
    values = v_t[...]
    lane = lax.broadcasted_iota(jnp.int32, (CHUNK, 128), 1)
    tops = [jnp.zeros((CHUNK, 128), F32) for _ in range(rows // CHUNK)]
    totals = []
    deltas = []
    for head in range(GROUP):
        start, low, high = head_window(head)
        wide = widened(keys, head)
        for part in range(rows // CHUNK):
            at = pl.ds(part * CHUNK, CHUNK)
            score = dot(q[at, low:high], wide) * scale + bias[head, at, :].astype(F32)
            top = jnp.max(score, axis=1, keepdims=True)
            exps[at, :] = jnp.exp(score - top).astype(BF)
            tops[part] = jnp.where(lane == head, top, tops[part])
        ones = jnp.ones((16, values.shape[1]), BF)
        weighted = dot_t(jnp.concatenate([values[start : start + HD], ones], axis=0), exps[...])
        total = weighted[HD : HD + 1]
        one = weighted[:HD] / total
        out_t[start : start + HD, :] = one
        totals.append(total)
        deltas.append(
            jnp.sum(g_t[start : start + HD, :].astype(F32) * one, axis=0, keepdims=True)
        )
    tops_t = jnp.concatenate(tops, axis=0).T[:GROUP]
    lse = tops_t + jnp.log(jnp.concatenate(totals, axis=0))
    delta = jnp.concatenate(deltas, axis=0)
    high = lse.astype(BF).astype(F32)
    middle = (lse - high).astype(BF).astype(F32)
    triple = jnp.concatenate([high, middle, delta], axis=0).astype(BF)
    for copy in range(copies):
        stats[copy, 0] = triple
    straight = out_t[...].astype(BF).T
    cols, own, _ = mixed.shape
    for k in range(cols):
        at = slice(slab(k, cols) * own, (slab(k, cols) + 1) * own)
        mixed[k] = straight[at]


def token_forward(core, k_t, v_t, mine, theirs, bias, cols):
    copies = cols // CORES
    half = mine.shape[0]
    tok_col = half
    rows = CORES * half
    span = GROUP * HD
    groups = H // GROUP
    return pl.pallas_call(
        forward_kernel,
        grid=(groups,),
        in_specs=[
            pl.BlockSpec(memory_space=pltpu.SMEM),
            pl.BlockSpec((span, tok_col), lambda i: (i, 0)),
            pl.BlockSpec((span, tok_col), lambda i: (i, 0)),
            pl.BlockSpec((half, span), lambda i: (0, i)),
            pl.BlockSpec((half, span), lambda i: (0, i)),
            pl.BlockSpec((half, span), lambda i: (0, groups + i)),
            pl.BlockSpec((half, span), lambda i: (0, groups + i)),
            pl.BlockSpec((GROUP, rows, tok_col), lambda i: (i, 0, 0)),
        ],
        out_specs=[
            pl.BlockSpec((rows, span), lambda i: (0, i)),
            pl.BlockSpec((span, rows), lambda i: (i, 0)),
            pl.BlockSpec((rows, span), lambda i: (0, i)),
            pl.BlockSpec((span, rows), lambda i: (i, 0)),
            pl.BlockSpec((cols, rows // cols, span), lambda i: (0, 0, i)),
            pl.BlockSpec((copies, 1, 3 * GROUP, rows), lambda i: (0, i, 0, 0)),
        ],
        out_shape=[
            pltpu.HBM((rows, D), BF),
            pltpu.HBM((D, rows), BF),
            pltpu.HBM((rows, D), BF),
            pltpu.HBM((D, rows), BF),
            pltpu.HBM((cols, rows // cols, D), BF),
            pltpu.HBM((copies, groups, 3 * GROUP, rows), BF),
        ],
        scratch_shapes=[pltpu.VMEM((rows, tok_col), BF), pltpu.VMEM((span, rows), F32)],
        compiler_params=pltpu.CompilerParams(vmem_limit_bytes=VMEM_LIMIT),
        name="token_forward",
    )(core, far(k_t), far(v_t), mine, theirs, mine, theirs, far(bias))


def backward_kernel(
    core, mine, theirs, q, q_t, g, g_t, k_t, v_t, bias, wk, wv, q_mine, q_theirs, kv_feat,
    probs, slopes, q_acc, k_acc, v_acc, straight, feat,
):
    rows = q.shape[0]
    tok_col = k_t.shape[1]
    scale = 1.0 / math.sqrt(HD)
    logs = []
    deltas = []
    for part in (mine, theirs):
        for k in range(part.shape[0]):
            triple = part[k, 0].astype(F32)
            logs.append(triple[:GROUP] + triple[GROUP : 2 * GROUP])
            deltas.append(triple[2 * GROUP :])
    top = logs[0]
    for one in logs[1:]:
        top = jnp.maximum(top, one)
    share_sum = jnp.zeros_like(top)
    delta = jnp.zeros_like(top)
    for one, other in zip(logs, deltas):
        share = jnp.exp(one - top)
        share_sum = share_sum + share
        delta = delta + share * other
    lse = top + jnp.log(share_sum)
    delta = delta / share_sum
    filler = jnp.zeros((128 - 2 * GROUP, rows), F32)
    columns = jnp.concatenate([lse, delta, filler], axis=0).T
    for head in range(GROUP):
        start, low, high = head_window(head)
        wide_k = widened(k_t[...], head)
        wide_v = widened(v_t[...], head)
        for part in range(rows // CHUNK):
            at = pl.ds(part * CHUNK, CHUNK)
            some = columns[part * CHUNK : (part + 1) * CHUNK]
            score = dot(q[at, low:high], wide_k) * scale + bias[head, at, :].astype(F32)
            prob = jnp.exp(score - some[:, head : head + 1])
            grad = dot(g[at, low:high], wide_v) - some[:, GROUP + head : GROUP + head + 1]
            probs[at, :] = prob.astype(BF)
            slopes[at, :] = (prob * grad).astype(BF)
        here = pl.ds(start, HD)
        k_acc[here, :] = dot(q_t[here, :], slopes[...]) * scale
        v_acc[here, :] = dot(g_t[here, :], probs[...])
        q_acc[here, :] = dot_t(k_t[here, :], slopes[...]) * scale
    new = dot(wk[...], k_acc[...].astype(BF)) + dot(wv[...], v_acc[...].astype(BF))

    @pl.when(pl.program_id(0) == 0)
    def _():
        feat[...] = new

    @pl.when(pl.program_id(0) > 0)
    def _():
        kv_feat[...] = (feat[...] + new).astype(BF).T

    straight[...] = q_acc[...].astype(BF).T
    half = q_mine.shape[0]
    q_mine[...] = straight[pl.ds(pl.multiple_of(core[0] * half, half), half), :]
    q_theirs[...] = straight[pl.ds(pl.multiple_of((1 - core[0]) * half, half), half), :]


def token_backward(core, mine, theirs, q, q_t, g, g_t, k_t, v_t, bias, w_keyval):
    rows = q.shape[0]
    tok_col = k_t.shape[1]
    parts = mine.shape[0]
    half = rows // CORES
    groups = H // GROUP
    span = GROUP * HD
    straight = lambda: pl.BlockSpec((rows, span), lambda i: (0, i))
    turned = lambda: pl.BlockSpec((span, rows), lambda i: (i, 0))
    keyed = lambda: pl.BlockSpec((span, tok_col), lambda i: (i, 0))
    return pl.pallas_call(
        backward_kernel,
        grid=(groups,),
        in_specs=[
            pl.BlockSpec(memory_space=pltpu.SMEM),
            pl.BlockSpec((parts, 1, 3 * GROUP, rows), lambda i: (0, i, 0, 0)),
            pl.BlockSpec((parts, 1, 3 * GROUP, rows), lambda i: (0, i, 0, 0)),
            straight(),
            turned(),
            straight(),
            turned(),
            keyed(),
            keyed(),
            pl.BlockSpec((GROUP, rows, tok_col), lambda i: (i, 0, 0)),
            pl.BlockSpec((D, span), lambda i: (0, i)),
            pl.BlockSpec((D, span), lambda i: (0, groups + i)),
        ],
        out_specs=[
            pl.BlockSpec((half, span), lambda i: (0, i)),
            pl.BlockSpec((half, span), lambda i: (0, i)),
            pl.BlockSpec((tok_col, D), lambda i: (0, 0)),
        ],
        out_shape=[
            pltpu.HBM((half, D), BF),
            pltpu.HBM((half, D), BF),
            pltpu.HBM((tok_col, D), BF),
        ],
        scratch_shapes=[
            pltpu.VMEM((rows, tok_col), BF),
            pltpu.VMEM((rows, tok_col), BF),
            pltpu.VMEM((span, rows), F32),
            pltpu.VMEM((span, tok_col), F32),
            pltpu.VMEM((span, tok_col), F32),
            pltpu.VMEM((rows, span), BF),
            pltpu.VMEM((D, tok_col), F32),
        ],
        compiler_params=pltpu.CompilerParams(vmem_limit_bytes=VMEM_LIMIT),
        name="token_backward",
    )(
        core,
        mine,
        theirs,
        far(q),
        far(q_t),
        far(g),
        far(g_t),
        far(k_t),
        far(v_t),
        far(bias),
        far(w_keyval),
        far(w_keyval),
    )


def far(x):
    return pltpu.with_memory_space_constraint(x, pltpu.HBM)


def shaped(shape, dtype):
    return jax.ShapeDtypeStruct(shape, dtype)


def whole(kernel, outs, args, name, scalars=0, scratch=()):
    specs = [pl.BlockSpec(memory_space=pltpu.SMEM)] * scalars
    specs += [pl.BlockSpec(memory_space=pltpu.VMEM)] * (len(args) - scalars)
    return pl.pallas_call(
        kernel,
        in_specs=specs,
        out_specs=[pl.BlockSpec(memory_space=pltpu.VMEM)] * len(outs),
        out_shape=list(outs),
        scratch_shapes=list(scratch),
        compiler_params=pltpu.CompilerParams(vmem_limit_bytes=SMALL_LIMIT),
        name=name,
    )(*args)


def head_lanes(head):
    lane = lax.broadcasted_iota(jnp.int32, (1, DA), 1)
    return (lane >= head * AHD) & (lane < (head + 1) * AHD)


def stacked(x):
    return jnp.concatenate(
        [jnp.where(head_lanes(head), x, jnp.zeros_like(x)) for head in range(AH)], axis=0
    )


def unstacked(x):
    total = jnp.zeros((QBLK, DA), F32)
    for head in range(AH):
        total = jnp.where(head_lanes(head), x[head * QBLK : (head + 1) * QBLK], total)
    return total


def picked(start, padded_rows):
    row = lax.broadcasted_iota(jnp.int32, (KWIN, padded_rows), 0)
    lane = lax.broadcasted_iota(jnp.int32, (KWIN, padded_rows), 1)
    return jnp.where(row + start == lane, 1.0, 0.0).astype(BF)


def atoms_forward_kernel(
    starts, before, atoms, after, bias, token, gain, wq, wkv, wo, wagg, cot, tokens, tokens_cot,
    part, mid, slope, query, window, prob, mixed,
):
    atom_dev = atoms.shape[0]
    blocks = window.shape[0]
    cols, own, _ = part.shape
    tok_row = cols * own
    scale = 1.0 / math.sqrt(AHD)
    padded = jnp.concatenate([before[...], atoms[...], after[...]], axis=0).astype(F32)
    padded_rows = padded.shape[0]
    normed = layer_norm(padded, gain[...]).astype(BF)
    query[...] = dot(normed[RIM : RIM + atom_dev], wq[...]).astype(BF)
    keyval = dot(normed, wkv[...]).astype(BF)
    for block in range(blocks):
        at = pl.ds(block * QBLK, QBLK)
        rows = dot(picked(starts[block], padded_rows), keyval).astype(BF)
        window[block] = rows
        score = dot_t(stacked(query[at, :]), rows[:, :DA]) * scale + bias[block].astype(F32)
        exps = jnp.exp(score - jnp.max(score, axis=-1, keepdims=True))
        one = exps / jnp.sum(exps, axis=-1, keepdims=True)
        prob[block] = one
        mixed[at, :] = unstacked(dot(one.astype(BF), rows[:, DA:])).astype(BF)
    mid[...] = (atoms[...].astype(F32) + dot(mixed[...], wo[...])).astype(BF)
    slot = lax.broadcasted_iota(jnp.int32, (tok_row, atom_dev), 0)
    member = jnp.where(slot == token[...], 1.0, 0.0).astype(BF)
    width = tokens.shape[0]
    cot_part = dot(member, cot[...]).astype(BF)
    blank = jnp.zeros((part.shape[2] - D - DA - 2 * width, tok_row), BF)
    rest = jnp.concatenate([tokens[...], tokens_cot[...], blank], axis=0).T
    for k in range(cols):
        at = slice(slab(k, cols) * own, (slab(k, cols) + 1) * own)
        part[k, :, D : D + DA] = cot_part[at]
        part[k, :, D + DA :] = rest[at]
    for low in range(0, D, 256):
        at = pl.ds(low, 256)
        pre = dot(mid[...], wagg[:, at])
        gate = sigmoid(pre)
        slope[:, at] = gate * (1.0 + pre * (1.0 - gate))
        sums = dot(member, (pre * gate).astype(BF)).astype(BF)
        for k in range(cols):
            part[k, :, at] = sums[slab(k, cols) * own : (slab(k, cols) + 1) * own]


def summed(parts):
    total = parts[0].astype(F32)
    for k in range(1, parts.shape[0]):
        total = total + parts[k].astype(F32)
    return total


def norm_kernel(parts, inverse, gain, mid, normed, spread):
    cols = parts.shape[0]
    width = D // cols
    low = D + DA
    for k in range(cols):
        mid[:, k * width : (k + 1) * width] = parts[k, :, low : low + width].astype(F32)
    value = mid[...] + summed(parts[:, :, :D]) * inverse[...]
    mid[...] = value
    out = layer_norm(value, gain[...]).astype(BF)
    normed[...] = out
    for k in range(spread.shape[0]):
        spread[k] = out


def keyval_kernel(parts, out):
    out[...] = summed(parts[...]).astype(BF)


def own_kernel(
    place, parts, mine, theirs, gate_ref, gated_ref, token_mid, wout, wgate, wt2a, tokens, lifted, feature, attended
):
    cols, own, _ = parts.shape
    span = GROUP * HD
    lane = lax.broadcasted_iota(jnp.int32, (GROUP, span), 1)
    row = lax.broadcasted_iota(jnp.int32, (GROUP, span), 0)
    widen = jnp.where((lane >= row * HD) & (lane < (row + 1) * HD), 1.0, 0.0).astype(BF)
    half = cols // CORES
    rows = mine.shape[3]
    slot = lax.broadcasted_iota(jnp.int32, (rows, own), 0)
    token = lax.broadcasted_iota(jnp.int32, (rows, own), 1)
    select = jnp.where(slot == token + place[0], 1.0, 0.0).astype(BF)
    tables = []
    for part in (mine, theirs):
        flat = part[...].reshape(half * (H // GROUP) * 3 * GROUP, rows)
        tables.append(dot(flat, select).T)
    for group in range(H // GROUP):
        logs = []
        for k in range(cols):
            low = (k // CORES * (H // GROUP) + group) * 3 * GROUP
            mine_first = jnp.where(place[1] == k % CORES, 1.0, 0.0)
            triple = (
                tables[0][:, low : low + 2 * GROUP] * mine_first
                + tables[1][:, low : low + 2 * GROUP] * (1.0 - mine_first)
            )
            logs.append(triple[:, :GROUP] + triple[:, GROUP:])
        top = logs[0]
        for k in range(1, cols):
            top = jnp.maximum(top, logs[k])
        shares = [jnp.exp(one - top) for one in logs]
        total = shares[0]
        for k in range(1, cols):
            total = total + shares[k]
        share = jnp.concatenate([one / total for one in shares], axis=0)
        high = share.astype(BF)
        rest = (share - high.astype(F32)).astype(BF)
        weight = dot(high, widen) + dot(rest, widen)
        value = jnp.zeros((own, span), F32)
        for k in range(cols):
            at = slice(group * span, (group + 1) * span)
            value = value + weight[k * own : (k + 1) * own] * parts[k, :, at].astype(F32)
        attended[:, group * span : (group + 1) * span] = value
    gate = gate_ref[...]
    value = attended[...]
    new = (token_mid[...] + dot((gate * value).astype(BF), wout[...])).astype(BF)
    tokens[...] = new
    lifted[...] = dot(new, wt2a[...]).astype(BF)
    grad_gate = (gated_ref[...] * value * gate * (1.0 - gate)).astype(BF)
    feature[...] = dot_t(grad_gate, wgate[...])


def token_kernel(parts, key_feature, feature, grad_new, token_mid, gain, wquery, tokens, lifted, out):
    cols = CORES * parts.shape[0]
    width = D // cols
    total = summed(parts[...]).astype(BF)
    normed_grad = dot_t(total, wquery[...]) + feature[...] + key_feature[...].astype(F32)
    grad = grad_new[...] + norm_back(token_mid[...], gain[...], normed_grad)
    grad = grad.astype(BF)
    new = tokens[...]
    low = D + DA
    pair = CORES * width
    for k in range(cols // CORES):
        out[k, :, :D] = grad
        out[k, :, D:low] = lifted[...]
        out[k, :, low:] = new[:, k * pair : (k + 1) * pair]


def atoms_backward_kernel(
    starts, place, mine, theirs, token, inverse, slope, cot, mid, query, window, prob, mixed,
    wagg, wo, wq, new, tokens_out, grad_tokens, inner, first, last, atoms_grad, feature, padded,
):
    atom_dev = cot.shape[0]
    blocks = window.shape[0]
    half = mine.shape[0]
    tok_row = CORES * half
    width = tokens_out.shape[1]
    core = place[0]
    padded_rows = padded.shape[0]
    scale = 1.0 / math.sqrt(AHD)
    slot = lax.broadcasted_iota(jnp.int32, (atom_dev, tok_row), 1)
    atom_inverse = jnp.sum(
        jnp.where(slot == token[...], inverse[...], 0.0), axis=1, keepdims=True
    )
    parts = ((mine, core * half), (theirs, (1 - core) * half))
    slot = lax.broadcasted_iota(jnp.int32, (atom_dev, half), 1)
    members = [
        jnp.where(slot + base == token[...], 1.0, 0.0).astype(BF) for _, base in parts
    ]

    def gathered(at):
        return dot(members[0], mine[:, at]) + dot(members[1], theirs[:, at])

    row = lax.broadcasted_iota(jnp.int32, (D, width), 0)
    lane = lax.broadcasted_iota(jnp.int32, (D, width), 1)
    column = jnp.where(row == lane + place[1] * width, 1.0, 0.0).astype(BF)
    for part, base in parts:
        here = pl.ds(pl.multiple_of(base, half), half)
        low = D + DA
        pair = part[:, low:].astype(F32)
        tokens_out[here, :] = jnp.where(core == 0, pair[:, :width], pair[:, width:]).astype(BF)
        grad_tokens[here, :] = dot(part[:, :D], column).astype(BF)
    grads = cot[...].astype(F32)
    for low in range(0, D, 256):
        at = pl.ds(low, 256)
        hidden = (gathered(at) * atom_inverse * slope[:, at]).astype(BF)
        grads = grads + dot_t(hidden, wagg[:, at])
    atoms_grad[...] = grads
    mixed_grad = dot_t(grads.astype(BF), wo[...]).astype(BF)
    padded[...] = jnp.zeros(padded.shape, F32)
    for block in range(blocks):
        at = slice(block * QBLK, (block + 1) * QBLK)
        rows = window[block]
        one = prob[block]
        grad_heads = stacked(mixed_grad[at])
        query_heads = stacked(query[at, :])
        grad_wide = grad_heads.astype(F32)
        tall = jnp.concatenate([mixed[at, :]] * AH, axis=0).astype(F32)
        delta = jnp.sum(grad_wide * tall, axis=-1, keepdims=True)
        sgrad = (one * (dot_t(grad_heads, rows[:, DA:]) - delta)).astype(BF)
        qgrad = (unstacked(dot(sgrad, rows[:, :DA])) * scale).astype(BF)
        feature[at, :] = dot_t(qgrad, wq[...])
        key_grad = rows_dot(sgrad, query_heads) * scale
        value_grad = rows_dot(one.astype(BF), grad_heads)
        both = jnp.concatenate([key_grad, value_grad], axis=1).astype(BF)
        padded[...] += rows_dot(picked(starts[block], padded_rows), both)
    first[...] = padded[:RIM, :].astype(BF)
    last[...] = padded[RIM + atom_dev :, :].astype(BF)
    inner[...] = padded[RIM : RIM + atom_dev, :]
    lift = gathered(slice(D, D + DA))
    new[...] = (mid[...].astype(F32) + lift).astype(BF)


def atoms_last_kernel(inner, before, after, feature, atoms_grad, atoms, gain, wkv, out):
    atom_dev = atoms.shape[0]
    keyval = jnp.concatenate(
        [
            inner[:RIM, :] + before[...].astype(F32),
            inner[RIM : atom_dev - RIM, :],
            inner[atom_dev - RIM :, :] + after[...].astype(F32),
        ],
        axis=0,
    ).astype(BF)
    feat = feature[...] + dot_t(keyval, wkv[...])
    back = norm_back(atoms[...].astype(F32), gain[...], feat)
    out[...] = (atoms_grad[...] + back).astype(BF)


def local(
    atoms,
    tokens,
    atom_bias,
    token_bias,
    atom_index,
    atom_counts,
    window_starts,
    gain_atom,
    w_atom_q,
    w_atom_kv,
    w_atom_o,
    w_agg,
    gain_token,
    w_query,
    w_keyval,
    w_gate,
    w_out,
    w_t2a,
    atoms_cot,
    tokens_cot,
):
    rows = lax.axis_size("row")
    cols = lax.axis_size("col")
    row_index = lax.axis_index("row")
    col_index = lax.axis_index("col")
    atom_dev = atoms.shape[0]
    blocks = window_starts.shape[0]
    tok_row = tokens.shape[0]
    tok_col = token_bias.shape[2]
    own = tok_row // cols
    width = tokens.shape[1]
    first_atom = (row_index * cols + col_index) * atom_dev

    before, after = neighbours(atoms, RIM)

    local_token = atom_index - row_index * tok_row
    inverse_count = 1.0 / atom_counts.astype(F32)
    core = col_index % CORES
    half = tok_row // CORES
    first_own = core * half + col_index // CORES * own
    inv_own = lax.dynamic_slice_in_dim(inverse_count, first_own, own, 0)

    starts = window_starts - first_atom + RIM
    gain_a = gain_atom[None, :]
    gain_t = gain_token[None, :]
    part, atoms_mid, slope, atom_query, window, atom_prob, atom_mixed = whole(
        atoms_forward_kernel,
        [
            pltpu.HBM((cols, own, D + 2 * DA), BF),
            pltpu.HBM((atom_dev, DA), BF),
            pltpu.HBM((atom_dev, D), F32),
            pltpu.HBM((atom_dev, DA), BF),
            pltpu.HBM((blocks, KWIN, 2 * DA), BF),
            pltpu.HBM((blocks, AH * QBLK, KWIN), F32),
            pltpu.HBM((atom_dev, DA), BF),
        ],
        (
            starts,
            before,
            far(atoms),
            after,
            far(atom_bias.reshape(blocks, AH * QBLK, KWIN)),
            local_token[None, :],
            gain_a,
            far(w_atom_q),
            far(w_atom_kv),
            far(w_atom_o),
            far(w_agg),
            far(atoms_cot),
            far(tokens.T),
            far(tokens_cot.T),
        ),
        "atoms_forward",
        scalars=1,
    )

    sums = exchange(part, "col")
    tokens_mid, normed_own, spread = whole(
        norm_kernel,
        [
            pltpu.HBM((own, D), F32),
            pltpu.HBM((own, D), BF),
            pltpu.HBM((rows, own, D), BF),
        ],
        (sums, inv_own[:, None], gain_t),
        "token_norm",
    )
    keys_own = exchange(spread, "row")
    gate_own, gated_own, grad_new, packed = token_project(
        sums, normed_own, w_t2a, w_query, w_gate, w_out, rows
    )
    packed = token_pack(packed, keys_own)
    mine, theirs = halves_of(packed)
    to_row = [
        (i * cols + r * CORES + p, r * cols + i * CORES + p)
        for r in range(rows)
        for i in range(rows)
        for p in range(CORES)
    ]
    k_t, v_t = token_keys(mine.reshape(half, 3 * D), w_keyval)
    q, q_t, g, g_t, mixed, stats = token_forward(
        core[None],
        k_t,
        v_t,
        mine.reshape(half, 3 * D),
        theirs.reshape(half, 3 * D),
        token_bias,
        cols,
    )
    stats = halves_of(stats)
    mixed_parts = exchange(mixed, "col")
    q_mine, q_theirs, kv_feat = token_backward(
        core[None], *stats, q, q_t, g, g_t, k_t, v_t, token_bias, w_keyval
    )
    swap = [(i, i ^ 1) for i in range(cols)]
    q_other = lax.ppermute(q_theirs, "col", swap)
    kv_parts = exchange(kv_feat.reshape(rows, own, D), "row")
    q_pair = (q_mine.astype(F32) + q_other.astype(F32)).astype(BF)
    q_parts = among_core(q_pair.reshape(cols // CORES, own, D))
    tokens_new, lifted, gate_feat = whole(
        own_kernel,
        [shaped((own, D), BF), shaped((own, DA), BF), shaped((own, D), F32)],
        (
            jnp.stack([first_own, core]),
            mixed_parts,
            *stats,
            far(gate_own),
            far(gated_own),
            far(tokens_mid),
            far(w_out),
            far(w_gate),
            far(w_t2a),
        ),
        "token_own",
        scalars=1,
        scratch=[pltpu.VMEM((own, D), F32)],
    )
    (kv_own,) = whole(
        keyval_kernel,
        [shaped((own, D), BF)],
        (kv_parts,),
        "token_keyval",
    )
    kv_back = lax.ppermute(kv_own, ("row", "col"), to_row)
    (mid_spread,) = whole(
        token_kernel,
        [pltpu.HBM((cols // CORES, own, D + DA + CORES * width), BF)],
        (
            q_parts,
            kv_back,
            gate_feat,
            far(grad_new),
            far(tokens_mid),
            gain_t,
            far(w_query),
            tokens_new,
            lifted,
        ),
        "token_grads",
    )
    mine, theirs = halves_of(mid_spread)

    atoms_new, tokens_out, grad_tokens, inner, first, last, atoms_grad, query_feat = whole(
        atoms_backward_kernel,
        [
            shaped((atom_dev, DA), BF),
            shaped((tok_row, width), BF),
            shaped((tok_row, width), BF),
            pltpu.HBM((atom_dev, 2 * DA), F32),
            shaped((RIM, 2 * DA), BF),
            shaped((RIM, 2 * DA), BF),
            pltpu.HBM((atom_dev, DA), F32),
            pltpu.HBM((atom_dev, DA), F32),
        ],
        (
            starts,
            jnp.stack([core, col_index]),
            mine.reshape(half, -1),
            theirs.reshape(half, -1),
            local_token[:, None],
            inverse_count[None, :],
            slope,
            far(atoms_cot),
            far(atoms_mid),
            far(atom_query),
            window,
            atom_prob,
            far(atom_mixed),
            far(w_agg),
            far(w_atom_o),
            far(w_atom_q),
        ),
        "atoms_backward",
        scalars=2,
        scratch=[pltpu.VMEM((atom_dev + 2 * RIM, 2 * DA), F32)],
    )
    axes = ("row", "col")
    up = [(i, i + 1) for i in range(rows * cols - 1)]
    down = [(j, i) for i, j in up]
    from_before = lax.ppermute(last, axes, up)
    from_after = lax.ppermute(first, axes, down)
    (grad_atoms,) = whole(
        atoms_last_kernel,
        [shaped((atom_dev, DA), BF)],
        (
            far(inner),
            from_before,
            from_after,
            far(query_feat),
            far(atoms_grad),
            far(atoms),
            gain_a,
            far(w_atom_kv),
        ),
        "atoms_last",
    )
    return (atoms_new, tokens_out, grad_atoms, grad_tokens)


def solution(mesh):
    placed = (
        P(("row", "col"), None),
        P("row", "col"),
        P(("row", "col"), None, None, None),
        P(None, "row", "col"),
        P(("row", "col")),
        P("row"),
        P(("row", "col")),
        P(),
        P(),
        P(),
        P(),
        P(),
        P(),
        P(),
        P(),
        P(),
        P(),
        P(),
        P(("row", "col"), None),
        P("row", "col"),
    )
    return jax.shard_map(
        local,
        mesh=mesh,
        in_specs=placed,
        out_specs=(
            P(("row", "col"), None),
            P("row", "col"),
            P(("row", "col"), None),
            P("row", "col"),
        ),
        check_vma=False,
    )
```

```python
import math

import jax
import jax.numpy as jnp
from jax import lax
from jax.experimental import pallas as pl
from jax.experimental.pallas import tpu as pltpu
from jax.sharding import PartitionSpec as P

D = 768
H = 16
HD = 48
DA = 128
AH = 4
AHD = 32
QBLK = 32
KWIN = 128
RIM = 64
EPS = 1e-05
BF = jnp.bfloat16
F32 = jnp.float32
GROUP = 8
CORES = 2
CHUNK = 128
VMEM_LIMIT = 24 * 1024 * 1024
SMALL_LIMIT = 14 * 1024 * 1024


def dot(a, b):
    return jnp.dot(a, b, preferred_element_type=F32)


def dot_t(a, b):
    return lax.dot_general(a, b, (((1,), (1,)), ((), ())), preferred_element_type=F32)


def centred(values):
    center = values - jnp.mean(values, axis=-1, keepdims=True)
    inv = lax.rsqrt(jnp.mean(center * center, axis=-1, keepdims=True) + EPS)
    return center * inv, inv


def layer_norm(values, gain_vec):
    return centred(values)[0] * gain_vec


def norm_back(values, gain_vec, cotangent):
    unit, inv = centred(values)
    g = cotangent * gain_vec
    return inv * (
        g
        - jnp.mean(g, axis=-1, keepdims=True)
        - unit * jnp.mean(g * unit, axis=-1, keepdims=True)
    )


def sigmoid(x):
    return 1.0 / (1.0 + jnp.exp(-x))


def exchange(x, axis):
    return lax.all_to_all(x, axis, 0, 0)


def among_core(x):
    cols = lax.axis_size("col")
    groups = [list(range(core, cols, CORES)) for core in range(CORES)]
    return lax.all_to_all(x, "col", 0, 0, axis_index_groups=groups)


def halves_of(x):
    cols = lax.axis_size("col")
    mine = among_core(x)
    theirs = lax.ppermute(mine, "col", [(i, i ^ 1) for i in range(cols)])
    return mine, theirs


def neighbours(x, width):
    axes = ("row", "col")
    devices = lax.axis_size("row") * lax.axis_size("col")
    up = [(i, i + 1) for i in range(devices - 1)]
    down = [(j, i) for i, j in up]
    before = lax.ppermute(x[x.shape[0] - width :], axes, up)
    after = lax.ppermute(x[:width], axes, down)
    return before, after


def slab(k, count):
    return k % CORES * (count // CORES) + k // CORES


def rows_dot(a, b):
    return lax.dot_general(a, b, (((0,), (0,)), ((), ())), preferred_element_type=F32)


def head_window(head):
    start = head * HD
    low = start // 128 * 128
    high = -(-(start + HD) // 128) * 128
    return start, low, high


def widened(x_t, head):
    start, low, high = head_window(head)
    parts = []
    if start > low:
        parts.append(jnp.zeros((start - low, x_t.shape[1]), x_t.dtype))
    parts.append(x_t[start : start + HD])
    if high > start + HD:
        parts.append(jnp.zeros((high - start - HD, x_t.shape[1]), x_t.dtype))
    return jnp.concatenate(parts, axis=0)


def project_kernel(parts, normed, wt2a, wq, wg, wout, gate, gated, grad_new, both):
    cols = parts.shape[0]
    width = D // cols
    for k in range(cols):
        at = slice(k * width, (k + 1) * width)
        grad_new[:, at] = parts[k, :, DA + width : DA + 2 * width].astype(F32)
    cot = summed(parts[:, :, :DA]).astype(BF)
    grad_new[...] = grad_new[...] + dot_t(cot, wt2a[...])
    query = dot(normed[...], wq[...]).astype(BF)
    opened = sigmoid(dot(normed[...], wg[...]))
    grad = dot_t(grad_new[...].astype(BF), wout[...])
    gate[...] = opened
    gated[...] = grad
    grad = (grad * opened).astype(BF)
    for k in range(both.shape[0]):
        both[k, :, :D] = query
        both[k, :, D:] = grad


def token_project(parts, normed, w_t2a, w_query, w_gate, w_out, copies):
    cols, own, _ = parts.shape
    last = D // (2 * DA)
    full = lambda *shape: pl.BlockSpec(shape, lambda i: (0,) * len(shape))
    return pl.pallas_call(
        project_kernel,
        grid=(1,),
        in_specs=[
            pl.BlockSpec((cols, own, 2 * DA), lambda i: (0, 0, last)),
            full(own, D),
            full(D, DA),
            full(D, D),
            full(D, D),
            full(D, D),
        ],
        out_specs=[full(own, D), full(own, D), full(own, D), full(copies, own, 2 * D)],
        out_shape=[
            pltpu.HBM((own, D), F32),
            pltpu.HBM((own, D), F32),
            pltpu.HBM((own, D), F32),
            pltpu.HBM((copies, own, 3 * D), BF),
        ],
        compiler_params=pltpu.CompilerParams(vmem_limit_bytes=SMALL_LIMIT),
        name="token_project",
    )(parts, far(normed), far(w_t2a), w_query, w_gate, w_out)


def pack_kernel(packed, keys, out):
    out[...] = keys[...]


def token_pack(packed, keys):
    return pl.pallas_call(
        pack_kernel,
        grid=(1,),
        in_specs=[
            pl.BlockSpec(memory_space=pl.ANY),
            pl.BlockSpec(keys.shape, lambda i: (0, 0, 0)),
        ],
        out_specs=pl.BlockSpec(keys.shape, lambda i: (0, 0, 2)),
        out_shape=pltpu.HBM(packed.shape, BF),
        input_output_aliases={0: 0},
        compiler_params=pltpu.CompilerParams(vmem_limit_bytes=SMALL_LIMIT),
        name="token_pack",
    )(packed, keys)


def key_kernel(key_normed, wk, wv, k_t, v_t):
    k_t[...] = dot(key_normed[...], wk[...]).astype(BF).T
    v_t[...] = dot(key_normed[...], wv[...]).astype(BF).T


def token_keys(mine, w_keyval):
    tok_col = mine.shape[0]
    span = GROUP * HD
    groups = H // GROUP
    return pl.pallas_call(
        key_kernel,
        grid=(groups,),
        in_specs=[
            pl.BlockSpec((tok_col, D), lambda i: (0, 2)),
            pl.BlockSpec((D, span), lambda i: (0, i)),
            pl.BlockSpec((D, span), lambda i: (0, groups + i)),
        ],
        out_specs=[pl.BlockSpec((span, tok_col), lambda i: (i, 0)) for _ in range(2)],
        out_shape=[pltpu.HBM((D, tok_col), BF) for _ in range(2)],
        compiler_params=pltpu.CompilerParams(vmem_limit_bytes=SMALL_LIMIT),
        name="token_keys",
    )(mine, far(w_keyval), far(w_keyval))


def forward_kernel(
    core, k_t, v_t, q_mine, q_theirs, g_mine, g_theirs, bias,
    q, q_t, g, g_t, mixed, stats, exps, out_t,
):
    half = q_mine.shape[0]
    mine = pl.ds(pl.multiple_of(core[0] * half, half), half)
    theirs = pl.ds(pl.multiple_of((1 - core[0]) * half, half), half)
    q[mine, :] = q_mine[...]
    q[theirs, :] = q_theirs[...]
    g[mine, :] = g_mine[...]
    g[theirs, :] = g_theirs[...]
    q_t[...] = q[...].T
    g_t[...] = g[...].T
    copies = stats.shape[0]
    rows = q.shape[0]
    scale = 1.0 / math.sqrt(HD)
    keys = k_t[...]
    values = v_t[...]
    lane = lax.broadcasted_iota(jnp.int32, (CHUNK, 128), 1)
    tops = [jnp.zeros((CHUNK, 128), F32) for _ in range(rows // CHUNK)]
    totals = []
    deltas = []
    for head in range(GROUP):
        start, low, high = head_window(head)
        wide = widened(keys, head)
        for part in range(rows // CHUNK):
            at = pl.ds(part * CHUNK, CHUNK)
            score = dot(q[at, low:high], wide) * scale + bias[head, at, :].astype(F32)
            top = jnp.max(score, axis=1, keepdims=True)
            exps[at, :] = jnp.exp(score - top).astype(BF)
            tops[part] = jnp.where(lane == head, top, tops[part])
        ones = jnp.ones((16, values.shape[1]), BF)
        weighted = dot_t(jnp.concatenate([values[start : start + HD], ones], axis=0), exps[...])
        total = weighted[HD : HD + 1]
        one = weighted[:HD] / total
        out_t[start : start + HD, :] = one
        totals.append(total)
        deltas.append(
            jnp.sum(g_t[start : start + HD, :].astype(F32) * one, axis=0, keepdims=True)
        )
    tops_t = jnp.concatenate(tops, axis=0).T[:GROUP]
    lse = tops_t + jnp.log(jnp.concatenate(totals, axis=0))
    delta = jnp.concatenate(deltas, axis=0)
    high = lse.astype(BF).astype(F32)
    middle = (lse - high).astype(BF).astype(F32)
    triple = jnp.concatenate([high, middle, delta], axis=0).astype(BF)
    for copy in range(copies):
        stats[copy, 0] = triple
    straight = out_t[...].astype(BF).T
    cols, own, _ = mixed.shape
    for k in range(cols):
        at = slice(slab(k, cols) * own, (slab(k, cols) + 1) * own)
        mixed[k] = straight[at]


def token_forward(core, k_t, v_t, mine, theirs, bias, cols):
    copies = cols // CORES
    half = mine.shape[0]
    tok_col = half
    rows = CORES * half
    span = GROUP * HD
    groups = H // GROUP
    return pl.pallas_call(
        forward_kernel,
        grid=(groups,),
        in_specs=[
            pl.BlockSpec(memory_space=pltpu.SMEM),
            pl.BlockSpec((span, tok_col), lambda i: (i, 0)),
            pl.BlockSpec((span, tok_col), lambda i: (i, 0)),
            pl.BlockSpec((half, span), lambda i: (0, i)),
            pl.BlockSpec((half, span), lambda i: (0, i)),
            pl.BlockSpec((half, span), lambda i: (0, groups + i)),
            pl.BlockSpec((half, span), lambda i: (0, groups + i)),
            pl.BlockSpec((GROUP, rows, tok_col), lambda i: (i, 0, 0)),
        ],
        out_specs=[
            pl.BlockSpec((rows, span), lambda i: (0, i)),
            pl.BlockSpec((span, rows), lambda i: (i, 0)),
            pl.BlockSpec((rows, span), lambda i: (0, i)),
            pl.BlockSpec((span, rows), lambda i: (i, 0)),
            pl.BlockSpec((cols, rows // cols, span), lambda i: (0, 0, i)),
            pl.BlockSpec((copies, 1, 3 * GROUP, rows), lambda i: (0, i, 0, 0)),
        ],
        out_shape=[
            pltpu.HBM((rows, D), BF),
            pltpu.HBM((D, rows), BF),
            pltpu.HBM((rows, D), BF),
            pltpu.HBM((D, rows), BF),
            pltpu.HBM((cols, rows // cols, D), BF),
            pltpu.HBM((copies, groups, 3 * GROUP, rows), BF),
        ],
        scratch_shapes=[pltpu.VMEM((rows, tok_col), BF), pltpu.VMEM((span, rows), F32)],
        compiler_params=pltpu.CompilerParams(vmem_limit_bytes=VMEM_LIMIT),
        name="token_forward",
    )(core, far(k_t), far(v_t), mine, theirs, mine, theirs, far(bias))


def backward_kernel(
    core, mine, theirs, q, q_t, g, g_t, k_t, v_t, bias, wk, wv, q_mine, q_theirs, kv_feat,
    probs, slopes, q_acc, k_acc, v_acc, straight, feat,
):
    rows = q.shape[0]
    tok_col = k_t.shape[1]
    scale = 1.0 / math.sqrt(HD)
    logs = []
    deltas = []
    for part in (mine, theirs):
        for k in range(part.shape[0]):
            triple = part[k, 0].astype(F32)
            logs.append(triple[:GROUP] + triple[GROUP : 2 * GROUP])
            deltas.append(triple[2 * GROUP :])
    top = logs[0]
    for one in logs[1:]:
        top = jnp.maximum(top, one)
    share_sum = jnp.zeros_like(top)
    delta = jnp.zeros_like(top)
    for one, other in zip(logs, deltas):
        share = jnp.exp(one - top)
        share_sum = share_sum + share
        delta = delta + share * other
    lse = top + jnp.log(share_sum)
    delta = delta / share_sum
    filler = jnp.zeros((128 - 2 * GROUP, rows), F32)
    columns = jnp.concatenate([lse, delta, filler], axis=0).T
    for head in range(GROUP):
        start, low, high = head_window(head)
        wide_k = widened(k_t[...], head)
        wide_v = widened(v_t[...], head)
        for part in range(rows // CHUNK):
            at = pl.ds(part * CHUNK, CHUNK)
            some = columns[part * CHUNK : (part + 1) * CHUNK]
            score = dot(q[at, low:high], wide_k) * scale + bias[head, at, :].astype(F32)
            prob = jnp.exp(score - some[:, head : head + 1])
            grad = dot(g[at, low:high], wide_v) - some[:, GROUP + head : GROUP + head + 1]
            probs[at, :] = prob.astype(BF)
            slopes[at, :] = (prob * grad).astype(BF)
        here = pl.ds(start, HD)
        k_acc[here, :] = dot(q_t[here, :], slopes[...]) * scale
        v_acc[here, :] = dot(g_t[here, :], probs[...])
        q_acc[here, :] = dot_t(k_t[here, :], slopes[...]) * scale
    new = dot(wk[...], k_acc[...].astype(BF)) + dot(wv[...], v_acc[...].astype(BF))

    @pl.when(pl.program_id(0) == 0)
    def _():
        feat[...] = new

    @pl.when(pl.program_id(0) > 0)
    def _():
        kv_feat[...] = (feat[...] + new).astype(BF).T

    straight[...] = q_acc[...].astype(BF).T
    half = q_mine.shape[0]
    q_mine[...] = straight[pl.ds(pl.multiple_of(core[0] * half, half), half), :]
    q_theirs[...] = straight[pl.ds(pl.multiple_of((1 - core[0]) * half, half), half), :]


def token_backward(core, mine, theirs, q, q_t, g, g_t, k_t, v_t, bias, w_keyval):
    rows = q.shape[0]
    tok_col = k_t.shape[1]
    parts = mine.shape[0]
    half = rows // CORES
    groups = H // GROUP
    span = GROUP * HD
    straight = lambda: pl.BlockSpec((rows, span), lambda i: (0, i))
    turned = lambda: pl.BlockSpec((span, rows), lambda i: (i, 0))
    keyed = lambda: pl.BlockSpec((span, tok_col), lambda i: (i, 0))
    return pl.pallas_call(
        backward_kernel,
        grid=(groups,),
        in_specs=[
            pl.BlockSpec(memory_space=pltpu.SMEM),
            pl.BlockSpec((parts, 1, 3 * GROUP, rows), lambda i: (0, i, 0, 0)),
            pl.BlockSpec((parts, 1, 3 * GROUP, rows), lambda i: (0, i, 0, 0)),
            straight(),
            turned(),
            straight(),
            turned(),
            keyed(),
            keyed(),
            pl.BlockSpec((GROUP, rows, tok_col), lambda i: (i, 0, 0)),
            pl.BlockSpec((D, span), lambda i: (0, i)),
            pl.BlockSpec((D, span), lambda i: (0, groups + i)),
        ],
        out_specs=[
            pl.BlockSpec((half, span), lambda i: (0, i)),
            pl.BlockSpec((half, span), lambda i: (0, i)),
            pl.BlockSpec((tok_col, D), lambda i: (0, 0)),
        ],
        out_shape=[
            pltpu.HBM((half, D), BF),
            pltpu.HBM((half, D), BF),
            pltpu.HBM((tok_col, D), BF),
        ],
        scratch_shapes=[
            pltpu.VMEM((rows, tok_col), BF),
            pltpu.VMEM((rows, tok_col), BF),
            pltpu.VMEM((span, rows), F32),
            pltpu.VMEM((span, tok_col), F32),
            pltpu.VMEM((span, tok_col), F32),
            pltpu.VMEM((rows, span), BF),
            pltpu.VMEM((D, tok_col), F32),
        ],
        compiler_params=pltpu.CompilerParams(vmem_limit_bytes=VMEM_LIMIT),
        name="token_backward",
    )(
        core,
        mine,
        theirs,
        far(q),
        far(q_t),
        far(g),
        far(g_t),
        far(k_t),
        far(v_t),
        far(bias),
        far(w_keyval),
        far(w_keyval),
    )


def far(x):
    return pltpu.with_memory_space_constraint(x, pltpu.HBM)


def shaped(shape, dtype):
    return jax.ShapeDtypeStruct(shape, dtype)


def whole(kernel, outs, args, name, scalars=0, scratch=()):
    specs = [pl.BlockSpec(memory_space=pltpu.SMEM)] * scalars
    specs += [pl.BlockSpec(memory_space=pltpu.VMEM)] * (len(args) - scalars)
    return pl.pallas_call(
        kernel,
        in_specs=specs,
        out_specs=[pl.BlockSpec(memory_space=pltpu.VMEM)] * len(outs),
        out_shape=list(outs),
        scratch_shapes=list(scratch),
        compiler_params=pltpu.CompilerParams(vmem_limit_bytes=SMALL_LIMIT),
        name=name,
    )(*args)


def head_lanes(head):
    lane = lax.broadcasted_iota(jnp.int32, (1, DA), 1)
    return (lane >= head * AHD) & (lane < (head + 1) * AHD)


def stacked(x):
    return jnp.concatenate(
        [jnp.where(head_lanes(head), x, jnp.zeros_like(x)) for head in range(AH)], axis=0
    )


def unstacked(x):
    total = jnp.zeros((QBLK, DA), F32)
    for head in range(AH):
        total = jnp.where(head_lanes(head), x[head * QBLK : (head + 1) * QBLK], total)
    return total


def picked(start, padded_rows):
    row = lax.broadcasted_iota(jnp.int32, (KWIN, padded_rows), 0)
    lane = lax.broadcasted_iota(jnp.int32, (KWIN, padded_rows), 1)
    return jnp.where(row + start == lane, 1.0, 0.0).astype(BF)


def atoms_forward_kernel(
    starts, base, before, atoms, after, bias, token, gain, wq, wkv, wo, wagg, cot, tokens, tokens_cot,
    part, mid, slope, query, window, prob, mixed,
):
    atom_dev = atoms.shape[0]
    blocks = window.shape[0]
    cols, own, _ = part.shape
    tok_row = cols * own
    scale = 1.0 / math.sqrt(AHD)
    padded = jnp.concatenate([before[...], atoms[...], after[...]], axis=0).astype(F32)
    padded_rows = padded.shape[0]
    normed = layer_norm(padded, gain[...]).astype(BF)
    query[...] = dot(normed[RIM : RIM + atom_dev], wq[...]).astype(BF)
    keyval = dot(normed, wkv[...]).astype(BF)
    for block in range(blocks):
        at = pl.ds(block * QBLK, QBLK)
        rows = dot(picked(starts[block] - base[0], padded_rows), keyval).astype(BF)
        window[block] = rows
        score = dot_t(stacked(query[at, :]), rows[:, :DA]) * scale + bias[block].astype(F32)
        exps = jnp.exp(score - jnp.max(score, axis=-1, keepdims=True))
        one = exps / jnp.sum(exps, axis=-1, keepdims=True)
        prob[block] = one
        mixed[at, :] = unstacked(dot(one.astype(BF), rows[:, DA:])).astype(BF)
    mid[...] = (atoms[...].astype(F32) + dot(mixed[...], wo[...])).astype(BF)
    slot = lax.broadcasted_iota(jnp.int32, (tok_row, atom_dev), 0)
    member = jnp.where(slot + base[1] == token[...], 1.0, 0.0).astype(BF)
    width = tokens.shape[0]
    cot_part = dot(member, cot[...]).astype(BF)
    blank = jnp.zeros((part.shape[2] - D - DA - 2 * width, tok_row), BF)
    rest = jnp.concatenate([tokens[...], tokens_cot[...], blank], axis=0).T
    for k in range(cols):
        at = slice(slab(k, cols) * own, (slab(k, cols) + 1) * own)
        part[k, :, D : D + DA] = cot_part[at]
        part[k, :, D + DA :] = rest[at]
    for low in range(0, D, 256):
        at = pl.ds(low, 256)
        pre = dot(mid[...], wagg[:, at])
        gate = sigmoid(pre)
        slope[:, at] = gate * (1.0 + pre * (1.0 - gate))
        sums = dot(member, (pre * gate).astype(BF)).astype(BF)
        for k in range(cols):
            part[k, :, at] = sums[slab(k, cols) * own : (slab(k, cols) + 1) * own]


def summed(parts):
    total = parts[0].astype(F32)
    for k in range(1, parts.shape[0]):
        total = total + parts[k].astype(F32)
    return total


def norm_kernel(parts, inverse, gain, mid, normed, spread):
    cols = parts.shape[0]
    width = D // cols
    low = D + DA
    for k in range(cols):
        mid[:, k * width : (k + 1) * width] = parts[k, :, low : low + width].astype(F32)
    value = mid[...] + summed(parts[:, :, :D]) * inverse[...]
    mid[...] = value
    out = layer_norm(value, gain[...]).astype(BF)
    normed[...] = out
    for k in range(spread.shape[0]):
        spread[k] = out


def keyval_kernel(parts, out):
    out[...] = summed(parts[...]).astype(BF)


def own_kernel(
    place, parts, mine, theirs, gate_ref, gated_ref, token_mid, wout, wgate, wt2a, tokens, lifted, feature, attended
):
    cols, own, _ = parts.shape
    span = GROUP * HD
    lane = lax.broadcasted_iota(jnp.int32, (GROUP, span), 1)
    row = lax.broadcasted_iota(jnp.int32, (GROUP, span), 0)
    widen = jnp.where((lane >= row * HD) & (lane < (row + 1) * HD), 1.0, 0.0).astype(BF)
    half = cols // CORES
    rows = mine.shape[3]
    slot = lax.broadcasted_iota(jnp.int32, (rows, own), 0)
    token = lax.broadcasted_iota(jnp.int32, (rows, own), 1)
    select = jnp.where(slot == token + place[0], 1.0, 0.0).astype(BF)
    tables = []
    for part in (mine, theirs):
        flat = part[...].reshape(half * (H // GROUP) * 3 * GROUP, rows)
        tables.append(dot(flat, select).T)
    for group in range(H // GROUP):
        logs = []
        for k in range(cols):
            low = (k // CORES * (H // GROUP) + group) * 3 * GROUP
            mine_first = jnp.where(place[1] == k % CORES, 1.0, 0.0)
            triple = (
                tables[0][:, low : low + 2 * GROUP] * mine_first
                + tables[1][:, low : low + 2 * GROUP] * (1.0 - mine_first)
            )
            logs.append(triple[:, :GROUP] + triple[:, GROUP:])
        top = logs[0]
        for k in range(1, cols):
            top = jnp.maximum(top, logs[k])
        shares = [jnp.exp(one - top) for one in logs]
        total = shares[0]
        for k in range(1, cols):
            total = total + shares[k]
        share = jnp.concatenate([one / total for one in shares], axis=0)
        high = share.astype(BF)
        rest = (share - high.astype(F32)).astype(BF)
        weight = dot(high, widen) + dot(rest, widen)
        value = jnp.zeros((own, span), F32)
        for k in range(cols):
            at = slice(group * span, (group + 1) * span)
            value = value + weight[k * own : (k + 1) * own] * parts[k, :, at].astype(F32)
        attended[:, group * span : (group + 1) * span] = value
    gate = gate_ref[...]
    value = attended[...]
    new = (token_mid[...] + dot((gate * value).astype(BF), wout[...])).astype(BF)
    tokens[...] = new
    lifted[...] = dot(new, wt2a[...]).astype(BF)
    grad_gate = (gated_ref[...] * value * gate * (1.0 - gate)).astype(BF)
    feature[...] = dot_t(grad_gate, wgate[...])


def token_kernel(parts, key_feature, feature, grad_new, token_mid, gain, wquery, tokens, lifted, out):
    cols = CORES * parts.shape[0]
    width = D // cols
    total = summed(parts[...]).astype(BF)
    normed_grad = dot_t(total, wquery[...]) + feature[...] + key_feature[...].astype(F32)
    grad = grad_new[...] + norm_back(token_mid[...], gain[...], normed_grad)
    grad = grad.astype(BF)
    new = tokens[...]
    low = D + DA
    pair = CORES * width
    for k in range(cols // CORES):
        out[k, :, :D] = grad
        out[k, :, D:low] = lifted[...]
        out[k, :, low:] = new[:, k * pair : (k + 1) * pair]


def atoms_backward_kernel(
    starts, place, mine, theirs, token, inverse, slope, cot, mid, query, window, prob, mixed,
    wagg, wo, wq, new, tokens_out, grad_tokens, inner, first, last, atoms_grad, feature, padded,
):
    atom_dev = cot.shape[0]
    blocks = window.shape[0]
    half = mine.shape[0]
    tok_row = CORES * half
    width = tokens_out.shape[1]
    core = place[0]
    padded_rows = padded.shape[0]
    scale = 1.0 / math.sqrt(AHD)
    slot = lax.broadcasted_iota(jnp.int32, (atom_dev, tok_row), 1)
    atom_inverse = jnp.sum(
        jnp.where(slot == token[...], inverse[...], 0.0), axis=1, keepdims=True
    )
    parts = ((mine, core * half), (theirs, (1 - core) * half))
    slot = lax.broadcasted_iota(jnp.int32, (atom_dev, half), 1)
    members = [
        jnp.where(slot + base == token[...], 1.0, 0.0).astype(BF) for _, base in parts
    ]

    def gathered(at):
        return dot(members[0], mine[:, at]) + dot(members[1], theirs[:, at])

    row = lax.broadcasted_iota(jnp.int32, (D, width), 0)
    lane = lax.broadcasted_iota(jnp.int32, (D, width), 1)
    column = jnp.where(row == lane + place[1] * width, 1.0, 0.0).astype(BF)
    for part, base in parts:
        here = pl.ds(pl.multiple_of(base, half), half)
        low = D + DA
        pair = part[:, low:].astype(F32)
        tokens_out[here, :] = jnp.where(core == 0, pair[:, :width], pair[:, width:]).astype(BF)
        grad_tokens[here, :] = dot(part[:, :D], column).astype(BF)
    grads = cot[...].astype(F32)
    for low in range(0, D, 256):
        at = pl.ds(low, 256)
        hidden = (gathered(at) * atom_inverse * slope[:, at]).astype(BF)
        grads = grads + dot_t(hidden, wagg[:, at])
    atoms_grad[...] = grads
    mixed_grad = dot_t(grads.astype(BF), wo[...]).astype(BF)
    padded[...] = jnp.zeros(padded.shape, F32)
    for block in range(blocks):
        at = slice(block * QBLK, (block + 1) * QBLK)
        rows = window[block]
        one = prob[block]
        grad_heads = stacked(mixed_grad[at])
        query_heads = stacked(query[at, :])
        grad_wide = grad_heads.astype(F32)
        tall = jnp.concatenate([mixed[at, :]] * AH, axis=0).astype(F32)
        delta = jnp.sum(grad_wide * tall, axis=-1, keepdims=True)
        sgrad = (one * (dot_t(grad_heads, rows[:, DA:]) - delta)).astype(BF)
        qgrad = (unstacked(dot(sgrad, rows[:, :DA])) * scale).astype(BF)
        feature[at, :] = dot_t(qgrad, wq[...])
        key_grad = rows_dot(sgrad, query_heads) * scale
        value_grad = rows_dot(one.astype(BF), grad_heads)
        both = jnp.concatenate([key_grad, value_grad], axis=1).astype(BF)
        padded[...] += rows_dot(picked(starts[block], padded_rows), both)
    first[...] = padded[:RIM, :].astype(BF)
    last[...] = padded[RIM + atom_dev :, :].astype(BF)
    inner[...] = padded[RIM : RIM + atom_dev, :]
    lift = gathered(slice(D, D + DA))
    new[...] = (mid[...].astype(F32) + lift).astype(BF)


def atoms_last_kernel(inner, before, after, feature, atoms_grad, atoms, gain, wkv, out):
    atom_dev = atoms.shape[0]
    keyval = jnp.concatenate(
        [
            inner[:RIM, :] + before[...].astype(F32),
            inner[RIM : atom_dev - RIM, :],
            inner[atom_dev - RIM :, :] + after[...].astype(F32),
        ],
        axis=0,
    ).astype(BF)
    feat = feature[...] + dot_t(keyval, wkv[...])
    back = norm_back(atoms[...].astype(F32), gain[...], feat)
    out[...] = (atoms_grad[...] + back).astype(BF)


def local(
    atoms,
    tokens,
    atom_bias,
    token_bias,
    atom_index,
    atom_counts,
    window_starts,
    gain_atom,
    w_atom_q,
    w_atom_kv,
    w_atom_o,
    w_agg,
    gain_token,
    w_query,
    w_keyval,
    w_gate,
    w_out,
    w_t2a,
    atoms_cot,
    tokens_cot,
):
    rows = lax.axis_size("row")
    cols = lax.axis_size("col")
    row_index = lax.axis_index("row")
    col_index = lax.axis_index("col")
    atom_dev = atoms.shape[0]
    blocks = window_starts.shape[0]
    tok_row = tokens.shape[0]
    tok_col = token_bias.shape[2]
    own = tok_row // cols
    width = tokens.shape[1]
    first_atom = (row_index * cols + col_index) * atom_dev

    before, after = neighbours(atoms, RIM)

    local_token = atom_index - row_index * tok_row
    inverse_count = 1.0 / atom_counts.astype(F32)
    core = col_index % CORES
    half = tok_row // CORES
    first_own = core * half + col_index // CORES * own
    inv_own = lax.dynamic_slice_in_dim(inverse_count, first_own, own, 0)

    starts = window_starts - first_atom + RIM
    gain_a = gain_atom[None, :]
    gain_t = gain_token[None, :]
    part, atoms_mid, slope, atom_query, window, atom_prob, atom_mixed = whole(
        atoms_forward_kernel,
        [
            pltpu.HBM((cols, own, D + 2 * DA), BF),
            pltpu.HBM((atom_dev, DA), BF),
            pltpu.HBM((atom_dev, D), F32),
            pltpu.HBM((atom_dev, DA), BF),
            pltpu.HBM((blocks, KWIN, 2 * DA), BF),
            pltpu.HBM((blocks, AH * QBLK, KWIN), F32),
            pltpu.HBM((atom_dev, DA), BF),
        ],
        (
            window_starts,
            jnp.stack([first_atom - RIM, row_index * tok_row]),
            before,
            far(atoms),
            after,
            far(atom_bias.reshape(blocks, AH * QBLK, KWIN)),
            far(atom_index[None, :]),
            far(gain_a),
            far(w_atom_q),
            far(w_atom_kv),
            far(w_atom_o),
            far(w_agg),
            far(atoms_cot),
            far(tokens.T),
            far(tokens_cot.T),
        ),
        "atoms_forward",
        scalars=2,
    )

    sums = exchange(part, "col")
    tokens_mid, normed_own, spread = whole(
        norm_kernel,
        [
            pltpu.HBM((own, D), F32),
            pltpu.HBM((own, D), BF),
            pltpu.HBM((rows, own, D), BF),
        ],
        (sums, inv_own[:, None], gain_t),
        "token_norm",
    )
    keys_own = exchange(spread, "row")
    gate_own, gated_own, grad_new, packed = token_project(
        sums, normed_own, w_t2a, w_query, w_gate, w_out, rows
    )
    packed = token_pack(packed, keys_own)
    mine, theirs = halves_of(packed)
    to_row = [
        (i * cols + r * CORES + p, r * cols + i * CORES + p)
        for r in range(rows)
        for i in range(rows)
        for p in range(CORES)
    ]
    k_t, v_t = token_keys(mine.reshape(half, 3 * D), w_keyval)
    q, q_t, g, g_t, mixed, stats = token_forward(
        core[None],
        k_t,
        v_t,
        mine.reshape(half, 3 * D),
        theirs.reshape(half, 3 * D),
        token_bias,
        cols,
    )
    stats = halves_of(stats)
    mixed_parts = exchange(mixed, "col")
    q_mine, q_theirs, kv_feat = token_backward(
        core[None], *stats, q, q_t, g, g_t, k_t, v_t, token_bias, w_keyval
    )
    swap = [(i, i ^ 1) for i in range(cols)]
    q_other = lax.ppermute(q_theirs, "col", swap)
    kv_parts = exchange(kv_feat.reshape(rows, own, D), "row")
    q_pair = (q_mine.astype(F32) + q_other.astype(F32)).astype(BF)
    q_parts = among_core(q_pair.reshape(cols // CORES, own, D))
    tokens_new, lifted, gate_feat = whole(
        own_kernel,
        [shaped((own, D), BF), shaped((own, DA), BF), shaped((own, D), F32)],
        (
            jnp.stack([first_own, core]),
            mixed_parts,
            *stats,
            far(gate_own),
            far(gated_own),
            far(tokens_mid),
            far(w_out),
            far(w_gate),
            far(w_t2a),
        ),
        "token_own",
        scalars=1,
        scratch=[pltpu.VMEM((own, D), F32)],
    )
    (kv_own,) = whole(
        keyval_kernel,
        [shaped((own, D), BF)],
        (kv_parts,),
        "token_keyval",
    )
    kv_back = lax.ppermute(kv_own, ("row", "col"), to_row)
    (mid_spread,) = whole(
        token_kernel,
        [pltpu.HBM((cols // CORES, own, D + DA + CORES * width), BF)],
        (
            q_parts,
            kv_back,
            gate_feat,
            far(grad_new),
            far(tokens_mid),
            gain_t,
            far(w_query),
            tokens_new,
            lifted,
        ),
        "token_grads",
    )
    mine, theirs = halves_of(mid_spread)

    atoms_new, tokens_out, grad_tokens, inner, first, last, atoms_grad, query_feat = whole(
        atoms_backward_kernel,
        [
            shaped((atom_dev, DA), BF),
            shaped((tok_row, width), BF),
            shaped((tok_row, width), BF),
            pltpu.HBM((atom_dev, 2 * DA), F32),
            shaped((RIM, 2 * DA), BF),
            shaped((RIM, 2 * DA), BF),
            pltpu.HBM((atom_dev, DA), F32),
            pltpu.HBM((atom_dev, DA), F32),
        ],
        (
            starts,
            jnp.stack([core, col_index]),
            mine.reshape(half, -1),
            theirs.reshape(half, -1),
            local_token[:, None],
            inverse_count[None, :],
            slope,
            far(atoms_cot),
            far(atoms_mid),
            far(atom_query),
            window,
            atom_prob,
            far(atom_mixed),
            far(w_agg),
            far(w_atom_o),
            far(w_atom_q),
        ),
        "atoms_backward",
        scalars=2,
        scratch=[pltpu.VMEM((atom_dev + 2 * RIM, 2 * DA), F32)],
    )
    axes = ("row", "col")
    up = [(i, i + 1) for i in range(rows * cols - 1)]
    down = [(j, i) for i, j in up]
    from_before = lax.ppermute(last, axes, up)
    from_after = lax.ppermute(first, axes, down)
    (grad_atoms,) = whole(
        atoms_last_kernel,
        [shaped((atom_dev, DA), BF)],
        (
            far(inner),
            from_before,
            from_after,
            far(query_feat),
            far(atoms_grad),
            far(atoms),
            gain_a,
            far(w_atom_kv),
        ),
        "atoms_last",
    )
    return (atoms_new, tokens_out, grad_atoms, grad_tokens)


def solution(mesh):
    placed = (
        P(("row", "col"), None),
        P("row", "col"),
        P(("row", "col"), None, None, None),
        P(None, "row", "col"),
        P(("row", "col")),
        P("row"),
        P(("row", "col")),
        P(),
        P(),
        P(),
        P(),
        P(),
        P(),
        P(),
        P(),
        P(),
        P(),
        P(),
        P(("row", "col"), None),
        P("row", "col"),
    )
    return jax.shard_map(
        local,
        mesh=mesh,
        in_specs=placed,
        out_specs=(
            P(("row", "col"), None),
            P("row", "col"),
            P(("row", "col"), None),
            P("row", "col"),
        ),
        check_vma=False,
    )
```

```python
import math

import jax
import jax.numpy as jnp
from jax import lax
from jax.experimental import pallas as pl
from jax.experimental.pallas import tpu as pltpu
from jax.sharding import PartitionSpec as P

D = 768
H = 16
HD = 48
DA = 128
AH = 4
AHD = 32
QBLK = 32
KWIN = 128
RIM = 64
EPS = 1e-05
BF = jnp.bfloat16
F32 = jnp.float32
GROUP = 8
CORES = 2
CHUNK = 128
VMEM_LIMIT = 24 * 1024 * 1024
SMALL_LIMIT = 14 * 1024 * 1024


def dot(a, b):
    return jnp.dot(a, b, preferred_element_type=F32)


def dot_t(a, b):
    return lax.dot_general(a, b, (((1,), (1,)), ((), ())), preferred_element_type=F32)


def centred(values):
    center = values - jnp.mean(values, axis=-1, keepdims=True)
    inv = lax.rsqrt(jnp.mean(center * center, axis=-1, keepdims=True) + EPS)
    return center * inv, inv


def layer_norm(values, gain_vec):
    return centred(values)[0] * gain_vec


def norm_back(values, gain_vec, cotangent):
    unit, inv = centred(values)
    g = cotangent * gain_vec
    return inv * (
        g
        - jnp.mean(g, axis=-1, keepdims=True)
        - unit * jnp.mean(g * unit, axis=-1, keepdims=True)
    )


def sigmoid(x):
    return 1.0 / (1.0 + jnp.exp(-x))


def exchange(x, axis):
    return lax.all_to_all(x, axis, 0, 0)


def among_core(x):
    cols = lax.axis_size("col")
    groups = [list(range(core, cols, CORES)) for core in range(CORES)]
    return lax.all_to_all(x, "col", 0, 0, axis_index_groups=groups)


def halves_of(x):
    cols = lax.axis_size("col")
    mine = among_core(x)
    theirs = lax.ppermute(mine, "col", [(i, i ^ 1) for i in range(cols)])
    return mine, theirs


def neighbours(x, width):
    axes = ("row", "col")
    devices = lax.axis_size("row") * lax.axis_size("col")
    up = [(i, i + 1) for i in range(devices - 1)]
    down = [(j, i) for i, j in up]
    before = lax.ppermute(x[x.shape[0] - width :], axes, up)
    after = lax.ppermute(x[:width], axes, down)
    return before, after


def slab(k, count):
    return k % CORES * (count // CORES) + k // CORES


def rows_dot(a, b):
    return lax.dot_general(a, b, (((0,), (0,)), ((), ())), preferred_element_type=F32)


def head_window(head):
    start = head * HD
    low = start // 128 * 128
    high = -(-(start + HD) // 128) * 128
    return start, low, high


def widened(x_t, head):
    start, low, high = head_window(head)
    parts = []
    if start > low:
        parts.append(jnp.zeros((start - low, x_t.shape[1]), x_t.dtype))
    parts.append(x_t[start : start + HD])
    if high > start + HD:
        parts.append(jnp.zeros((high - start - HD, x_t.shape[1]), x_t.dtype))
    return jnp.concatenate(parts, axis=0)


def project_kernel(parts, normed, wt2a, wq, wg, wout, gate, gated, grad_new, both):
    cols = parts.shape[0]
    width = D // cols
    for k in range(cols):
        at = slice(k * width, (k + 1) * width)
        grad_new[:, at] = parts[k, :, DA + width : DA + 2 * width].astype(F32)
    cot = summed(parts[:, :, :DA]).astype(BF)
    grad_new[...] = grad_new[...] + dot_t(cot, wt2a[...])
    query = dot(normed[...], wq[...]).astype(BF)
    opened = sigmoid(dot(normed[...], wg[...]))
    grad = dot_t(grad_new[...].astype(BF), wout[...])
    gate[...] = opened
    gated[...] = grad
    grad = (grad * opened).astype(BF)
    for k in range(both.shape[0]):
        both[k, :, :D] = query
        both[k, :, D:] = grad


def token_project(parts, normed, w_t2a, w_query, w_gate, w_out, copies):
    cols, own, _ = parts.shape
    last = D // (2 * DA)
    full = lambda *shape: pl.BlockSpec(shape, lambda i: (0,) * len(shape))
    return pl.pallas_call(
        project_kernel,
        grid=(1,),
        in_specs=[
            pl.BlockSpec((cols, own, 2 * DA), lambda i: (0, 0, last)),
            full(own, D),
            full(D, DA),
            full(D, D),
            full(D, D),
            full(D, D),
        ],
        out_specs=[full(own, D), full(own, D), full(own, D), full(copies, own, 2 * D)],
        out_shape=[
            pltpu.HBM((own, D), F32),
            pltpu.HBM((own, D), F32),
            pltpu.HBM((own, D), F32),
            pltpu.HBM((copies, own, 3 * D), BF),
        ],
        compiler_params=pltpu.CompilerParams(vmem_limit_bytes=SMALL_LIMIT),
        name="token_project",
    )(parts, far(normed), far(w_t2a), w_query, w_gate, w_out)


def pack_kernel(packed, keys, out):
    out[...] = keys[...]


def token_pack(packed, keys):
    return pl.pallas_call(
        pack_kernel,
        grid=(1,),
        in_specs=[
            pl.BlockSpec(memory_space=pl.ANY),
            pl.BlockSpec(keys.shape, lambda i: (0, 0, 0)),
        ],
        out_specs=pl.BlockSpec(keys.shape, lambda i: (0, 0, 2)),
        out_shape=pltpu.HBM(packed.shape, BF),
        input_output_aliases={0: 0},
        compiler_params=pltpu.CompilerParams(vmem_limit_bytes=SMALL_LIMIT),
        name="token_pack",
    )(packed, keys)


def key_kernel(key_normed, wk, wv, k_t, v_t):
    k_t[...] = dot(key_normed[...], wk[...]).astype(BF).T
    v_t[...] = dot(key_normed[...], wv[...]).astype(BF).T


def token_keys(mine, w_keyval):
    tok_col = mine.shape[0]
    span = GROUP * HD
    groups = H // GROUP
    return pl.pallas_call(
        key_kernel,
        grid=(groups,),
        in_specs=[
            pl.BlockSpec((tok_col, D), lambda i: (0, 2)),
            pl.BlockSpec((D, span), lambda i: (0, i)),
            pl.BlockSpec((D, span), lambda i: (0, groups + i)),
        ],
        out_specs=[pl.BlockSpec((span, tok_col), lambda i: (i, 0)) for _ in range(2)],
        out_shape=[pltpu.HBM((D, tok_col), BF) for _ in range(2)],
        compiler_params=pltpu.CompilerParams(vmem_limit_bytes=SMALL_LIMIT),
        name="token_keys",
    )(mine, far(w_keyval), far(w_keyval))


def forward_kernel(
    core, k_t, v_t, q_mine, q_theirs, g_mine, g_theirs, bias,
    q, q_t, g, g_t, mixed, stats, exps, out_t,
):
    half = q_mine.shape[0]
    mine = pl.ds(pl.multiple_of(core[0] * half, half), half)
    theirs = pl.ds(pl.multiple_of((1 - core[0]) * half, half), half)
    q[mine, :] = q_mine[...]
    q[theirs, :] = q_theirs[...]
    g[mine, :] = g_mine[...]
    g[theirs, :] = g_theirs[...]
    q_t[...] = q[...].T
    g_t[...] = g[...].T
    copies = stats.shape[0]
    rows = q.shape[0]
    scale = 1.0 / math.sqrt(HD)
    keys = k_t[...]
    values = v_t[...]
    lane = lax.broadcasted_iota(jnp.int32, (CHUNK, 128), 1)
    tops = [jnp.zeros((CHUNK, 128), F32) for _ in range(rows // CHUNK)]
    totals = []
    deltas = []
    for head in range(GROUP):
        start, low, high = head_window(head)
        wide = widened(keys, head)
        for part in range(rows // CHUNK):
            at = pl.ds(part * CHUNK, CHUNK)
            score = dot(q[at, low:high], wide) * scale + bias[head, at, :].astype(F32)
            top = jnp.max(score, axis=1, keepdims=True)
            exps[at, :] = jnp.exp(score - top).astype(BF)
            tops[part] = jnp.where(lane == head, top, tops[part])
        ones = jnp.ones((16, values.shape[1]), BF)
        weighted = dot_t(jnp.concatenate([values[start : start + HD], ones], axis=0), exps[...])
        total = weighted[HD : HD + 1]
        one = weighted[:HD] / total
        out_t[start : start + HD, :] = one
        totals.append(total)
        deltas.append(
            jnp.sum(g_t[start : start + HD, :].astype(F32) * one, axis=0, keepdims=True)
        )
    tops_t = jnp.concatenate(tops, axis=0).T[:GROUP]
    lse = tops_t + jnp.log(jnp.concatenate(totals, axis=0))
    delta = jnp.concatenate(deltas, axis=0)
    high = lse.astype(BF).astype(F32)
    middle = (lse - high).astype(BF).astype(F32)
    triple = jnp.concatenate([high, middle, delta], axis=0).astype(BF)
    for copy in range(copies):
        stats[copy, 0] = triple
    straight = out_t[...].astype(BF).T
    cols, own, _ = mixed.shape
    for k in range(cols):
        at = slice(slab(k, cols) * own, (slab(k, cols) + 1) * own)
        mixed[k] = straight[at]


def token_forward(core, k_t, v_t, mine, theirs, bias, cols):
    copies = cols // CORES
    half = mine.shape[0]
    tok_col = half
    rows = CORES * half
    span = GROUP * HD
    groups = H // GROUP
    return pl.pallas_call(
        forward_kernel,
        grid=(groups,),
        in_specs=[
            pl.BlockSpec(memory_space=pltpu.SMEM),
            pl.BlockSpec((span, tok_col), lambda i: (i, 0)),
            pl.BlockSpec((span, tok_col), lambda i: (i, 0)),
            pl.BlockSpec((half, span), lambda i: (0, i)),
            pl.BlockSpec((half, span), lambda i: (0, i)),
            pl.BlockSpec((half, span), lambda i: (0, groups + i)),
            pl.BlockSpec((half, span), lambda i: (0, groups + i)),
            pl.BlockSpec((GROUP, rows, tok_col), lambda i: (i, 0, 0)),
        ],
        out_specs=[
            pl.BlockSpec((rows, span), lambda i: (0, i)),
            pl.BlockSpec((span, rows), lambda i: (i, 0)),
            pl.BlockSpec((rows, span), lambda i: (0, i)),
            pl.BlockSpec((span, rows), lambda i: (i, 0)),
            pl.BlockSpec((cols, rows // cols, span), lambda i: (0, 0, i)),
            pl.BlockSpec((copies, 1, 3 * GROUP, rows), lambda i: (0, i, 0, 0)),
        ],
        out_shape=[
            pltpu.HBM((rows, D), BF),
            pltpu.HBM((D, rows), BF),
            pltpu.HBM((rows, D), BF),
            pltpu.HBM((D, rows), BF),
            pltpu.HBM((cols, rows // cols, D), BF),
            pltpu.HBM((copies, groups, 3 * GROUP, rows), BF),
        ],
        scratch_shapes=[pltpu.VMEM((rows, tok_col), BF), pltpu.VMEM((span, rows), F32)],
        compiler_params=pltpu.CompilerParams(vmem_limit_bytes=VMEM_LIMIT),
        name="token_forward",
    )(core, far(k_t), far(v_t), mine, theirs, mine, theirs, bias)


def backward_kernel(
    core, mine, theirs, q, q_t, g, g_t, k_t, v_t, bias, wk, wv, q_mine, q_theirs, kv_feat,
    probs, slopes, q_acc, k_acc, v_acc, straight, feat,
):
    rows = q.shape[0]
    tok_col = k_t.shape[1]
    scale = 1.0 / math.sqrt(HD)
    logs = []
    deltas = []
    for part in (mine, theirs):
        for k in range(part.shape[0]):
            triple = part[k, 0].astype(F32)
            logs.append(triple[:GROUP] + triple[GROUP : 2 * GROUP])
            deltas.append(triple[2 * GROUP :])
    top = logs[0]
    for one in logs[1:]:
        top = jnp.maximum(top, one)
    share_sum = jnp.zeros_like(top)
    delta = jnp.zeros_like(top)
    for one, other in zip(logs, deltas):
        share = jnp.exp(one - top)
        share_sum = share_sum + share
        delta = delta + share * other
    lse = top + jnp.log(share_sum)
    delta = delta / share_sum
    filler = jnp.zeros((128 - 2 * GROUP, rows), F32)
    columns = jnp.concatenate([lse, delta, filler], axis=0).T
    for head in range(GROUP):
        start, low, high = head_window(head)
        wide_k = widened(k_t[...], head)
        wide_v = widened(v_t[...], head)
        for part in range(rows // CHUNK):
            at = pl.ds(part * CHUNK, CHUNK)
            some = columns[part * CHUNK : (part + 1) * CHUNK]
            score = dot(q[at, low:high], wide_k) * scale + bias[head, at, :].astype(F32)
            prob = jnp.exp(score - some[:, head : head + 1])
            grad = dot(g[at, low:high], wide_v) - some[:, GROUP + head : GROUP + head + 1]
            probs[at, :] = prob.astype(BF)
            slopes[at, :] = (prob * grad).astype(BF)
        here = pl.ds(start, HD)
        k_acc[here, :] = dot(q_t[here, :], slopes[...]) * scale
        v_acc[here, :] = dot(g_t[here, :], probs[...])
        q_acc[here, :] = dot_t(k_t[here, :], slopes[...]) * scale
    new = dot(wk[...], k_acc[...].astype(BF)) + dot(wv[...], v_acc[...].astype(BF))

    @pl.when(pl.program_id(0) == 0)
    def _():
        feat[...] = new

    @pl.when(pl.program_id(0) > 0)
    def _():
        kv_feat[...] = (feat[...] + new).astype(BF).T

    straight[...] = q_acc[...].astype(BF).T
    half = q_mine.shape[0]
    q_mine[...] = straight[pl.ds(pl.multiple_of(core[0] * half, half), half), :]
    q_theirs[...] = straight[pl.ds(pl.multiple_of((1 - core[0]) * half, half), half), :]


def token_backward(core, mine, theirs, q, q_t, g, g_t, k_t, v_t, bias, w_keyval):
    rows = q.shape[0]
    tok_col = k_t.shape[1]
    parts = mine.shape[0]
    half = rows // CORES
    groups = H // GROUP
    span = GROUP * HD
    straight = lambda: pl.BlockSpec((rows, span), lambda i: (0, i))
    turned = lambda: pl.BlockSpec((span, rows), lambda i: (i, 0))
    keyed = lambda: pl.BlockSpec((span, tok_col), lambda i: (i, 0))
    return pl.pallas_call(
        backward_kernel,
        grid=(groups,),
        in_specs=[
            pl.BlockSpec(memory_space=pltpu.SMEM),
            pl.BlockSpec((parts, 1, 3 * GROUP, rows), lambda i: (0, i, 0, 0)),
            pl.BlockSpec((parts, 1, 3 * GROUP, rows), lambda i: (0, i, 0, 0)),
            straight(),
            turned(),
            straight(),
            turned(),
            keyed(),
            keyed(),
            pl.BlockSpec((GROUP, rows, tok_col), lambda i: (i, 0, 0)),
            pl.BlockSpec((D, span), lambda i: (0, i)),
            pl.BlockSpec((D, span), lambda i: (0, groups + i)),
        ],
        out_specs=[
            pl.BlockSpec((half, span), lambda i: (0, i)),
            pl.BlockSpec((half, span), lambda i: (0, i)),
            pl.BlockSpec((tok_col, D), lambda i: (0, 0)),
        ],
        out_shape=[
            pltpu.HBM((half, D), BF),
            pltpu.HBM((half, D), BF),
            pltpu.HBM((tok_col, D), BF),
        ],
        scratch_shapes=[
            pltpu.VMEM((rows, tok_col), BF),
            pltpu.VMEM((rows, tok_col), BF),
            pltpu.VMEM((span, rows), F32),
            pltpu.VMEM((span, tok_col), F32),
            pltpu.VMEM((span, tok_col), F32),
            pltpu.VMEM((rows, span), BF),
            pltpu.VMEM((D, tok_col), F32),
        ],
        compiler_params=pltpu.CompilerParams(vmem_limit_bytes=VMEM_LIMIT),
        name="token_backward",
    )(
        core,
        mine,
        theirs,
        far(q),
        far(q_t),
        far(g),
        far(g_t),
        far(k_t),
        far(v_t),
        far(bias),
        far(w_keyval),
        far(w_keyval),
    )


def far(x):
    return pltpu.with_memory_space_constraint(x, pltpu.HBM)


def shaped(shape, dtype):
    return jax.ShapeDtypeStruct(shape, dtype)


def whole(kernel, outs, args, name, scalars=0, scratch=()):
    specs = [pl.BlockSpec(memory_space=pltpu.SMEM)] * scalars
    specs += [pl.BlockSpec(memory_space=pltpu.VMEM)] * (len(args) - scalars)
    return pl.pallas_call(
        kernel,
        in_specs=specs,
        out_specs=[pl.BlockSpec(memory_space=pltpu.VMEM)] * len(outs),
        out_shape=list(outs),
        scratch_shapes=list(scratch),
        compiler_params=pltpu.CompilerParams(vmem_limit_bytes=SMALL_LIMIT),
        name=name,
    )(*args)


def head_lanes(head):
    lane = lax.broadcasted_iota(jnp.int32, (1, DA), 1)
    return (lane >= head * AHD) & (lane < (head + 1) * AHD)


def stacked(x):
    return jnp.concatenate(
        [jnp.where(head_lanes(head), x, jnp.zeros_like(x)) for head in range(AH)], axis=0
    )


def unstacked(x):
    total = jnp.zeros((QBLK, DA), F32)
    for head in range(AH):
        total = jnp.where(head_lanes(head), x[head * QBLK : (head + 1) * QBLK], total)
    return total


def picked(start, padded_rows):
    row = lax.broadcasted_iota(jnp.int32, (KWIN, padded_rows), 0)
    lane = lax.broadcasted_iota(jnp.int32, (KWIN, padded_rows), 1)
    return jnp.where(row + start == lane, 1.0, 0.0).astype(BF)


def atoms_forward_kernel(
    starts, before, atoms, after, bias, token, gain, wq, wkv, wo, wagg, cot, tokens, tokens_cot,
    part, mid, slope, query, window, prob, mixed,
):
    atom_dev = atoms.shape[0]
    blocks = window.shape[0]
    cols, own, _ = part.shape
    tok_row = cols * own
    scale = 1.0 / math.sqrt(AHD)
    padded = jnp.concatenate([before[...], atoms[...], after[...]], axis=0).astype(F32)
    padded_rows = padded.shape[0]
    normed = layer_norm(padded, gain[...]).astype(BF)
    query[...] = dot(normed[RIM : RIM + atom_dev], wq[...]).astype(BF)
    keyval = dot(normed, wkv[...]).astype(BF)
    for block in range(blocks):
        at = pl.ds(block * QBLK, QBLK)
        rows = dot(picked(starts[block], padded_rows), keyval).astype(BF)
        window[block] = rows
        score = dot_t(stacked(query[at, :]), rows[:, :DA]) * scale + bias[block].astype(F32)
        exps = jnp.exp(score - jnp.max(score, axis=-1, keepdims=True))
        one = exps / jnp.sum(exps, axis=-1, keepdims=True)
        prob[block] = one
        mixed[at, :] = unstacked(dot(one.astype(BF), rows[:, DA:])).astype(BF)
    mid[...] = (atoms[...].astype(F32) + dot(mixed[...], wo[...])).astype(BF)
    slot = lax.broadcasted_iota(jnp.int32, (tok_row, atom_dev), 0)
    member = jnp.where(slot == token[...], 1.0, 0.0).astype(BF)
    width = tokens.shape[0]
    cot_part = dot(member, cot[...]).astype(BF)
    blank = jnp.zeros((part.shape[2] - D - DA - 2 * width, tok_row), BF)
    rest = jnp.concatenate([tokens[...], tokens_cot[...], blank], axis=0).T
    for k in range(cols):
        at = slice(slab(k, cols) * own, (slab(k, cols) + 1) * own)
        part[k, :, D : D + DA] = cot_part[at]
        part[k, :, D + DA :] = rest[at]
    for low in range(0, D, 256):
        at = pl.ds(low, 256)
        pre = dot(mid[...], wagg[:, at])
        gate = sigmoid(pre)
        slope[:, at] = gate * (1.0 + pre * (1.0 - gate))
        sums = dot(member, (pre * gate).astype(BF)).astype(BF)
        for k in range(cols):
            part[k, :, at] = sums[slab(k, cols) * own : (slab(k, cols) + 1) * own]


def summed(parts):
    total = parts[0].astype(F32)
    for k in range(1, parts.shape[0]):
        total = total + parts[k].astype(F32)
    return total


def norm_kernel(parts, inverse, gain, mid, normed, spread):
    cols = parts.shape[0]
    width = D // cols
    low = D + DA
    for k in range(cols):
        mid[:, k * width : (k + 1) * width] = parts[k, :, low : low + width].astype(F32)
    value = mid[...] + summed(parts[:, :, :D]) * inverse[...]
    mid[...] = value
    out = layer_norm(value, gain[...]).astype(BF)
    normed[...] = out
    for k in range(spread.shape[0]):
        spread[k] = out


def keyval_kernel(parts, out):
    out[...] = summed(parts[...]).astype(BF)


def own_kernel(
    place, parts, mine, theirs, gate_ref, gated_ref, token_mid, wout, wgate, wt2a, tokens, lifted, feature, attended
):
    cols, own, _ = parts.shape
    span = GROUP * HD
    lane = lax.broadcasted_iota(jnp.int32, (GROUP, span), 1)
    row = lax.broadcasted_iota(jnp.int32, (GROUP, span), 0)
    widen = jnp.where((lane >= row * HD) & (lane < (row + 1) * HD), 1.0, 0.0).astype(BF)
    half = cols // CORES
    rows = mine.shape[3]
    slot = lax.broadcasted_iota(jnp.int32, (rows, own), 0)
    token = lax.broadcasted_iota(jnp.int32, (rows, own), 1)
    select = jnp.where(slot == token + place[0], 1.0, 0.0).astype(BF)
    tables = []
    for part in (mine, theirs):
        flat = part[...].reshape(half * (H // GROUP) * 3 * GROUP, rows)
        tables.append(dot(flat, select).T)
    for group in range(H // GROUP):
        logs = []
        for k in range(cols):
            low = (k // CORES * (H // GROUP) + group) * 3 * GROUP
            mine_first = jnp.where(place[1] == k % CORES, 1.0, 0.0)
            triple = (
                tables[0][:, low : low + 2 * GROUP] * mine_first
                + tables[1][:, low : low + 2 * GROUP] * (1.0 - mine_first)
            )
            logs.append(triple[:, :GROUP] + triple[:, GROUP:])
        top = logs[0]
        for k in range(1, cols):
            top = jnp.maximum(top, logs[k])
        shares = [jnp.exp(one - top) for one in logs]
        total = shares[0]
        for k in range(1, cols):
            total = total + shares[k]
        share = jnp.concatenate([one / total for one in shares], axis=0)
        high = share.astype(BF)
        rest = (share - high.astype(F32)).astype(BF)
        weight = dot(high, widen) + dot(rest, widen)
        value = jnp.zeros((own, span), F32)
        for k in range(cols):
            at = slice(group * span, (group + 1) * span)
            value = value + weight[k * own : (k + 1) * own] * parts[k, :, at].astype(F32)
        attended[:, group * span : (group + 1) * span] = value
    gate = gate_ref[...]
    value = attended[...]
    new = (token_mid[...] + dot((gate * value).astype(BF), wout[...])).astype(BF)
    tokens[...] = new
    lifted[...] = dot(new, wt2a[...]).astype(BF)
    grad_gate = (gated_ref[...] * value * gate * (1.0 - gate)).astype(BF)
    feature[...] = dot_t(grad_gate, wgate[...])


def token_kernel(parts, key_feature, feature, grad_new, token_mid, gain, wquery, tokens, lifted, out):
    cols = CORES * parts.shape[0]
    width = D // cols
    total = summed(parts[...]).astype(BF)
    normed_grad = dot_t(total, wquery[...]) + feature[...] + key_feature[...].astype(F32)
    grad = grad_new[...] + norm_back(token_mid[...], gain[...], normed_grad)
    grad = grad.astype(BF)
    new = tokens[...]
    low = D + DA
    pair = CORES * width
    for k in range(cols // CORES):
        out[k, :, :D] = grad
        out[k, :, D:low] = lifted[...]
        out[k, :, low:] = new[:, k * pair : (k + 1) * pair]


def atoms_backward_kernel(
    starts, place, mine, theirs, token, inverse, slope, cot, mid, query, window, prob, mixed,
    wagg, wo, wq, new, tokens_out, grad_tokens, inner, first, last, atoms_grad, feature, padded,
):
    atom_dev = cot.shape[0]
    blocks = window.shape[0]
    half = mine.shape[0]
    tok_row = CORES * half
    width = tokens_out.shape[1]
    core = place[0]
    padded_rows = padded.shape[0]
    scale = 1.0 / math.sqrt(AHD)
    slot = lax.broadcasted_iota(jnp.int32, (atom_dev, tok_row), 1)
    atom_inverse = jnp.sum(
        jnp.where(slot == token[...], inverse[...], 0.0), axis=1, keepdims=True
    )
    parts = ((mine, core * half), (theirs, (1 - core) * half))
    slot = lax.broadcasted_iota(jnp.int32, (atom_dev, half), 1)
    members = [
        jnp.where(slot + base == token[...], 1.0, 0.0).astype(BF) for _, base in parts
    ]

    def gathered(at):
        return dot(members[0], mine[:, at]) + dot(members[1], theirs[:, at])

    row = lax.broadcasted_iota(jnp.int32, (D, width), 0)
    lane = lax.broadcasted_iota(jnp.int32, (D, width), 1)
    column = jnp.where(row == lane + place[1] * width, 1.0, 0.0).astype(BF)
    for part, base in parts:
        here = pl.ds(pl.multiple_of(base, half), half)
        low = D + DA
        pair = part[:, low:].astype(F32)
        tokens_out[here, :] = jnp.where(core == 0, pair[:, :width], pair[:, width:]).astype(BF)
        grad_tokens[here, :] = dot(part[:, :D], column).astype(BF)
    grads = cot[...].astype(F32)
    for low in range(0, D, 256):
        at = pl.ds(low, 256)
        hidden = (gathered(at) * atom_inverse * slope[:, at]).astype(BF)
        grads = grads + dot_t(hidden, wagg[:, at])
    atoms_grad[...] = grads
    mixed_grad = dot_t(grads.astype(BF), wo[...]).astype(BF)
    padded[...] = jnp.zeros(padded.shape, F32)
    for block in range(blocks):
        at = slice(block * QBLK, (block + 1) * QBLK)
        rows = window[block]
        one = prob[block]
        grad_heads = stacked(mixed_grad[at])
        query_heads = stacked(query[at, :])
        grad_wide = grad_heads.astype(F32)
        tall = jnp.concatenate([mixed[at, :]] * AH, axis=0).astype(F32)
        delta = jnp.sum(grad_wide * tall, axis=-1, keepdims=True)
        sgrad = (one * (dot_t(grad_heads, rows[:, DA:]) - delta)).astype(BF)
        qgrad = (unstacked(dot(sgrad, rows[:, :DA])) * scale).astype(BF)
        feature[at, :] = dot_t(qgrad, wq[...])
        key_grad = rows_dot(sgrad, query_heads) * scale
        value_grad = rows_dot(one.astype(BF), grad_heads)
        both = jnp.concatenate([key_grad, value_grad], axis=1).astype(BF)
        padded[...] += rows_dot(picked(starts[block], padded_rows), both)
    first[...] = padded[:RIM, :].astype(BF)
    last[...] = padded[RIM + atom_dev :, :].astype(BF)
    inner[...] = padded[RIM : RIM + atom_dev, :]
    lift = gathered(slice(D, D + DA))
    new[...] = (mid[...].astype(F32) + lift).astype(BF)


def atoms_last_kernel(inner, before, after, feature, atoms_grad, atoms, gain, wkv, out):
    atom_dev = atoms.shape[0]
    keyval = jnp.concatenate(
        [
            inner[:RIM, :] + before[...].astype(F32),
            inner[RIM : atom_dev - RIM, :],
            inner[atom_dev - RIM :, :] + after[...].astype(F32),
        ],
        axis=0,
    ).astype(BF)
    feat = feature[...] + dot_t(keyval, wkv[...])
    back = norm_back(atoms[...].astype(F32), gain[...], feat)
    out[...] = (atoms_grad[...] + back).astype(BF)


def local(
    atoms,
    tokens,
    atom_bias,
    token_bias,
    atom_index,
    atom_counts,
    window_starts,
    gain_atom,
    w_atom_q,
    w_atom_kv,
    w_atom_o,
    w_agg,
    gain_token,
    w_query,
    w_keyval,
    w_gate,
    w_out,
    w_t2a,
    atoms_cot,
    tokens_cot,
):
    rows = lax.axis_size("row")
    cols = lax.axis_size("col")
    row_index = lax.axis_index("row")
    col_index = lax.axis_index("col")
    atom_dev = atoms.shape[0]
    blocks = window_starts.shape[0]
    tok_row = tokens.shape[0]
    tok_col = token_bias.shape[2]
    own = tok_row // cols
    width = tokens.shape[1]
    first_atom = (row_index * cols + col_index) * atom_dev

    before, after = neighbours(atoms, RIM)

    local_token = atom_index - row_index * tok_row
    inverse_count = 1.0 / atom_counts.astype(F32)
    core = col_index % CORES
    half = tok_row // CORES
    first_own = core * half + col_index // CORES * own
    inv_own = lax.dynamic_slice_in_dim(inverse_count, first_own, own, 0)

    starts = window_starts - first_atom + RIM
    gain_a = gain_atom[None, :]
    gain_t = gain_token[None, :]
    part, atoms_mid, slope, atom_query, window, atom_prob, atom_mixed = whole(
        atoms_forward_kernel,
        [
            pltpu.HBM((cols, own, D + 2 * DA), BF),
            pltpu.HBM((atom_dev, DA), BF),
            pltpu.HBM((atom_dev, D), F32),
            pltpu.HBM((atom_dev, DA), BF),
            pltpu.HBM((blocks, KWIN, 2 * DA), BF),
            pltpu.HBM((blocks, AH * QBLK, KWIN), F32),
            pltpu.HBM((atom_dev, DA), BF),
        ],
        (
            starts,
            before,
            far(atoms),
            after,
            far(atom_bias.reshape(blocks, AH * QBLK, KWIN)),
            local_token[None, :],
            gain_a,
            far(w_atom_q),
            far(w_atom_kv),
            far(w_atom_o),
            far(w_agg),
            far(atoms_cot),
            far(tokens.T),
            far(tokens_cot.T),
        ),
        "atoms_forward",
        scalars=1,
    )

    sums = exchange(part, "col")
    tokens_mid, normed_own, spread = whole(
        norm_kernel,
        [
            pltpu.HBM((own, D), F32),
            pltpu.HBM((own, D), BF),
            pltpu.HBM((rows, own, D), BF),
        ],
        (sums, inv_own[:, None], gain_t),
        "token_norm",
    )
    keys_own = exchange(spread, "row")
    gate_own, gated_own, grad_new, packed = token_project(
        sums, normed_own, w_t2a, w_query, w_gate, w_out, rows
    )
    packed = token_pack(packed, keys_own)
    mine, theirs = halves_of(packed)
    to_row = [
        (i * cols + r * CORES + p, r * cols + i * CORES + p)
        for r in range(rows)
        for i in range(rows)
        for p in range(CORES)
    ]
    k_t, v_t = token_keys(mine.reshape(half, 3 * D), w_keyval)
    q, q_t, g, g_t, mixed, stats = token_forward(
        core[None],
        k_t,
        v_t,
        mine.reshape(half, 3 * D),
        theirs.reshape(half, 3 * D),
        token_bias,
        cols,
    )
    stats = halves_of(stats)
    mixed_parts = exchange(mixed, "col")
    q_mine, q_theirs, kv_feat = token_backward(
        core[None], *stats, q, q_t, g, g_t, k_t, v_t, token_bias, w_keyval
    )
    swap = [(i, i ^ 1) for i in range(cols)]
    q_other = lax.ppermute(q_theirs, "col", swap)
    kv_parts = exchange(kv_feat.reshape(rows, own, D), "row")
    q_pair = (q_mine.astype(F32) + q_other.astype(F32)).astype(BF)
    q_parts = among_core(q_pair.reshape(cols // CORES, own, D))
    tokens_new, lifted, gate_feat = whole(
        own_kernel,
        [shaped((own, D), BF), shaped((own, DA), BF), shaped((own, D), F32)],
        (
            jnp.stack([first_own, core]),
            mixed_parts,
            *stats,
            far(gate_own),
            far(gated_own),
            far(tokens_mid),
            far(w_out),
            far(w_gate),
            far(w_t2a),
        ),
        "token_own",
        scalars=1,
        scratch=[pltpu.VMEM((own, D), F32)],
    )
    (kv_own,) = whole(
        keyval_kernel,
        [shaped((own, D), BF)],
        (kv_parts,),
        "token_keyval",
    )
    kv_back = lax.ppermute(kv_own, ("row", "col"), to_row)
    (mid_spread,) = whole(
        token_kernel,
        [pltpu.HBM((cols // CORES, own, D + DA + CORES * width), BF)],
        (
            q_parts,
            kv_back,
            gate_feat,
            far(grad_new),
            far(tokens_mid),
            gain_t,
            far(w_query),
            tokens_new,
            lifted,
        ),
        "token_grads",
    )
    mine, theirs = halves_of(mid_spread)

    atoms_new, tokens_out, grad_tokens, inner, first, last, atoms_grad, query_feat = whole(
        atoms_backward_kernel,
        [
            shaped((atom_dev, DA), BF),
            shaped((tok_row, width), BF),
            shaped((tok_row, width), BF),
            pltpu.HBM((atom_dev, 2 * DA), F32),
            shaped((RIM, 2 * DA), BF),
            shaped((RIM, 2 * DA), BF),
            pltpu.HBM((atom_dev, DA), F32),
            pltpu.HBM((atom_dev, DA), F32),
        ],
        (
            starts,
            jnp.stack([core, col_index]),
            mine.reshape(half, -1),
            theirs.reshape(half, -1),
            local_token[:, None],
            inverse_count[None, :],
            slope,
            far(atoms_cot),
            far(atoms_mid),
            far(atom_query),
            window,
            atom_prob,
            far(atom_mixed),
            far(w_agg),
            far(w_atom_o),
            far(w_atom_q),
        ),
        "atoms_backward",
        scalars=2,
        scratch=[pltpu.VMEM((atom_dev + 2 * RIM, 2 * DA), F32)],
    )
    axes = ("row", "col")
    up = [(i, i + 1) for i in range(rows * cols - 1)]
    down = [(j, i) for i, j in up]
    from_before = lax.ppermute(last, axes, up)
    from_after = lax.ppermute(first, axes, down)
    (grad_atoms,) = whole(
        atoms_last_kernel,
        [shaped((atom_dev, DA), BF)],
        (
            far(inner),
            from_before,
            from_after,
            far(query_feat),
            far(atoms_grad),
            far(atoms),
            gain_a,
            far(w_atom_kv),
        ),
        "atoms_last",
    )
    return (atoms_new, tokens_out, grad_atoms, grad_tokens)


def solution(mesh):
    placed = (
        P(("row", "col"), None),
        P("row", "col"),
        P(("row", "col"), None, None, None),
        P(None, "row", "col"),
        P(("row", "col")),
        P("row"),
        P(("row", "col")),
        P(),
        P(),
        P(),
        P(),
        P(),
        P(),
        P(),
        P(),
        P(),
        P(),
        P(),
        P(("row", "col"), None),
        P("row", "col"),
    )
    return jax.shard_map(
        local,
        mesh=mesh,
        in_specs=placed,
        out_specs=(
            P(("row", "col"), None),
            P("row", "col"),
            P(("row", "col"), None),
            P("row", "col"),
        ),
        check_vma=False,
    )
```
